32 devices in a mesh: dp: 8 (over y, x, core), ctx: 4 (over z).
Axes of the slice: x: 2, y: 2, z: 4, core: 2. Of those that a mesh axis runs over, the one named last changes fastest.
Arguments:
- tokens: bfloat16 [64, 512, 1024], P('dp', 'ctx'), may hold values from -6 to 6
- lengths: int32 [64], P('dp'), may hold values from 128 to 512, as said below
- w_qkv: bfloat16 [1024, 3072], P('dp'), may hold values from -0.1875 to 0.1875
- bias_qv: bfloat16 [2048], P('dp'), may hold values from -3 to 3
- w_out: bfloat16 [1024, 1024], P('dp'), may hold values from -1.5 to 1.5
- bias_out: bfloat16 [1024], P('dp'), may hold values from -3 to 3
- gain_one: bfloat16 [1024], P('dp'), may hold values from 0.5 to 1.5
- shift_one: bfloat16 [1024], P('dp'), may hold values from -3 to 3
- w_up: bfloat16 [1024, 4096], P('dp'), may hold values from -0.1875 to 0.1875
- bias_up: bfloat16 [4096], P('dp'), may hold values from -3 to 3
- w_down: bfloat16 [4096, 1024], P('dp'), may hold values from -0.09375 to 0.09375
- bias_down: bfloat16 [1024], P('dp'), may hold values from -3 to 3
- gain_two: bfloat16 [1024], P('dp'), may hold values from 0.5 to 1.5
- shift_two: bfloat16 [1024], P('dp'), may hold values from -3 to 3
- cotangent: bfloat16 [64, 512, 1024], P('dp', 'ctx'), may hold values from -6 to 6
Outputs:
- output: bfloat16 [64, 512, 1024], P('dp', 'ctx')
- grad_input: float32 [64, 512, 1024], P('dp', 'ctx')
- grad_w_qkv: float32 [1024, 3072], P('dp')
- grad_bias_qv: float32 [2048], P('dp')
- grad_w_out: float32 [1024, 1024], P('dp')
- grad_bias_out: float32 [1024], P('dp')
- grad_gain_one: float32 [1024], P('dp')
- grad_shift_one: float32 [1024], P('dp')
- grad_w_up: float32 [1024, 4096], P('dp')
- grad_bias_up: float32 [4096], P('dp')
- grad_w_down: float32 [4096, 1024], P('dp')
- grad_bias_down: float32 [1024], P('dp')
- grad_gain_two: float32 [1024], P('dp')
- grad_shift_two: float32 [1024], P('dp')
The draws below stay inside these ranges and needn't reach their ends.
Inputs may be any that keep to these rules, and one draw needn't show every extreme that they name: `lengths`: in each group of 8 slots that one index of dp holds, one slot has length 512 and another length 128.
All inputs are finite; a program needn't handle non-finite values.
Results may differ from the reference program's by a relative error of at most 0.017.
Values may be sent and summed in bfloat16 or wider, within the bound.
No kernel may reach another device: no remote copies, remote signals or barrier semaphores. Data moves between devices by JAX's collectives and lax.ppermute only.
A program may use at most 256 MiB of HBM per device.

```python
import jax
import jax.numpy as jnp
from jax import lax

D = 1024
H = 16
HD = 64
FF = 4096
SEQS = 8
SLOT = 512
MINLEN = 128
SEQS_ALL = 64
N_DP = 8


def draw_lengths(key, part):
    key = jax.random.fold_in(key, 11)
    first_key, second_key = jax.random.split(key)
    groups = SEQS_ALL // SEQS
    base = jax.random.randint(first_key, (groups, SEQS), MINLEN, SLOT + 1)
    pick = jax.random.randint(second_key, (groups, 1), 0, SEQS)
    slot_ids = jnp.arange(SEQS, dtype=jnp.int32)[None, :]
    filled = jnp.where(slot_ids == pick, SLOT, base)
    filled = jnp.where(slot_ids == (pick + 1) % SEQS, MINLEN, filled)
    return filled.reshape(SEQS_ALL).astype(jnp.int32)


def levels(stream_key, extent, cuts, low, largest):
    factor_of = 1.0
    for dim, parts in cuts:
        steps = jax.random.uniform(jax.random.fold_in(jax.random.fold_in(stream_key, 6), dim), (parts,), jnp.float32, low / len(cuts), largest / len(cuts))
        factor_of = factor_of * jnp.repeat(jnp.exp(steps), extent[dim] // parts).reshape((-1,) + (1,) * (len(extent) - 1 - dim))
    return factor_of


def normal_values(own_key, extent, width, bound, cuts=(), held_as=jnp.bfloat16):
    factor_of = levels(own_key, extent, cuts, -0.22, 0.18) if cuts else 1.0
    array = jax.random.normal(own_key, extent, jnp.float32) * width * factor_of
    return jnp.minimum(jnp.maximum(array, -bound), bound).astype(held_as)


def setup_inputs(seed: int = 0) -> dict:
    key_list = jax.random.split(jax.random.key(seed), 16)
    return {
        "tokens": normal_values(key_list[0], (SEQS_ALL, SLOT, D), 1.0, 6.0, ((0, 8), (1, 4))),
        "lengths": draw_lengths(jax.random.fold_in(key_list[15], 71), 0),
        "w_qkv": normal_values(key_list[2], (D, 3 * D), D ** -0.5, 0.1875, ((0, 8),)),
        "bias_qv": normal_values(key_list[3], (2 * D,), 0.5, 3.0, ((0, 8),)),
        "w_out": normal_values(key_list[4], (D, D), (HD // 4) ** -0.5, 1.5, ((0, 8),)),
        "bias_out": normal_values(key_list[5], (D,), 0.5, 3.0, ((0, 8),)),
        "gain_one": jnp.clip(1.0 + 0.1 * jax.random.normal(key_list[6], (D,), jnp.float32), 0.5, 1.5).astype(jnp.bfloat16),
        "shift_one": normal_values(key_list[7], (D,), 0.5, 3.0, ((0, 8),)),
        "w_up": normal_values(key_list[8], (D, FF), D ** -0.5, 0.1875, ((0, 8),)),
        "bias_up": normal_values(key_list[9], (FF,), 0.5, 3.0, ((0, 8),)),
        "w_down": normal_values(key_list[10], (FF, D), FF ** -0.5, 0.09375, ((0, 8),)),
        "bias_down": normal_values(key_list[11], (D,), 0.5, 3.0, ((0, 8),)),
        "gain_two": jnp.clip(1.0 + 0.1 * jax.random.normal(key_list[12], (D,), jnp.float32), 0.5, 1.5).astype(jnp.bfloat16),
        "shift_two": normal_values(key_list[13], (D,), 0.5, 3.0, ((0, 8),)),
        "cotangent": normal_values(key_list[14], (SEQS_ALL, SLOT, D), 1.0, 6.0, ((0, 8), (1, 4))),
    }


neg_big = -1e+30
eps_norm = 1e-06

@jax.custom_vjp
def low(v):
    return lax.optimization_barrier(v.astype(jnp.bfloat16)).astype(jnp.float32)

@jax.custom_vjp
def low_back(v):
    return v

def low_keep(v):
    return (low(v), None)

def low_pass(kept, grad):
    return (grad,)

def back_keep(v):
    return (v, None)

def back_low(kept, grad):
    return (low(grad),)
low.defvjp(low_keep, low_pass)
low_back.defvjp(back_keep, back_low)

def matmul(left, right):
    return jnp.dot(left, right, precision=lax.Precision.HIGHEST, preferred_element_type=jnp.float32)

def layer_norm(rows, gain, shift):
    centre = rows - lax.optimization_barrier(jnp.mean(rows, axis=-1, keepdims=True))
    inverse = lax.rsqrt(lax.optimization_barrier(jnp.mean(centre * centre, axis=-1, keepdims=True)) + eps_norm)
    return centre * inverse * gain + shift

def forward(block, params, lens_block):
    w_qkv, bias_qv, w_out, bias_out, gain_one, shift_one, w_up, bias_up, w_down, bias_down, gain_two, shift_two = params
    seqs = block.shape[0]
    rows = block.reshape(seqs * SLOT, D)
    projected = matmul(rows, w_qkv) + jnp.concatenate([bias_qv[:D], jnp.zeros((D,), jnp.float32), bias_qv[D:]])
    projected = low_back(low(projected))
    queries = projected[:, :D].reshape(seqs, SLOT, H, HD)
    keys = projected[:, D:2 * D].reshape(seqs, SLOT, H, HD)
    values = projected[:, 2 * D:].reshape(seqs, SLOT, H, HD)
    valid = jnp.arange(SLOT, dtype=jnp.int32)[None, :] < lens_block[:, None]
    raw = jnp.einsum('sqhd,skhd->shqk', queries, keys, precision=lax.Precision.HIGHEST) * HD ** (-0.5)
    raw = low_back(raw)
    key_mask = valid[:, None, None, :]
    masked = jnp.where(key_mask, raw, neg_big)
    peak = lax.optimization_barrier(jnp.max(masked, axis=-1, keepdims=True))
    weights = jnp.where(key_mask, jnp.exp(masked - peak), 0.0)
    probs = low(weights / lax.optimization_barrier(jnp.sum(weights, axis=-1, keepdims=True)))
    mixed = jnp.einsum('shqk,skhd->sqhd', probs, values, precision=lax.Precision.HIGHEST).reshape(seqs * SLOT, D)
    mixed = low_back(low(mixed))
    branch = low_back(matmul(mixed, w_out) + bias_out)
    first = layer_norm(rows + branch, gain_one, shift_one)
    hidden = low_back(matmul(low(first), w_up) + bias_up)
    active = low(jax.nn.gelu(hidden, approximate=False))
    second = low_back(matmul(active, w_down) + bias_down)
    result = layer_norm(first + second, gain_two, shift_two)
    row_valid = valid.reshape(seqs * SLOT, 1).astype(jnp.float32)
    return (result * row_valid).reshape(seqs, SLOT, D)

def reference(tokens, lengths, w_qkv, bias_qv, w_out, bias_out, gain_one, shift_one, w_up, bias_up, w_down, bias_down, gain_two, shift_two, cotangent):
    params = tuple((p.astype(jnp.float32) for p in (w_qkv, bias_qv, w_out, bias_out, gain_one, shift_one, w_up, bias_up, w_down, bias_down, gain_two, shift_two)))
    inputs = tokens.astype(jnp.float32).reshape(N_DP, SEQS, SLOT, D)
    cots = cotangent.astype(jnp.float32).reshape(N_DP, SEQS, SLOT, D)
    lens = lengths.reshape(N_DP, SEQS)

    def step(carry, item):
        block, lens_block, cot_block = item
        result, pull = jax.vjp(lambda t, p: forward(t, p, lens_block), block, params)
        grad_block, grad_params = pull(cot_block)
        return (tuple((c + g for c, g in zip(carry, grad_params))), (result.astype(jnp.bfloat16), grad_block))
    zeros = tuple((jnp.zeros_like(p) for p in params))
    totals, (outs, grads) = lax.scan(step, zeros, (inputs, lens, cots))
    return (outs.reshape(SEQS_ALL, SLOT, D), grads.reshape(SEQS_ALL, SLOT, D), totals[0], totals[1], totals[2], totals[3], totals[4], totals[5], totals[6], totals[7], totals[8], totals[9], totals[10], totals[11])
```

```python
import functools

import jax
import jax.numpy as jnp
from jax import lax
from jax.experimental import pallas as pl
from jax.experimental.pallas import tpu as pltpu
from jax.sharding import PartitionSpec as P

HD = 64
NEG = -1e30
EPS = 1e-06
BF = jnp.bfloat16
F32 = jnp.float32
MIB = 1024 * 1024
ANY = pl.BlockSpec(memory_space=pl.ANY)


def swap(x, axis, bit):
    n = lax.axis_size(axis)
    return lax.ppermute(x, axis, [(i, i ^ bit) for i in range(n)])


def gather_dp(own):
    n = lax.axis_size("dp")
    if n == 8:
        half = own.shape[1] // 2
        at_x = swap(own, "dp", 2)
        at_y = swap(own, "dp", 4)
        left = swap(at_x[:, :half], "dp", 4)
        right = swap(at_y[:, half:], "dp", 2)
        mine = jnp.stack([own, at_x, at_y, jnp.concatenate([left, right], axis=1)])
    else:
        mine = own[None]
        bit = 2
        while bit < n:
            mine = jnp.concatenate([mine, swap(mine, "dp", bit)])
            bit *= 2
    return mine, swap(mine, "dp", 1)


def add_low(*parts):
    total = parts[0].astype(F32)
    for part in parts[1:]:
        total = total + part.astype(F32)
    return total.astype(BF)


def reduce_dp(grad):
    n = lax.axis_size("dp")
    me = lax.axis_index("dp")
    rows = grad.shape[0] // n
    width = grad.shape[1]

    def shard(rel):
        return lax.dynamic_slice(grad, ((me ^ rel) * rows, 0), (rows, width))

    away = jnp.stack([shard(2 * k + 1) for k in range(n // 2)])
    come = swap(away, "dp", 1)
    if n == 8:
        half = width // 2
        own, to_x, to_y, to_xy = (add_low(shard(2 * k), come[k]) for k in range(4))
        left = swap(to_xy[:, :half], "dp", 4)
        right = swap(to_xy[:, half:], "dp", 2)
        to_x = jnp.concatenate([add_low(to_x[:, :half], left), to_x[:, half:]], axis=1)
        to_y = jnp.concatenate([to_y[:, :half], add_low(to_y[:, half:], right)], axis=1)
        return add_low(own, swap(to_x, "dp", 2), swap(to_y, "dp", 4))
    mine = add_low(jnp.stack([shard(2 * k) for k in range(n // 2)]), come)
    bit = n // 2
    while bit > 1:
        keep = mine.shape[0] // 2
        mine = add_low(mine[:keep], swap(mine[keep:], "dp", bit))
        bit //= 2
    return mine[0]


def sum_ctx(share):
    n = lax.axis_size("ctx")
    if n != 4:
        return lax.psum(share.astype(F32), "ctx")
    inner = add_low(share, lax.ppermute(share, "ctx", [(0, 1), (3, 2)]))
    total = add_low(inner, lax.ppermute(inner, "ctx", [(1, 2), (2, 1)]))
    outer = lax.ppermute(total, "ctx", [(1, 0), (2, 3)])
    place = lax.axis_index("ctx")
    return jnp.where((place == 0) | (place == 3), outer, total).astype(F32)


def to_sequences(block, order):
    n = lax.axis_size("ctx")
    me = lax.axis_index("ctx")
    per = block.shape[0] // n

    def part(j):
        return lax.dynamic_slice_in_dim(block, (me ^ j) * per, per, axis=0)

    return jnp.stack([part(0)] + [swap(part(j), "ctx", j) for j in range(1, n)])


def from_sequences(parts, dtype):
    n = lax.axis_size("ctx")
    me = lax.axis_index("ctx")
    per = parts.shape[1]
    out = jnp.zeros((n * per,) + parts.shape[2:], dtype)
    for j in range(n):
        piece = parts[j] if j == 0 else swap(parts[j], "ctx", j)
        out = lax.dynamic_update_slice_in_dim(out, piece.astype(dtype), (me ^ j) * per, axis=0)
    return out


def nn(left, right):
    return jnp.dot(left, right, preferred_element_type=F32)


def nt(left, right):
    return lax.dot_general(left, right, (((1,), (1,)), ((), ())), preferred_element_type=F32)


def tn(left, right):
    return lax.dot_general(left, right, (((0,), (0,)), ((), ())), preferred_element_type=F32)


def fold(rows):
    return jnp.sum(rows.reshape(rows.shape[0] // 8, 8, rows.shape[1]), axis=0)


def fetch(stacks, whole, sems, me):
    copies = []
    for odd, stack in enumerate(stacks):
        count, rows, _ = stack.shape
        for k in range(count):
            start = pl.multiple_of((me ^ (2 * k + odd)) * rows, rows)
            copies.append(
                pltpu.make_async_copy(
                    stack.at[k], whole.at[pl.ds(start, rows)], sems.at[odd * count + k]
                )
            )
    for copy in copies:
        copy.start()
    for copy in copies:
        copy.wait()


def row_spec(tile, width):
    return pl.BlockSpec((tile, width), lambda i, *_: (i, 0))


def one_spec(height, width):
    return pl.BlockSpec((height, width), lambda i, *_: (0, 0))


def dense(body, name, meta, rows, tile, row_ins, vec_ins, weights, row_outs, sums, flops):
    stacks = [s for pair in weights for s in pair]
    scratch = []
    for mine, other in weights:
        count, r, width = mine.shape
        scratch.append(pltpu.VMEM((2 * count * r, width), BF))
        scratch.append(pltpu.SemaphoreType.DMA((2 * count,)))
    n_row, n_vec, n_stack = len(row_ins), len(vec_ins), len(stacks)
    n_out, n_sum = len(row_outs), len(sums)

    def kernel(meta_ref, *refs):
        pos = 0
        groups = []
        for count in (n_row, n_vec, n_stack, n_out, n_sum, 2 * len(weights)):
            groups.append(refs[pos : pos + count])
            pos += count
        row_refs, vec_refs, stack_refs, out_refs, sum_refs, scratch_refs = groups

        @pl.when(pl.program_id(0) == 0)
        def _():
            for w in range(len(weights)):
                fetch(stack_refs[2 * w : 2 * w + 2], scratch_refs[2 * w], scratch_refs[2 * w + 1], meta_ref[0])
            for ref in sum_refs:
                ref[...] = jnp.zeros_like(ref)

        body(meta_ref, row_refs, vec_refs, scratch_refs[::2], out_refs, sum_refs)

    in_specs = (
        [row_spec(tile, a.shape[-1]) if a.ndim == 2 else pl.BlockSpec((a.shape[0], tile, a.shape[2]), lambda i, *_: (0, i, 0)) for a in row_ins]
        + [one_spec(1, v.shape[1]) for v in vec_ins]
        + [ANY] * n_stack
    )
    out_specs = [row_spec(tile, w) for w, _ in row_outs] + [one_spec(8, w) for w in sums]
    out_shape = [jax.ShapeDtypeStruct((rows, w), d) for w, d in row_outs] + [
        jax.ShapeDtypeStruct((8, w), F32) for w in sums
    ]
    nbytes = sum(a.size * a.dtype.itemsize for a in list(row_ins) + stacks)
    return pl.pallas_call(
        kernel,
        grid_spec=pltpu.PrefetchScalarGridSpec(
            num_scalar_prefetch=1,
            grid=(rows // tile,),
            in_specs=in_specs,
            out_specs=out_specs,
            scratch_shapes=scratch,
        ),
        out_shape=out_shape,
        compiler_params=pltpu.CompilerParams(vmem_limit_bytes=56 * MIB, dimension_semantics=("arbitrary",)),
        cost_estimate=pl.CostEstimate(flops=flops, bytes_accessed=nbytes, transcendentals=0),
        name=name,
    )(meta, *row_ins, *vec_ins, *stacks)


def qkv_body(meta, rows, vecs, whole, outs, sums):
    (x,) = rows
    (bias,) = vecs
    width = whole[0].shape[1]
    for c in range(0, width, 1024):
        outs[0][:, c : c + 1024] = (nn(x[...], whole[0][:, c : c + 1024]) + bias[:, c : c + 1024]).astype(BF)


def out_body(meta, rows, vecs, whole, outs, sums):
    mixed, x = rows
    bias, gain, shift = vecs
    total = x[...].astype(F32) + (nn(mixed[...], whole[0][...]) + bias[...])
    centre = total - jnp.mean(total, axis=-1, keepdims=True)
    inverse = lax.rsqrt(jnp.mean(centre * centre, axis=-1, keepdims=True) + EPS)
    normed = centre * inverse
    outs[0][...] = normed
    outs[1][...] = jnp.broadcast_to(inverse, outs[1].shape)
    outs[2][...] = (normed * gain[...] + shift[...]).astype(BF)


def up_body(meta, rows, vecs, whole, outs, sums):
    (low,) = rows
    (bias,) = vecs
    width = whole[0].shape[1]
    step = 512
    for c in range(0, width, step):
        cols = slice(c, c + step)
        hidden = nn(low[...], whole[0][:, cols]) + bias[:, cols]
        cdf = 0.5 + 0.5 * lax.erf(hidden * 0.7071067811865476)
        pdf = jnp.exp(-0.5 * hidden * hidden) * 0.3989422804014327
        outs[0][:, cols] = (hidden * cdf).astype(BF)
        outs[1][:, cols] = (cdf + hidden * pdf).astype(BF)


def down_body(blk, per, meta, rows, vecs, whole, outs, sums):
    active, normed_one, cot = rows
    bias, gain_one, shift_one, gain, shift = vecs
    total = (normed_one[...] * gain_one[...] + shift_one[...]) + (nn(active[...], whole[0][...]) + bias[...])
    centre = total - jnp.mean(total, axis=-1, keepdims=True)
    inverse = lax.rsqrt(jnp.mean(centre * centre, axis=-1, keepdims=True) + EPS)
    normed = centre * inverse
    place = meta[2 + pl.program_id(0)]
    at = lax.broadcasted_iota(jnp.int32, (total.shape[0], 1), 0)
    valid = jnp.zeros(at.shape, jnp.bool_)
    for s in range(per):
        here = at - s * blk
        valid = valid | ((here >= 0) & (here < blk) & (here + place < meta[2 + pl.num_programs(0) + s]))
    keep = jnp.where(valid, 1.0, 0.0)
    outs[0][...] = ((normed * gain[...] + shift[...]) * keep).astype(BF)
    grad = cot[...].astype(F32) * keep
    sums[0][...] += fold(grad * normed)
    sums[1][...] += fold(grad)
    scaled = grad * gain[...]
    back = inverse * (
        scaled
        - jnp.mean(scaled, axis=-1, keepdims=True)
        - normed * jnp.mean(scaled * normed, axis=-1, keepdims=True)
    )
    low = back.astype(BF)
    outs[1][...] = back
    outs[2][...] = low
    sums[2][...] += fold(low.astype(F32))


def hidden_body(meta, rows, vecs, whole, outs, sums):
    second, deriv = rows
    width = deriv.shape[1]
    step = 512
    for c in range(0, width, step):
        cols = slice(c, c + step)
        low = (nt(second[...], whole[0][cols, :]) * deriv[:, cols].astype(F32)).astype(BF)
        outs[0][:, cols] = low
        sums[0][:, cols] += fold(low.astype(F32))


def first_body(meta, rows, vecs, whole, outs, sums):
    hidden, sum_two, normed, inverse = rows
    (gain,) = vecs
    grad = sum_two[...] + nt(hidden[...], whole[0][...])
    n1 = normed[...]
    sums[0][...] += fold(grad * n1)
    sums[1][...] += fold(grad)
    scaled = grad * gain[...]
    back = inverse[:, 0:1] * (
        scaled - jnp.mean(scaled, axis=-1, keepdims=True) - n1 * jnp.mean(scaled * n1, axis=-1, keepdims=True)
    )
    low = back.astype(BF)
    outs[0][...] = back
    outs[1][...] = low
    sums[2][...] += fold(low.astype(F32))
    outs[2][...] = nt(low, whole[1][...]).astype(BF)


def input_body(meta, rows, vecs, whole, outs, sums):
    proj, sum_one = rows
    width = sum_one.shape[1]
    total = sum_one[...]
    for c in range(3):
        total = total + nt(proj[c], whole[0][:, c * width : (c + 1) * width])
    outs[0][...] = total.astype(BF)


def key_mask(meta, n, blk):
    s = pl.program_id(0)
    length = meta[2 + n + s]
    at = lax.broadcasted_iota(jnp.int32, (n * blk, 1), 0)
    ok = jnp.zeros(at.shape, jnp.bool_)
    for j in range(n):
        here = at - j * blk
        ok = ok | ((here >= 0) & (here < blk) & (here + meta[2 + j] < length))
    return ok


def attend_kernel(n, blk, meta, q_ref, k_ref, v_ref, mixed_ref, lse_ref):
    ok = key_mask(meta, n, blk)
    q2 = q_ref[...].reshape(n * blk, 2 * HD) * BF(HD ** (-0.5))
    k2 = k_ref[...].reshape(n * blk, 2 * HD)
    v2 = v_ref[...].reshape(n * blk, 2 * HD)
    outs = []
    for h in range(2):
        lanes = slice(h * HD, (h + 1) * HD)
        scores = jnp.where(ok, nt(k2[:, lanes], q2[:, lanes]), NEG)
        peak = jnp.max(scores, axis=0, keepdims=True)
        weights = jnp.exp(scores - peak)
        total = jnp.sum(weights, axis=0, keepdims=True)
        probs = (weights * (1.0 / total)).astype(BF)
        lse_ref[h : h + 1, :] = peak + jnp.log(total)
        outs.append(tn(probs, v2[:, lanes]))
    mixed_ref[...] = jnp.concatenate(outs, axis=1).astype(BF).reshape(mixed_ref.shape)


def attend_back_kernel(n, blk, meta, q_ref, k_ref, v_ref, g_ref, lse_ref, proj_ref, sum_ref):
    ok = key_mask(meta, n, blk)
    scale = HD ** (-0.5)
    q2 = q_ref[...].reshape(n * blk, 2 * HD) * BF(scale)
    k2 = k_ref[...].reshape(n * blk, 2 * HD)
    v2 = v_ref[...].reshape(n * blk, 2 * HD)
    g2 = g_ref[...].reshape(n * blk, 2 * HD)
    gq, gk, gv = [], [], []
    for h in range(2):
        lanes = slice(h * HD, (h + 1) * HD)
        q, k, v, g = q2[:, lanes], k2[:, lanes], v2[:, lanes], g2[:, lanes]
        scores = jnp.where(ok, nt(k, q), NEG)
        exact = jnp.exp(scores - lse_ref[h : h + 1, :])
        mixed = exact * nt(v, g)
        inner = jnp.sum(mixed, axis=0, keepdims=True)
        low = (mixed - exact * inner).astype(BF)
        gq.append(tn(low, k) * scale)
        gk.append(nn(low, q))
        gv.append(nn(exact.astype(BF), g))
    for c, parts in enumerate((gq, gk, gv)):
        whole = jnp.concatenate(parts, axis=1).astype(BF)
        proj_ref[c] = whole.reshape(proj_ref.shape[1:])
        sum_ref[c] = fold(whole.astype(F32))


def attend(meta, proj, n, per, blk):
    heads = proj.shape[-1] // 3 // (2 * HD)
    shaped = proj.reshape(n, per, blk, proj.shape[-1])

    def spec(c):
        return pl.BlockSpec((n, None, blk, 2 * HD), lambda s, h, *_: (0, s, 0, c * heads + h))

    flops = per * heads * 2 * 4 * (n * blk) ** 2 * HD
    mixed, lse = pl.pallas_call(
        functools.partial(attend_kernel, n, blk),
        grid_spec=pltpu.PrefetchScalarGridSpec(
            num_scalar_prefetch=1,
            grid=(per, heads),
            in_specs=[spec(0), spec(1), spec(2)],
            out_specs=[spec(0), pl.BlockSpec((None, None, 2, n * blk), lambda s, h, *_: (s, h, 0, 0))],
        ),
        out_shape=[
            jax.ShapeDtypeStruct((n, per, blk, heads * 2 * HD), BF),
            jax.ShapeDtypeStruct((per, heads, 2, n * blk), F32),
        ],
        compiler_params=pltpu.CompilerParams(vmem_limit_bytes=48 * MIB),
        cost_estimate=pl.CostEstimate(flops=4 * flops, bytes_accessed=proj.size * 2, transcendentals=0),
        name="attend",
    )(meta, shaped, shaped, shaped)
    return mixed.reshape(n * per * blk, -1), lse


def attend_back(meta, proj, grad, lse, n, per, blk):
    width = proj.shape[-1] // 3
    heads = width // (2 * HD)
    shaped = proj.reshape(n, per, blk, proj.shape[-1])

    def spec(c):
        return pl.BlockSpec((n, None, blk, 2 * HD), lambda s, h, *_: (0, s, 0, c * heads + h))

    flops = per * heads * 2 * 10 * (n * blk) ** 2 * HD
    out, sums = pl.pallas_call(
        functools.partial(attend_back_kernel, n, blk),
        grid_spec=pltpu.PrefetchScalarGridSpec(
            num_scalar_prefetch=1,
            grid=(per, heads),
            in_specs=[spec(0), spec(1), spec(2), spec(0), pl.BlockSpec((None, None, 2, n * blk), lambda s, h, *_: (s, h, 0, 0))],
            out_specs=[
                pl.BlockSpec((3, n, None, blk, 2 * HD), lambda s, h, *_: (0, 0, s, 0, h)),
                pl.BlockSpec((3, None, 8, 2 * HD), lambda s, h, *_: (0, s, 0, h)),
            ],
        ),
        out_shape=[
            jax.ShapeDtypeStruct((3, n, per, blk, width), BF),
            jax.ShapeDtypeStruct((3, per, 8, width), F32),
        ],
        compiler_params=pltpu.CompilerParams(vmem_limit_bytes=48 * MIB),
        cost_estimate=pl.CostEstimate(flops=4 * flops, bytes_accessed=proj.size * 4, transcendentals=0),
        name="attend_back",
    )(meta, shaped, shaped, shaped, grad.reshape(n, per, blk, width), lse)
    return out.reshape(3, n * per * blk, width), sums


def contract_rows(left, right):
    return tn(left, right).astype(BF)


def shards(
    tokens, lengths, w_qkv, bias_qv, w_out, bias_out, gain_one, shift_one,
    w_up, bias_up, w_down, bias_down, gain_two, shift_two, cotangent,
):
    seqs, blk, width = tokens.shape
    n = lax.axis_size("ctx")
    ndp = lax.axis_size("dp")
    me = lax.axis_index("dp")
    place = lax.axis_index("ctx")
    per = seqs // n
    rows = seqs * blk
    tile = per * blk

    own = lax.dynamic_slice_in_dim(lengths, place * per, per)
    meta = jnp.concatenate(
        [
            jnp.stack([me, place]).astype(jnp.int32),
            (place ^ jnp.arange(n, dtype=jnp.int32)) * blk,
            own,
        ]
    )

    vectors = (bias_qv, bias_out, gain_one, shift_one, bias_up, bias_down, gain_two, shift_two)
    sizes = [v.shape[0] for v in vectors]
    packed = lax.all_gather(jnp.concatenate(vectors).reshape(1, -1), "dp", axis=0, tiled=True).astype(F32)
    fulls, pos = [], 0
    for size in sizes:
        fulls.append(packed[:, pos : pos + size].reshape(1, ndp * size))
        pos += size
    bqv, bout, gone, sone, bup, bdown, gtwo, stwo = fulls
    bqkv = jnp.concatenate([bqv[:, :width], jnp.zeros((1, width), F32), bqv[:, width:]], axis=1)

    x = to_sequences(tokens, None).reshape(rows, width)
    qkv_w = gather_dp(w_qkv)
    out_w = gather_dp(w_out)
    up_w = gather_dp(w_up)
    down_w = gather_dp(w_down)
    cot = to_sequences(cotangent, None).reshape(rows, width)

    ff = w_up.shape[1]
    flops = 2 * rows * width
    (proj,) = dense(qkv_body, "qkv", meta, rows, tile, [x], [bqkv], [qkv_w], [(3 * width, BF)], [], flops * 3 * width)
    mixed, lse = attend(meta, proj, n, per, blk)
    normed_one, inverse_one, first_low = dense(
        out_body, "out", meta, rows, tile, [mixed, x], [bout, gone, sone], [out_w],
        [(width, F32), (128, F32), (width, BF)], [], flops * width,
    )
    active, deriv = dense(up_body, "up", meta, rows, tile, [first_low], [bup], [up_w], [(ff, BF), (ff, BF)], [], flops * ff)
    out_parts, sum_two, second, s_gtwo, s_stwo, s_bdown = dense(
        functools.partial(down_body, blk, per), "down", meta, rows, tile, [active, normed_one, cot], [bdown, gone, sone, gtwo, stwo], [down_w],
        [(width, BF), (width, F32), (width, BF)], [width] * 3, flops * ff,
    )
    output = from_sequences(out_parts.reshape(n, per, blk, width), BF)
    grad_down = contract_rows(active, second)
    share_down = reduce_dp(grad_down)
    hidden, s_bup = dense(hidden_body, "hidden", meta, rows, tile, [second, deriv], [], [down_w], [(ff, BF)], [ff], flops * ff)
    grad_up = contract_rows(first_low, hidden)
    share_up = reduce_dp(grad_up)
    sum_one, branch, g_mixed, s_gone, s_sone, s_bout = dense(
        first_body, "first", meta, rows, tile, [hidden, sum_two, normed_one, inverse_one], [gone], [up_w, out_w],
        [(width, F32), (width, BF), (width, BF)], [width] * 3, flops * (ff + width),
    )
    grad_out = contract_rows(mixed, branch)
    share_out = reduce_dp(grad_out)
    g_proj, s_proj = attend_back(meta, proj, g_mixed, lse, n, per, blk)
    (grad_in,) = dense(input_body, "input", meta, rows, tile, [g_proj, sum_one], [], [qkv_w], [(width, BF)], [], flops * 3 * width)
    grad_input = from_sequences(grad_in.reshape(n, per, blk, width), F32)
    grad_qkv = jnp.concatenate([contract_rows(x, g_proj[c]) for c in range(3)], axis=1)
    share_qkv = reduce_dp(grad_qkv)

    s_proj = jnp.sum(s_proj, axis=(1, 2))
    vec = [jnp.concatenate([s_proj[0], s_proj[2]])] + [
        jnp.sum(s, axis=0) for s in (s_bout, s_gone, s_sone, s_bup, s_bdown, s_gtwo, s_stwo)
    ]
    vec = jnp.concatenate([v.reshape(ndp, -1) for v in vec], axis=1)
    vec = lax.psum(lax.psum_scatter(vec, "dp", scatter_dimension=0, tiled=True), "ctx").reshape(-1)
    grads, pos = [], 0
    for size in sizes:
        grads.append(vec[pos : pos + size])
        pos += size
    g_bqv, g_bout, g_gone, g_sone, g_bup, g_bdown, g_gtwo, g_stwo = grads
    return (
        output, grad_input, sum_ctx(share_qkv), g_bqv, sum_ctx(share_out), g_bout, g_gone, g_sone,
        sum_ctx(share_up), g_bup, sum_ctx(share_down), g_bdown, g_gtwo, g_stwo,
    )


def solution(mesh):
    row = P("dp", "ctx", None)
    mat = P("dp", None)
    vec = P("dp")
    weights = (mat, vec, mat, vec, vec, vec, mat, vec, mat, vec, vec, vec)
    return jax.shard_map(
        shards, mesh=mesh, in_specs=(row, vec) + weights + (row,), out_specs=(row, row) + weights, check_vma=False
    )
```

```python
import functools

import jax
import jax.numpy as jnp
from jax import lax
from jax.experimental import pallas as pl
from jax.experimental.pallas import tpu as pltpu
from jax.sharding import PartitionSpec as P

HD = 64
NEG = -1e30
EPS = 1e-06
BF = jnp.bfloat16
F32 = jnp.float32
MIB = 1024 * 1024
COSTS = {'qkv': 13, 'out': 10, 'up': 23, 'down': 21, 'hidden': 18, 'first': 23, 'input': 14, 'attend': 24, 'attend_back': 21, 'gd_away': 11, 'gd_keep': 11, 'gu_away': 11, 'gu_keep': 11, 'gb_away': 10, 'gb_keep': 10, 'gc_away': 8, 'gc_keep': 8}


def cost(name):
    return pl.CostEstimate(flops=COSTS[name] * 1000000000, bytes_accessed=1000000, transcendentals=0)


ANY = pl.BlockSpec(memory_space=pl.ANY)


def swap(x, axis, bit):
    n = lax.axis_size(axis)
    return lax.ppermute(x, axis, [(i, i ^ bit) for i in range(n)])


def after(x, *others):
    return lax.optimization_barrier((x,) + others)[0]


def sync(*values):
    return lax.optimization_barrier(values)


def gather_near(own):
    if lax.axis_size("dp") != 8:
        return ()
    return swap(own, "dp", 2), swap(own, "dp", 4)


def gather_far(near):
    if not near:
        return ()
    half = near[0].shape[1] // 2
    return swap(near[0][:, :half], "dp", 4), swap(near[1][:, half:], "dp", 2)


def gather_stack(own, near, far):
    if near:
        return jnp.stack([own, near[0], near[1], jnp.concatenate(far, axis=1)])
    mine = own[None]
    bit = 2
    while bit < lax.axis_size("dp"):
        mine = jnp.concatenate([mine, swap(mine, "dp", bit)])
        bit *= 2
    return mine


def gather_direct(own):
    if lax.axis_size("dp") != 8:
        return (own,)
    return (own,) + tuple(swap(own, "dp", bit) for bit in (2, 4, 6))


def add_low(*parts):
    total = parts[0].astype(F32)
    for part in parts[1:]:
        total = total + part.astype(F32)
    return total.astype(BF)


def reduce_any(grad):
    n = lax.axis_size("dp")
    me = lax.axis_index("dp")
    rows = grad.shape[0] // n
    width = grad.shape[1]

    def stack(odd):
        return jnp.stack(
            [lax.dynamic_slice(grad, ((me ^ (2 * k + odd)) * rows, 0), (rows, width)) for k in range(n // 2)]
        )

    mine = add_low(stack(0), swap(stack(1), "dp", 1))
    bit = n // 2
    while bit > 1:
        keep = mine.shape[0] // 2
        mine = add_low(mine[:keep], swap(mine[keep:], "dp", bit))
        bit //= 2
    return mine[0]


def send_far(sums):
    return swap(sums[3], "dp", 4), swap(sums[4], "dp", 2)


def send_near(sums, far):
    own, to_x, to_y = sums[:3]
    cut = far[0].shape[1]
    to_x = jnp.concatenate([add_low(to_x[:, :cut], far[0]), to_x[:, cut:]], axis=1)
    to_y = jnp.concatenate([to_y[:, :cut], add_low(to_y[:, cut:], far[1])], axis=1)
    return swap(to_x, "dp", 2), swap(to_y, "dp", 4)


def sum_ctx(share):
    if lax.axis_size("ctx") != 4:
        return lax.psum(share.astype(F32), "ctx").astype(BF)
    inner = add_low(share, send_in(share))
    total = add_low(inner, send_mid(inner))
    return pick(total, send_out(total))


def send_in(share):
    return lax.ppermute(share, "ctx", [(0, 1), (3, 2)])


def send_mid(inner):
    return lax.ppermute(inner, "ctx", [(1, 2), (2, 1)])


def send_out(total):
    return lax.ppermute(total, "ctx", [(1, 0), (2, 3)])


def pick(total, outer):
    place = lax.axis_index("ctx")
    return jnp.where((place == 0) | (place == 3), outer, total)


def to_sequences(block):
    n = lax.axis_size("ctx")
    return lax.all_to_all(block.reshape((n, -1) + block.shape[1:]), "ctx", 0, 0, tiled=True)


def part_of(block, j):
    n = lax.axis_size("ctx")
    per = block.shape[0] // n
    return lax.dynamic_slice_in_dim(block, (lax.axis_index("ctx") ^ j) * per, per, axis=0)


def put_slots(pieces, dtype):
    n = len(pieces)
    me = lax.axis_index("ctx")
    per = pieces[0].shape[0]
    out = jnp.zeros((n * per,) + pieces[0].shape[1:], dtype)
    for j in range(n):
        out = lax.dynamic_update_slice_in_dim(out, pieces[j].astype(dtype), (me ^ j) * per, axis=0)
    return out


def trade(block, j):
    return swap(block, "ctx", j)


def nn(left, right):
    return jnp.dot(left, right, preferred_element_type=F32)


def nt(left, right):
    return lax.dot_general(left, right, (((1,), (1,)), ((), ())), preferred_element_type=F32)


def tn(left, right):
    return lax.dot_general(left, right, (((0,), (0,)), ((), ())), preferred_element_type=F32)


def fold(rows):
    return jnp.sum(rows.reshape(rows.shape[0] // 8, 8, rows.shape[1]), axis=0)


def fetch(stacks, whole, sems, me, rows, first):
    copies = []
    width = whole.shape[1]
    for odd, stack in enumerate(stacks):
        count = stack.shape[0]
        for k in range(count):
            start = pl.multiple_of((me ^ (2 * k + odd)) * rows, rows)
            copies.append(
                pltpu.make_async_copy(
                    stack.at[k, pl.ds(0, rows), pl.ds(first, width)], whole.at[pl.ds(start, rows)], sems.at[odd * count + k]
                )
            )
    for copy in copies:
        copy.start()
    for copy in copies:
        copy.wait()


def row_spec(tile, width):
    return pl.BlockSpec((tile, width), lambda i, *_: (i, 0))


def one_spec(height, width):
    return pl.BlockSpec((height, width), lambda i, *_: (0, 0))


def dense(body, name, meta, rows, tile, row_ins, vec_ins, weights, row_outs, sums):
    stacks = [s for w in weights for s in w[:2]]
    scratch = []
    for mine, other, r, _, width in weights:
        count = mine.shape[0]
        scratch.append(pltpu.VMEM((2 * count * r, width), BF))
        scratch.append(pltpu.SemaphoreType.DMA((2 * count,)))
    n_row, n_vec, n_stack = len(row_ins), len(vec_ins), len(stacks)
    n_out, n_sum = len(row_outs), len(sums)

    def kernel(meta_ref, *refs):
        pos = 0
        groups = []
        for count in (n_row, n_vec, n_stack, n_out, n_sum, 2 * len(weights)):
            groups.append(refs[pos : pos + count])
            pos += count
        row_refs, vec_refs, stack_refs, out_refs, sum_refs, scratch_refs = groups

        @pl.when(pl.program_id(0) == 0)
        def _():
            for w in range(len(weights)):
                fetch(stack_refs[2 * w : 2 * w + 2], scratch_refs[2 * w], scratch_refs[2 * w + 1], meta_ref[0], weights[w][2], weights[w][3])
            for ref in sum_refs:
                ref[...] = jnp.zeros_like(ref)

        body(meta_ref, row_refs, vec_refs, scratch_refs[::2], out_refs, sum_refs)

    in_specs = (
        [row_spec(tile, a.shape[-1]) if a.ndim == 2 else pl.BlockSpec((a.shape[0], tile, a.shape[2]), lambda i, *_: (0, i, 0)) for a in row_ins]
        + [one_spec(1, v.shape[1]) for v in vec_ins]
        + [ANY] * n_stack
    )
    out_specs = [row_spec(tile, w) for w, _ in row_outs] + [one_spec(8, w) for w in sums]
    out_shape = [jax.ShapeDtypeStruct((rows, w), d) for w, d in row_outs] + [
        jax.ShapeDtypeStruct((8, w), F32) for w in sums
    ]
    return pl.pallas_call(
        kernel,
        grid_spec=pltpu.PrefetchScalarGridSpec(
            num_scalar_prefetch=1,
            grid=(rows // tile,),
            in_specs=in_specs,
            out_specs=out_specs,
            scratch_shapes=scratch,
        ),
        out_shape=out_shape,
        compiler_params=pltpu.CompilerParams(vmem_limit_bytes=56 * MIB, dimension_semantics=("arbitrary",)),
        cost_estimate=cost(name),
        name=name,
    )(meta, *row_ins, *vec_ins, *stacks)


def qkv_body(meta, rows, vecs, whole, outs, sums):
    (x,) = rows
    (bias,) = vecs
    width = whole[0].shape[1]
    for c in range(0, width, 1024):
        outs[0][:, c : c + 1024] = (nn(x[...], whole[0][:, c : c + 1024]) + bias[:, c : c + 1024]).astype(BF)


def out_body(meta, rows, vecs, whole, outs, sums):
    mixed, x = rows
    bias, gain, shift = vecs
    total = x[...].astype(F32) + (nn(mixed[...], whole[0][...]) + bias[...])
    centre = total - jnp.mean(total, axis=-1, keepdims=True)
    inverse = lax.rsqrt(jnp.mean(centre * centre, axis=-1, keepdims=True) + EPS)
    normed = centre * inverse
    outs[0][...] = normed
    outs[1][...] = jnp.broadcast_to(inverse, outs[1].shape)
    outs[2][...] = (normed * gain[...] + shift[...]).astype(BF)


def up_body(meta, rows, vecs, whole, outs, sums):
    (low,) = rows
    (bias,) = vecs
    width = whole[0].shape[1]
    step = 512
    for c in range(0, width, step):
        cols = slice(c, c + step)
        hidden = nn(low[...], whole[0][:, cols]) + bias[:, cols]
        cdf = 0.5 + 0.5 * lax.erf(hidden * 0.7071067811865476)
        pdf = jnp.exp(-0.5 * hidden * hidden) * 0.3989422804014327
        outs[0][:, cols] = (hidden * cdf).astype(BF)
        outs[1][:, cols] = (cdf + hidden * pdf).astype(BF)


def down_body(blk, per, meta, rows, vecs, whole, outs, sums):
    active, normed_one, cot = rows
    bias, gain_one, shift_one, gain, shift = vecs
    total = (normed_one[...] * gain_one[...] + shift_one[...]) + (nn(active[...], whole[0][...]) + bias[...])
    centre = total - jnp.mean(total, axis=-1, keepdims=True)
    inverse = lax.rsqrt(jnp.mean(centre * centre, axis=-1, keepdims=True) + EPS)
    normed = centre * inverse
    place = meta[2 + pl.program_id(0)]
    at = lax.broadcasted_iota(jnp.int32, (total.shape[0], 1), 0)
    valid = jnp.zeros(at.shape, jnp.bool_)
    for s in range(per):
        here = at - s * blk
        valid = valid | ((here >= 0) & (here < blk) & (here + place < meta[2 + pl.num_programs(0) + s]))
    keep = jnp.where(valid, 1.0, 0.0)
    outs[0][...] = ((normed * gain[...] + shift[...]) * keep).astype(BF)
    grad = cot[...].astype(F32) * keep
    sums[0][...] += fold(grad * normed)
    sums[1][...] += fold(grad)
    scaled = grad * gain[...]
    back = inverse * (
        scaled
        - jnp.mean(scaled, axis=-1, keepdims=True)
        - normed * jnp.mean(scaled * normed, axis=-1, keepdims=True)
    )
    low = back.astype(BF)
    outs[1][...] = back
    outs[2][...] = low
    sums[2][...] += fold(low.astype(F32))


def hidden_body(meta, rows, vecs, whole, outs, sums):
    second, deriv = rows
    width = deriv.shape[1]
    step = 512
    for c in range(0, width, step):
        cols = slice(c, c + step)
        low = (nt(second[...], whole[0][cols, :]) * deriv[:, cols].astype(F32)).astype(BF)
        outs[0][:, cols] = low
        sums[0][:, cols] += fold(low.astype(F32))


def first_body(meta, rows, vecs, whole, outs, sums):
    hidden, sum_two, normed, inverse = rows
    (gain,) = vecs
    grad = sum_two[...] + nt(hidden[...], whole[0][...])
    n1 = normed[...]
    sums[0][...] += fold(grad * n1)
    sums[1][...] += fold(grad)
    scaled = grad * gain[...]
    back = inverse[:, 0:1] * (
        scaled - jnp.mean(scaled, axis=-1, keepdims=True) - n1 * jnp.mean(scaled * n1, axis=-1, keepdims=True)
    )
    low = back.astype(BF)
    outs[0][...] = back
    outs[1][...] = low
    sums[2][...] += fold(low.astype(F32))
    outs[2][...] = nt(low, whole[1][...]).astype(BF)


def input_body(meta, rows, vecs, whole, outs, sums):
    sum_one = rows[-1]
    width = sum_one.shape[1]
    total = sum_one[...]
    first = 0
    for proj in rows[:-1]:
        part = proj.shape[2]
        for c in range(3):
            start = c * width + first
            total = total + nt(proj[c], whole[0][:, start : start + part])
        first += part
    outs[0][...] = total.astype(BF)


def key_mask(meta, n, blk):
    s = pl.program_id(0)
    length = meta[2 + n + s]
    at = lax.broadcasted_iota(jnp.int32, (n * blk, 1), 0)
    ok = jnp.zeros(at.shape, jnp.bool_)
    for j in range(n):
        here = at - j * blk
        ok = ok | ((here >= 0) & (here < blk) & (here + meta[2 + j] < length))
    return ok


def attend_kernel(n, blk, meta, q_ref, k_ref, v_ref, mixed_ref, lse_ref):
    ok = key_mask(meta, n, blk)
    q2 = q_ref[...].reshape(n * blk, 2 * HD) * BF(HD ** (-0.5))
    k2 = k_ref[...].reshape(n * blk, 2 * HD)
    v2 = v_ref[...].reshape(n * blk, 2 * HD)
    outs = []
    for h in range(2):
        lanes = slice(h * HD, (h + 1) * HD)
        scores = jnp.where(ok, nt(k2[:, lanes], q2[:, lanes]), NEG)
        peak = jnp.max(scores, axis=0, keepdims=True)
        weights = jnp.exp(scores - peak)
        total = jnp.sum(weights, axis=0, keepdims=True)
        probs = (weights * (1.0 / total)).astype(BF)
        lse_ref[h : h + 1, :] = peak + jnp.log(total)
        outs.append(tn(probs, v2[:, lanes]))
    mixed_ref[...] = jnp.concatenate(outs, axis=1).astype(BF).reshape(mixed_ref.shape)


def attend_back_kernel(n, blk, meta, q_ref, k_ref, v_ref, g_ref, lse_ref, proj_ref, sum_ref):
    ok = key_mask(meta, n, blk)
    scale = HD ** (-0.5)
    q2 = q_ref[...].reshape(n * blk, 2 * HD) * BF(scale)
    k2 = k_ref[...].reshape(n * blk, 2 * HD)
    v2 = v_ref[...].reshape(n * blk, 2 * HD)
    g2 = g_ref[...].reshape(n * blk, 2 * HD)
    gq, gk, gv = [], [], []
    for h in range(2):
        lanes = slice(h * HD, (h + 1) * HD)
        q, k, v, g = q2[:, lanes], k2[:, lanes], v2[:, lanes], g2[:, lanes]
        scores = jnp.where(ok, nt(k, q), NEG)
        exact = jnp.exp(scores - lse_ref[h : h + 1, :])
        mixed = exact * nt(v, g)
        inner = jnp.sum(mixed, axis=0, keepdims=True)
        low = (mixed - exact * inner).astype(BF)
        gq.append(tn(low, k) * scale)
        gk.append(nn(low, q))
        gv.append(nn(exact.astype(BF), g))
    for c, parts in enumerate((gq, gk, gv)):
        whole = jnp.concatenate(parts, axis=1).astype(BF)
        proj_ref[c] = whole.reshape(proj_ref.shape[1:])
        sum_ref[c] = fold(whole.astype(F32))


def attend(meta, proj, n, per, blk):
    heads = proj.shape[-1] // 3 // (2 * HD)
    shaped = proj.reshape(n, per, blk, proj.shape[-1])

    def spec(c):
        return pl.BlockSpec((n, None, blk, 2 * HD), lambda s, h, *_: (0, s, 0, c * heads + h))

    mixed, lse = pl.pallas_call(
        functools.partial(attend_kernel, n, blk),
        grid_spec=pltpu.PrefetchScalarGridSpec(
            num_scalar_prefetch=1,
            grid=(per, heads),
            in_specs=[spec(0), spec(1), spec(2)],
            out_specs=[spec(0), pl.BlockSpec((None, None, 2, n * blk), lambda s, h, *_: (s, h, 0, 0))],
        ),
        out_shape=[
            jax.ShapeDtypeStruct((n, per, blk, heads * 2 * HD), BF),
            jax.ShapeDtypeStruct((per, heads, 2, n * blk), F32),
        ],
        compiler_params=pltpu.CompilerParams(vmem_limit_bytes=48 * MIB),
        cost_estimate=cost("attend"),
        name="attend",
    )(meta, shaped, shaped, shaped)
    return mixed.reshape(n * per * blk, -1), lse


def attend_back(meta, proj, grad, lse, n, per, blk, first, count):
    width = proj.shape[-1] // 3
    heads = width // (2 * HD)
    shaped = proj.reshape(n, per, blk, proj.shape[-1])

    def spec(c):
        return pl.BlockSpec((n, None, blk, 2 * HD), lambda s, h, *_: (0, s, 0, c * heads + first + h))

    out, sums = pl.pallas_call(
        functools.partial(attend_back_kernel, n, blk),
        grid_spec=pltpu.PrefetchScalarGridSpec(
            num_scalar_prefetch=1,
            grid=(per, count),
            in_specs=[spec(0), spec(1), spec(2), spec(0), pl.BlockSpec((None, None, 2, n * blk), lambda s, h, *_: (s, first + h, 0, 0))],
            out_specs=[
                pl.BlockSpec((3, n, None, blk, 2 * HD), lambda s, h, *_: (0, 0, s, 0, h)),
                pl.BlockSpec((3, None, 8, 2 * HD), lambda s, h, *_: (0, s, 0, h)),
            ],
        ),
        out_shape=[
            jax.ShapeDtypeStruct((3, n, per, blk, count * 2 * HD), BF),
            jax.ShapeDtypeStruct((3, per, 8, count * 2 * HD), F32),
        ],
        compiler_params=pltpu.CompilerParams(vmem_limit_bytes=48 * MIB),
        cost_estimate=cost("attend_back"),
        name="attend_back",
    )(meta, shaped, shaped, shaped, grad.reshape(n, per, blk, width), lse)
    return out.reshape(3, n * per * blk, count * 2 * HD), sums


def weight_grad(name, meta, odd, lefts, rights, chunk, come=None, extra=None):
    rows = lefts[0].shape[0]
    tall = lefts[0].shape[1] // 8
    plan = []
    for li, group in enumerate(rights):
        for right in group:
            for c in range((right.shape[0] if right.ndim == 3 else 1) * (right.shape[-1] // chunk)):
                plan.append((li, right, c))
    steps = len(plan)
    flat = [r for group in rights for r in group]
    firsts, pos = [], 0
    for right in flat:
        firsts.append(pos)
        pos += (right.shape[0] if right.ndim == 3 else 1) * (right.shape[-1] // chunk)
    owners = [li for li, group in enumerate(rights) for _ in group]
    below = 0 if extra is None else extra.shape[1]
    cut = (steps + 1) // 2
    n_left = len(lefts)

    def kernel(meta_ref, *refs):
        left_refs = refs[: 4 * n_left]
        pos = 4 * n_left
        right_refs = refs[pos : pos + len(flat)]
        pos += len(flat)
        extra_refs = refs[pos : pos + 4] if below else ()
        pos += len(extra_refs)
        come_ref = refs[pos] if come is not None else None
        pos += come is not None
        outs = refs[pos:-1]
        turned = refs[-1]
        c = pl.program_id(0)

        @pl.when(c == 0)
        def _():
            for i in range(4 * n_left):
                turned[i * tall : (i + 1) * tall, :] = left_refs[i][...].T

        def store(total):
            for k in range(4):
                part = total[k * tall : (k + 1) * tall]
                if come is None:
                    outs[0][k, 0:tall, :] = part.astype(BF)
                    if below:
                        outs[0][k, tall:, :] = extra_refs[k][...]
                    continue
                part = (part + come_ref[k, 0:tall, :].astype(F32)).astype(BF)
                if below:
                    low = (extra_refs[k][...].astype(F32) + come_ref[k, tall:, :].astype(F32)).astype(BF)
                if k < 3:
                    outs[k][0:tall, :] = part
                    if below:
                        outs[k][tall:, :] = low
                    continue

                @pl.when(c < cut)
                def _():
                    outs[3][0:tall, :] = part
                    if below:
                        outs[3][tall:, :] = low

                @pl.when(c >= cut)
                def _():
                    outs[4][0:tall, :] = part
                    if below:
                        outs[4][tall:, :] = low

        for i, right_ref in enumerate(right_refs):
            last = firsts[i + 1] if i + 1 < len(flat) else steps
            li = owners[i]

            @pl.when((c >= firsts[i]) & (c < last))
            def _(right_ref=right_ref, li=li):
                store(nn(turned[4 * li * tall : 4 * (li + 1) * tall, :], right_ref[...]))

    def left_spec(k):
        return pl.BlockSpec((rows, tall), lambda c, m: (0, m[0] ^ (2 * k + odd)))

    def right_spec(i, right):
        last = (firsts[i + 1] if i + 1 < len(flat) else steps) - 1
        inner = right.shape[-1] // chunk

        def place(c):
            return jnp.clip(c, firsts[i], last) - firsts[i]

        if right.ndim == 3:
            return pl.BlockSpec((None, rows, chunk), lambda c, m: (place(c) // inner, 0, place(c) % inner))
        return pl.BlockSpec((rows, chunk), lambda c, m: (0, place(c)))

    def extra_spec(k):
        return pl.BlockSpec((None, below, chunk), lambda c, m: (m[0] ^ (2 * k + odd), 0, c))

    high = tall + below
    four = pl.BlockSpec((4, high, chunk), lambda c, m: (0, 0, c))
    in_specs = [left_spec(k) for _ in lefts for k in range(4)] + [right_spec(i, r) for i, r in enumerate(flat)]
    args = [left for left in lefts for _ in range(4)] + flat
    if below:
        in_specs += [extra_spec(k) for k in range(4)]
        args += [extra] * 4
    if come is None:
        out_specs = [four]
        out_shape = [jax.ShapeDtypeStruct((4, high, steps * chunk), BF)]
    else:
        in_specs.append(four)
        args.append(come)
        out_specs = [pl.BlockSpec((high, chunk), lambda c, m: (0, c))] * 3 + [
            pl.BlockSpec((high, chunk), lambda c, m: (0, jnp.minimum(c, cut - 1))),
            pl.BlockSpec((high, chunk), lambda c, m: (0, jnp.maximum(c - cut, 0))),
        ]
        out_shape = [jax.ShapeDtypeStruct((high, steps * chunk), BF)] * 3 + [
            jax.ShapeDtypeStruct((high, cut * chunk), BF),
            jax.ShapeDtypeStruct((high, (steps - cut) * chunk), BF),
        ]
    return pl.pallas_call(
        kernel,
        grid_spec=pltpu.PrefetchScalarGridSpec(
            num_scalar_prefetch=1,
            grid=(steps,),
            in_specs=in_specs,
            out_specs=out_specs,
            scratch_shapes=[pltpu.VMEM((4 * n_left * tall, rows), BF)],
        ),
        out_shape=out_shape,
        compiler_params=pltpu.CompilerParams(vmem_limit_bytes=56 * MIB),
        cost_estimate=cost(name),
        name=name,
    )(meta, *args)


def shards(
    tokens, lengths, w_qkv, bias_qv, w_out, bias_out, gain_one, shift_one,
    w_up, bias_up, w_down, bias_down, gain_two, shift_two, cotangent,
):
    seqs, blk, width = tokens.shape
    n = lax.axis_size("ctx")
    ndp = lax.axis_size("dp")
    me = lax.axis_index("dp")
    place = lax.axis_index("ctx")
    per = seqs // n
    rows = seqs * blk
    tile = per * blk
    ff = w_up.shape[1]
    thin = w_qkv.shape[0]
    tuned = ndp == 8
    half = width // (2 * HD) // 2

    own = lax.dynamic_slice_in_dim(lengths, place * per, per)
    meta = jnp.concatenate(
        [jnp.stack([me, place]).astype(jnp.int32), jnp.arange(n, dtype=jnp.int32) * blk, own]
    )

    vectors = (bias_qv, bias_out, gain_one, shift_one, bias_up, bias_down, gain_two, shift_two)
    sizes = [v.shape[0] for v in vectors]
    count = sum(sizes)
    line = jnp.pad(jnp.concatenate(vectors).reshape(1, count), ((0, 15), (0, 3 * width - count)))
    qkv_own = jnp.concatenate([w_qkv, line])
    qkv_parts = gather_direct(qkv_own)
    mid_own = jnp.concatenate([w_out, w_up], axis=1)
    mid_near = gather_near(mid_own)
    x = to_sequences(tokens).reshape(rows, width)
    x, qkv_parts, mid_near, cotangent = sync(x, qkv_parts, mid_near, cotangent)
    qkv_mine = jnp.stack(qkv_parts) if tuned else gather_stack(qkv_parts[0], (), ())
    qkv_other = swap(qkv_mine, "dp", 1)
    mid_far = gather_far(mid_near)
    cot_1 = trade(part_of(cotangent, 1), 1)

    both = jnp.concatenate([qkv_mine[:, thin, :count], qkv_other[:, thin, :count]])
    index = jnp.arange(ndp, dtype=jnp.int32) ^ me
    packed = jnp.take(both, (index >> 1) + (index & 1) * (ndp // 2), axis=0).astype(F32)
    fulls, pos = [], 0
    for size in sizes:
        fulls.append(packed[:, pos : pos + size].reshape(1, ndp * size))
        pos += size
    bqv, bout, gone, sone, bup, bdown, gtwo, stwo = fulls
    bqkv = jnp.concatenate([bqv[:, :width], jnp.zeros((1, width), F32), bqv[:, width:]], axis=1)

    qkv_w = (qkv_mine, qkv_other, thin, 0, 3 * width)
    (proj,) = dense(qkv_body, "qkv", meta, rows, tile, [x], [bqkv], [qkv_w], [(3 * width, BF)], [])
    proj, mid_far, cot_1, w_down, cotangent = sync(proj, mid_far, cot_1, w_down, cotangent)
    mid_mine = gather_stack(mid_own, mid_near, mid_far)
    mid_other = swap(mid_mine, "dp", 1)
    down_near = gather_near(w_down)
    cot_2 = trade(part_of(cotangent, 2), 2)
    mixed, lse = attend(meta, proj, n, per, blk)
    mixed, mid_other, down_near, cot_2 = sync(mixed, mid_other, down_near, cot_2)
    out_w = (mid_mine, mid_other, thin, 0, width)
    up_w = (mid_mine, mid_other, thin, width, ff)
    down_far = gather_far(down_near)
    normed_one, inverse_one, first_low = dense(
        out_body, "out", meta, rows, tile, [mixed, x], [bout, gone, sone], [out_w], [(width, F32), (128, F32), (width, BF)], []
    )
    first_low, down_far, cotangent = sync(first_low, down_far, cotangent)
    down_mine = gather_stack(w_down, down_near, down_far)
    down_other = swap(down_mine, "dp", 1)
    cot_3 = trade(part_of(cotangent, 3), 3)
    active, deriv = dense(up_body, "up", meta, rows, tile, [first_low], [bup], [up_w], [(ff, BF), (ff, BF)], [])
    active, down_other, cot_3 = sync(active, down_other, cot_3)
    down_w = (down_mine, down_other, w_down.shape[0], 0, width)
    cot = put_slots([part_of(cotangent, 0), cot_1, cot_2, cot_3], BF).reshape(rows, width)
    out_parts, sum_two, second, s_gtwo, s_stwo, s_bdown = dense(
        functools.partial(down_body, blk, per), "down", meta, rows, tile, [active, normed_one, cot],
        [bdown, gone, sone, gtwo, stwo], [down_w], [(width, BF), (width, F32), (width, BF)], [width] * 3,
    )
    out_parts = out_parts.reshape(n * per, blk, width)
    out_own = part_of(out_parts, 0)
    out_2 = trade(part_of(out_parts, 2), 2)

    come = ()
    if tuned:
        (away,) = weight_grad("gd_away", meta, 1, [active], [[second]], 256)
        come = swap(away, "dp", 1)
        second = after(second, away)
    hidden, s_bup = dense(hidden_body, "hidden", meta, rows, tile, [second, deriv], [], [down_w], [(ff, BF)], [ff])
    hidden, come, out_2, out_parts = sync(hidden, come, out_2, out_parts)
    out_1 = trade(part_of(out_parts, 1), 1)
    d_far, d_near = (), ()
    if tuned:
        d_sums = weight_grad("gd_keep", meta, 0, [active], [[second]], 256, come=come)
        d_far = send_far(d_sums)
        (away,) = weight_grad("gu_away", meta, 1, [first_low], [[after(hidden, d_sums[0])]], 512)
        hidden = after(hidden, away)
        away, d_far, out_1 = sync(away, d_far, out_1)
        come = swap(away, "dp", 1)
    hidden, d_far, out_1, out_parts = sync(hidden, d_far, out_1, out_parts)
    if tuned:
        d_near = send_near(d_sums, d_far)
    out_3 = trade(part_of(out_parts, 3), 3)
    sum_one, branch, g_mixed, s_gone, s_sone, s_bout = dense(
        first_body, "first", meta, rows, tile, [hidden, sum_two, normed_one, inverse_one], [gone], [up_w, out_w],
        [(width, F32), (width, BF), (width, BF)], [width] * 3,
    )
    branch, g_mixed, come, d_near, out_3 = sync(branch, g_mixed, come, d_near, out_3)
    output = put_slots([out_own, out_1, out_2, out_3], BF)
    d_in, u_far = (), ()
    if tuned:
        d_share = add_low(d_sums[0], *d_near)
        d_in = send_in(d_share)
        u_sums = weight_grad("gu_keep", meta, 0, [first_low], [[hidden]], 512, come=come)
        u_far = send_far(u_sums)
        g_mixed = after(g_mixed, u_sums[0])
    p_one, s_one = attend_back(meta, proj, g_mixed, lse, n, per, blk, 0, half)
    p_one, d_in, u_far = sync(p_one, d_in, u_far)
    d_mid, u_near = (), ()
    if tuned:
        u_near = send_near(u_sums, u_far)
        d_inner = add_low(d_share, d_in)
        d_mid = send_mid(d_inner)
        (away,) = weight_grad("gb_away", meta, 1, [x, mixed], [[p_one], [branch]], 256)
        come = swap(away, "dp", 1)
        g_mixed = after(g_mixed, away)
    p_two, s_two = attend_back(meta, proj, g_mixed, lse, n, per, blk, half, half)
    p_two, come, u_near, d_mid = sync(p_two, come, u_near, d_mid)

    s_proj = jnp.concatenate([jnp.sum(s_one, axis=(1, 2)), jnp.sum(s_two, axis=(1, 2))], axis=1)
    vec = [jnp.concatenate([s_proj[0], s_proj[2]])] + [
        jnp.sum(s, axis=0) for s in (s_bout, s_gone, s_sone, s_bup, s_bdown, s_gtwo, s_stwo)
    ]
    vec = jnp.concatenate([v.reshape(ndp, -1) for v in vec], axis=1)

    d_out, u_in, come_two = (), (), ()
    if tuned:
        d_total = add_low(d_inner, d_mid)
        d_out = send_out(d_total)
        u_share = add_low(u_sums[0], *u_near)
        u_in = send_in(u_share)
        extra = jnp.pad(vec[:, None, :].astype(BF), ((0, 0), (0, 15), (0, 3 * (width // 2) - count)))
        (away,) = weight_grad("gc_away", meta, 1, [x], [[p_two]], 256, extra=extra)
        come_two = swap(away, "dp", 1)
        sum_one = after(sum_one, away)
    (grad_in,) = dense(input_body, "input", meta, rows, tile, [p_one, p_two, sum_one], [], [qkv_w], [(width, BF)], [])
    grad_in, d_out, u_in, come_two = sync(grad_in, d_out, u_in, come_two)
    grad_in = grad_in.reshape(n * per, blk, width)
    in_own = part_of(grad_in, 0)
    in_2, in_3 = trade(part_of(grad_in, 2), 2), trade(part_of(grad_in, 3), 3)
    if tuned:
        u_inner = add_low(u_share, u_in)
        u_mid = send_mid(u_inner)
        b_sums = weight_grad("gb_keep", meta, 0, [x, mixed], [[p_one], [branch]], 256, come=after(come, grad_in))
        b_sums, come_two, u_mid = sync(b_sums, come_two, u_mid)
        b_far = send_far(b_sums)
        c_sums = weight_grad("gc_keep", meta, 0, [x], [[p_two]], 256, come=come_two, extra=extra)
        c_sums, b_far = sync(c_sums, b_far)
        b_near = send_near(b_sums, b_far)
        c_sums, b_near = sync(c_sums, b_near)
        c_far = send_far(c_sums)
        b_share = add_low(b_sums[0], *b_near)
        b_in = send_in(b_share)
        c_near = send_near(c_sums, c_far)
        c_near, b_in, in_2, in_3, grad_in = sync(c_near, b_in, in_2, in_3, grad_in)
    in_1 = trade(part_of(grad_in, 1), 1)
    if tuned:
        c_share = add_low(c_sums[0], *c_near)
        c_in = send_in(c_share)
        b_inner = add_low(b_share, b_in)
        b_mid = send_mid(b_inner)
        u_total = add_low(u_inner, u_mid)
        u_out = send_out(u_total)
        b_mid, c_in, u_out, in_1 = sync(b_mid, c_in, u_out, in_1)
        b_total = add_low(b_inner, b_mid)
        b_out = send_out(b_total)
        c_inner = add_low(c_share, c_in)
        c_total = add_low(c_inner, send_mid(c_inner))
        d_total = pick(d_total, d_out)
        u_total = pick(u_total, u_out)
        b_total = pick(b_total, b_out)
        c_total = pick(c_total, send_out(c_total)).astype(F32)
        b_total = b_total.astype(F32)
        part = width // 2
        pieces = []
        for c in range(3):
            pieces += [b_total[:, c * part : (c + 1) * part], c_total[:thin, c * part : (c + 1) * part]]
        g_qkv = jnp.concatenate(pieces, axis=1)
        g_out = b_total[:, 3 * part :]
        g_up = u_total.astype(F32)
        g_down = d_total.astype(F32)
        vec = c_total[thin, :count]
    else:
        def whole(*products):
            return jnp.concatenate([tn(a, b).astype(BF) for a, b in products], axis=1)

        def total(grad):
            return sum_ctx(reduce_any(grad)).astype(F32)

        g_down = total(whole((active, second)))
        g_up = total(whole((first_low, hidden)))
        g_out = total(whole((mixed, branch)))
        g_qkv = total(whole(*[(x, p[c]) for c in range(3) for p in (p_one, p_two)]))
        vec = lax.psum(lax.psum_scatter(vec, "dp", scatter_dimension=0, tiled=True), "ctx").reshape(-1)
    grads, pos = [], 0
    for size in sizes:
        grads.append(vec[pos : pos + size])
        pos += size
    g_bqv, g_bout, g_gone, g_sone, g_bup, g_bdown, g_gtwo, g_stwo = grads
    grad_input = put_slots([in_own, in_1, in_2, in_3], F32)
    return (
        output, grad_input, g_qkv, g_bqv, g_out, g_bout, g_gone, g_sone, g_up, g_bup, g_down, g_bdown, g_gtwo, g_stwo,
    )


def solution(mesh):
    row = P("dp", "ctx", None)
    mat = P("dp", None)
    vec = P("dp")
    weights = (mat, vec, mat, vec, vec, vec, mat, vec, mat, vec, vec, vec)
    return jax.shard_map(
        shards, mesh=mesh, in_specs=(row, vec) + weights + (row,), out_specs=(row, row) + weights, check_vma=False
    )
```

```python
import functools

import jax
import jax.numpy as jnp
from jax import lax
from jax.experimental import pallas as pl
from jax.experimental.pallas import tpu as pltpu
from jax.sharding import PartitionSpec as P

HD = 64
GROUP = 4
NEG = -1e30
EPS = 1e-06
BF = jnp.bfloat16
F32 = jnp.float32
MIB = 1024 * 1024
COSTS = {'qkv': 13, 'out': 10, 'up': 23, 'down': 21, 'hidden': 18, 'first': 23, 'input': 14, 'attend': 24, 'attend_back': 21, 'gd_away': 11, 'gd_keep': 11, 'gu_away': 11, 'gu_keep': 11, 'gb_away': 14, 'gb_keep': 3, 'gc_away': 8, 'gc_keep': 8}


def cost(name):
    return pl.CostEstimate(flops=COSTS[name] * 1000000000, bytes_accessed=1000000, transcendentals=0)


ANY = pl.BlockSpec(memory_space=pl.ANY)


def swap(x, axis, bit):
    n = lax.axis_size(axis)
    return lax.ppermute(x, axis, [(i, i ^ bit) for i in range(n)])


def after(x, *others):
    return lax.optimization_barrier((x,) + others)[0]


def sync(*values):
    return lax.optimization_barrier(values)


def gather_near(own):
    if lax.axis_size("dp") != 8:
        return ()
    return swap(own, "dp", 2), swap(own, "dp", 4)


def gather_far(near):
    if not near:
        return ()
    half = near[0].shape[1] // 2
    return swap(near[0][:, :half], "dp", 4), swap(near[1][:, half:], "dp", 2)


def gather_stack(own, near, far):
    if near:
        return jnp.stack([own, near[0], near[1], jnp.concatenate(far, axis=1)])
    mine = own[None]
    bit = 2
    while bit < lax.axis_size("dp"):
        mine = jnp.concatenate([mine, swap(mine, "dp", bit)])
        bit *= 2
    return mine


def add_low(*parts):
    total = parts[0].astype(F32)
    for part in parts[1:]:
        total = total + part.astype(F32)
    return total.astype(BF)


def reduce_any(grad):
    n = lax.axis_size("dp")
    me = lax.axis_index("dp")
    rows = grad.shape[0] // n
    width = grad.shape[1]

    def stack(odd):
        return jnp.stack(
            [lax.dynamic_slice(grad, ((me ^ (2 * k + odd)) * rows, 0), (rows, width)) for k in range(n // 2)]
        )

    mine = add_low(stack(0), swap(stack(1), "dp", 1))
    bit = n // 2
    while bit > 1:
        keep = mine.shape[0] // 2
        mine = add_low(mine[:keep], swap(mine[keep:], "dp", bit))
        bit //= 2
    return mine[0]


def send_far(sums):
    return swap(sums[3], "dp", 4), swap(sums[4], "dp", 2)


def send_near(sums, far):
    own, to_x, to_y = sums[:3]
    cut, width = far[0].shape[1], to_x.shape[1]
    to_x = add_low(to_x, jnp.pad(far[0], ((0, 0), (0, width - cut))))
    to_y = add_low(to_y, jnp.pad(far[1], ((0, 0), (cut, 0))))
    return swap(to_x, "dp", 2), swap(to_y, "dp", 4)


def halves_ctx(share, bit):
    half = share.shape[1] // 2
    mine = (lax.axis_index("ctx") // bit) % 2
    keep = lax.dynamic_slice_in_dim(share, mine * half, half, axis=1)
    return keep, lax.dynamic_slice_in_dim(share, (1 - mine) * half, half, axis=1)


def halve_ctx(share, bit):
    keep, away = halves_ctx(share, bit)
    return add_low(keep, swap(away, "ctx", bit))


def join_ctx(half, other, bit):
    low = (lax.axis_index("ctx") // bit) % 2 == 0
    return jnp.concatenate([jnp.where(low, half, other), jnp.where(low, other, half)], axis=1)


def whole_ctx(half, bit):
    return join_ctx(half, swap(half, "ctx", bit), bit)


def to_sequences(block):
    return lax.all_to_all(block, "ctx", 0, 0, tiled=True)


def part_of(block, j, axis=0):
    n = lax.axis_size("ctx")
    per = block.shape[axis] // n
    return lax.dynamic_slice_in_dim(block, (lax.axis_index("ctx") ^ j) * per, per, axis=axis)


def put_slots(pieces, per, dtype):
    n = lax.axis_size("ctx")
    out = jnp.zeros((n * per,) + pieces[0][2].shape[1:], dtype)
    for j, first, piece in pieces:
        start = (lax.axis_index("ctx") ^ j) * per + first
        out = lax.dynamic_update_slice_in_dim(out, piece.astype(dtype), start, axis=0)
    return out


def put_positions(pieces):
    n = len(pieces)
    per, blk, width = pieces[0].shape
    out = jnp.zeros((per, n * blk, width), pieces[0].dtype)
    for j in range(n):
        out = lax.dynamic_update_slice_in_dim(out, pieces[j], (lax.axis_index("ctx") ^ j) * blk, axis=1)
    return out


def trade(block, j):
    return swap(block, "ctx", j)


def nn(left, right):
    return jnp.dot(left, right, preferred_element_type=F32)


def nt(left, right):
    return lax.dot_general(left, right, (((1,), (1,)), ((), ())), preferred_element_type=F32)


def tn(left, right):
    return lax.dot_general(left, right, (((0,), (0,)), ((), ())), preferred_element_type=F32)


def fold(rows):
    return jnp.sum(rows.reshape(rows.shape[0] // 8, 8, rows.shape[1]), axis=0)


class Weight:
    def __init__(self, stacks, whole, sems, me, rows, first, pieces):
        self.whole, self.pieces = whole, pieces
        self.step = whole.shape[1] // max(pieces, 1)
        self.copies, self.starts = [], []
        for odd, stack in enumerate(stacks):
            count = stack.shape[0]
            for k in range(count):
                start = pl.multiple_of((me ^ (2 * k + odd)) * rows, rows)
                self.starts.append(pl.ds(start, rows))
                for p in range(max(pieces, 1)):
                    here, there = pl.ds(first + p * self.step, self.step), pl.ds(p * self.step, self.step)
                    copy = pltpu.make_async_copy(
                        stack.at[k, pl.ds(0, rows), here], whole.at[self.starts[-1], there], sems.at[odd * count + k, p]
                    )
                    self.copies.append((k * 2 + odd, p, copy))
        self.wait_for = False

    def start(self):
        for _, _, copy in sorted(self.copies, key=lambda c: c[1] if self.pieces else c[0]):
            copy.start()

    def cols(self, p):
        if self.wait_for:
            for _, q, copy in self.copies:
                if q == p:
                    copy.wait()
        return slice(p * self.step, (p + 1) * self.step)

    def rows(self, c):
        _, _, copy = self.copies[c]
        if self.wait_for:
            copy.wait()
        return self.starts[c]


def row_spec(tile, width):
    return pl.BlockSpec((tile, width), lambda i, *_: (i, 0))


def one_spec(height, width):
    return pl.BlockSpec((height, width), lambda i, *_: (0, 0))


def dense(body, name, meta, rows, tile, row_ins, vec_ins, weights, row_outs, sums):
    stacks = [s for w in weights for s in w[:2]]
    scratch = []
    for mine, other, r, _, width, pieces in weights:
        count = mine.shape[0]
        scratch.append(pltpu.VMEM((2 * count * r, width), BF))
        scratch.append(pltpu.SemaphoreType.DMA((2 * count, max(pieces, 1))))
    n_row, n_vec, n_stack = len(row_ins), len(vec_ins), len(stacks)
    n_out, n_sum = len(row_outs), len(sums)

    def kernel(meta_ref, *refs):
        pos = 0
        groups = []
        for count in (n_row, n_vec, n_stack, n_out, n_sum, 2 * len(weights)):
            groups.append(refs[pos : pos + count])
            pos += count
        row_refs, vec_refs, stack_refs, out_refs, sum_refs, scratch_refs = groups

        whole = [
            Weight(stack_refs[2 * w : 2 * w + 2], scratch_refs[2 * w], scratch_refs[2 * w + 1], meta_ref[0], weights[w][2], weights[w][3], weights[w][5])
            for w in range(len(weights))
        ]

        def work(wait_for):
            for weight in whole:
                weight.wait_for = wait_for
            body(meta_ref, row_refs, vec_refs, whole, out_refs, sum_refs)

        @pl.when(pl.program_id(0) == 0)
        def _():
            for weight in whole:
                weight.start()
            for ref in sum_refs:
                ref[...] = jnp.zeros_like(ref)
            work(True)

        @pl.when(pl.program_id(0) > 0)
        def _():
            work(False)

    in_specs = (
        [row_spec(tile, a.shape[-1]) if a.ndim == 2 else pl.BlockSpec((a.shape[0], tile, a.shape[2]), lambda i, *_: (0, i, 0)) for a in row_ins]
        + [one_spec(1, v.shape[1]) for v in vec_ins]
        + [ANY] * n_stack
    )
    out_specs = [row_spec(tile, w) for w, _ in row_outs] + [one_spec(8, w) for w in sums]
    out_shape = [jax.ShapeDtypeStruct((rows, w), d) for w, d in row_outs] + [
        jax.ShapeDtypeStruct((8, w), F32) for w in sums
    ]
    return pl.pallas_call(
        kernel,
        grid_spec=pltpu.PrefetchScalarGridSpec(
            num_scalar_prefetch=1,
            grid=(rows // tile,),
            in_specs=in_specs,
            out_specs=out_specs,
            scratch_shapes=scratch,
        ),
        out_shape=out_shape,
        compiler_params=pltpu.CompilerParams(vmem_limit_bytes=60 * MIB, dimension_semantics=("arbitrary",)),
        cost_estimate=cost(name),
        name=name,
    )(meta, *row_ins, *vec_ins, *stacks)


def by_columns(left, weight):
    parts = []
    for p in range(weight.pieces):
        cols = weight.cols(p)
        parts.append(nn(left[...], weight.whole[:, cols]))
    return jnp.concatenate(parts, axis=1)


def by_columns_turned(left, weight):
    total = None
    for p in range(weight.pieces):
        cols = weight.cols(p)
        part = nt(left[:, cols], weight.whole[:, cols])
        total = part if total is None else total + part
    return total


def by_shards(left, weight):
    if weight.pieces:
        return by_columns(left, weight)
    if not weight.wait_for:
        return nn(left[...], weight.whole[...])
    total = None
    for c in range(len(weight.copies)):
        here = weight.rows(c)
        part = nn(left[:, here], weight.whole[here, :])
        total = part if total is None else total + part
    return total


def qkv_body(meta, rows, vecs, whole, outs, sums):
    (x,) = rows
    (bias,) = vecs
    for p in range(whole[0].pieces):
        cols = whole[0].cols(p)
        outs[0][:, cols] = (nn(x[...], whole[0].whole[:, cols]) + bias[:, cols]).astype(BF)


def out_body(meta, rows, vecs, whole, outs, sums):
    mixed, x = rows
    bias, gain, shift = vecs
    total = x[...].astype(F32) + (by_columns(mixed, whole[0]) + bias[...])
    centre = total - jnp.mean(total, axis=-1, keepdims=True)
    inverse = lax.rsqrt(jnp.mean(centre * centre, axis=-1, keepdims=True) + EPS)
    normed = centre * inverse
    outs[0][...] = normed
    outs[1][...] = jnp.broadcast_to(inverse, outs[1].shape)
    outs[2][...] = (normed * gain[...] + shift[...]).astype(BF)


def up_body(meta, rows, vecs, whole, outs, sums):
    (low,) = rows
    (bias,) = vecs
    for p in range(whole[0].pieces):
        cols = whole[0].cols(p)
        hidden = nn(low[...], whole[0].whole[:, cols]) + bias[:, cols]
        cdf = 0.5 + 0.5 * lax.erf(hidden * 0.7071067811865476)
        pdf = jnp.exp(-0.5 * hidden * hidden) * 0.3989422804014327
        outs[0][:, cols] = (hidden * cdf).astype(BF)
        outs[1][:, cols] = (cdf + hidden * pdf).astype(BF)


def down_body(seq, per, meta, rows, vecs, whole, outs, sums):
    active, normed_one, cot = rows
    bias, gain_one, shift_one, gain, shift = vecs
    total = (normed_one[...] * gain_one[...] + shift_one[...]) + (by_shards(active, whole[0]) + bias[...])
    centre = total - jnp.mean(total, axis=-1, keepdims=True)
    inverse = lax.rsqrt(jnp.mean(centre * centre, axis=-1, keepdims=True) + EPS)
    normed = centre * inverse
    tile = total.shape[0]
    at = lax.broadcasted_iota(jnp.int32, (tile, 1), 0) + pl.program_id(0) * tile
    valid = jnp.zeros(at.shape, jnp.bool_)
    for s in range(per):
        valid = valid | ((at >= s * seq) & (at < s * seq + meta[2 + s]))
    keep = jnp.where(valid, 1.0, 0.0)
    outs[0][...] = ((normed * gain[...] + shift[...]) * keep).astype(BF)
    grad = cot[...].astype(F32) * keep
    sums[0][...] += fold(grad * normed)
    sums[1][...] += fold(grad)
    scaled = grad * gain[...]
    back = inverse * (
        scaled
        - jnp.mean(scaled, axis=-1, keepdims=True)
        - normed * jnp.mean(scaled * normed, axis=-1, keepdims=True)
    )
    low = back.astype(BF)
    outs[1][...] = back
    outs[2][...] = low
    sums[2][...] += fold(low.astype(F32))


def hidden_body(meta, rows, vecs, whole, outs, sums):
    second, deriv = rows
    if whole[0].pieces:
        whole[0].cols(0)
        places = [slice(c, c + 512) for c in range(0, deriv.shape[1], 512)]
    else:
        places = range(len(whole[0].copies))
    for cols in places:
        if not whole[0].pieces:
            cols = whole[0].rows(cols)
        low = (nt(second[...], whole[0].whole[cols, :]) * deriv[:, cols].astype(F32)).astype(BF)
        outs[0][:, cols] = low
        sums[0][:, cols] += fold(low.astype(F32))


def first_body(meta, rows, vecs, whole, outs, sums):
    hidden, sum_two, normed, inverse = rows
    (gain,) = vecs
    grad = sum_two[...] + by_columns_turned(hidden, whole[0])
    n1 = normed[...]
    sums[0][...] += fold(grad * n1)
    sums[1][...] += fold(grad)
    scaled = grad * gain[...]
    back = inverse[:, 0:1] * (
        scaled - jnp.mean(scaled, axis=-1, keepdims=True) - n1 * jnp.mean(scaled * n1, axis=-1, keepdims=True)
    )
    low = back.astype(BF)
    outs[0][...] = back
    outs[1][...] = low
    sums[2][...] += fold(low.astype(F32))
    whole[1].cols(0)
    outs[2][...] = nt(low, whole[1].whole[...]).astype(BF)


def input_body(meta, rows, vecs, whole, outs, sums):
    sum_one = rows[-1]
    total = sum_one[...]
    parts = len(rows) - 1
    for p in range(whole[0].pieces):
        cols = whole[0].cols(p)
        total = total + nt(rows[p % parts][p // parts], whole[0].whole[:, cols])
    outs[0][...] = total.astype(BF)


def key_mask(meta, seq):
    at = lax.broadcasted_iota(jnp.int32, (seq, 1), 0)
    return at < meta[2 + pl.program_id(0)]


def attend_kernel(meta, q_ref, k_ref, v_ref, mixed_ref, lse_ref):
    seq, lanes = q_ref.shape
    ok = key_mask(meta, seq)
    q_all = q_ref[...] * BF(HD ** (-0.5))
    k_all, v_turned = k_ref[...], v_ref[...].T
    ones = jnp.ones((16, seq), BF)
    outs = []
    for h in range(lanes // HD):
        cols = slice(h * HD, (h + 1) * HD)
        scores = jnp.where(ok, nt(k_all[:, cols], q_all[:, cols]), NEG)
        peak = jnp.max(scores, axis=0, keepdims=True)
        weights = jnp.exp(scores - peak).astype(BF)
        both = nn(jnp.concatenate([v_turned[cols], ones], axis=0), weights)
        total = both[HD : HD + 1]
        lse_ref[h : h + 1, :] = peak + jnp.log(total)
        outs.append(both[:HD] * (1.0 / total))
    mixed_ref[...] = jnp.concatenate(outs, axis=0).T.astype(BF)


def attend_back_kernel(meta, q_ref, k_ref, v_ref, g_ref, mixed_ref, lse_ref, proj_ref, sum_ref):
    seq, lanes = q_ref.shape
    ok = key_mask(meta, seq)
    scale = HD ** (-0.5)
    q_all = q_ref[...] * BF(scale)
    k_all, v_all, g_all = k_ref[...], v_ref[...], g_ref[...]
    k_turned = k_all.T
    inners = (g_all.astype(F32) * mixed_ref[...].astype(F32)).T
    gq, gk, gv = [], [], []
    for h in range(lanes // HD):
        cols = slice(h * HD, (h + 1) * HD)
        q, k, v, g = q_all[:, cols], k_all[:, cols], v_all[:, cols], g_all[:, cols]
        exact = jnp.exp(jnp.where(ok, nt(k, q), NEG) - lse_ref[h : h + 1, :])
        inner = jnp.sum(inners[cols], axis=0, keepdims=True)
        low = (exact * (nt(v, g) - inner)).astype(BF)
        gq.append(nn(k_turned[cols], low) * scale)
        gk.append(nn(low, q))
        gv.append(nn(exact.astype(BF), g))
    wholes = (jnp.concatenate(gq, axis=0).T, jnp.concatenate(gk, axis=1), jnp.concatenate(gv, axis=1))
    for c, whole in enumerate(wholes):
        low = whole.astype(BF)
        proj_ref[c] = low
        sum_ref[c] = fold(low.astype(F32))


def attend(meta, proj, per, seq):
    lanes = GROUP * HD
    groups = proj.shape[-1] // 3 // lanes
    shaped = proj.reshape(per, seq, proj.shape[-1])

    def spec(c):
        return pl.BlockSpec((None, seq, lanes), lambda s, h, *_: (s, 0, c * groups + h))

    mixed, lse = pl.pallas_call(
        attend_kernel,
        grid_spec=pltpu.PrefetchScalarGridSpec(
            num_scalar_prefetch=1,
            grid=(per, groups),
            in_specs=[spec(0), spec(1), spec(2)],
            out_specs=[spec(0), pl.BlockSpec((None, None, GROUP, seq), lambda s, h, *_: (s, h, 0, 0))],
        ),
        out_shape=[
            jax.ShapeDtypeStruct((per, seq, groups * lanes), BF),
            jax.ShapeDtypeStruct((per, groups, GROUP, seq), F32),
        ],
        compiler_params=pltpu.CompilerParams(vmem_limit_bytes=60 * MIB),
        cost_estimate=cost("attend"),
        name="attend",
    )(meta, shaped, shaped, shaped)
    return mixed.reshape(per * seq, -1), lse


def attend_back(meta, proj, grad, mixed, lse, per, seq, first, count):
    width = proj.shape[-1] // 3
    lanes = GROUP * HD
    groups = width // lanes
    shaped = proj.reshape(per, seq, proj.shape[-1])

    def spec(c):
        return pl.BlockSpec((None, seq, lanes), lambda s, h, *_: (s, 0, c * groups + first + h))

    out, sums = pl.pallas_call(
        attend_back_kernel,
        grid_spec=pltpu.PrefetchScalarGridSpec(
            num_scalar_prefetch=1,
            grid=(per, count),
            in_specs=[spec(0), spec(1), spec(2), spec(0), spec(0)]
            + [pl.BlockSpec((None, None, GROUP, seq), lambda s, h, *_: (s, first + h, 0, 0))],
            out_specs=[
                pl.BlockSpec((3, None, seq, lanes), lambda s, h, *_: (0, s, 0, h)),
                pl.BlockSpec((3, None, 8, lanes), lambda s, h, *_: (0, s, 0, h)),
            ],
        ),
        out_shape=[
            jax.ShapeDtypeStruct((3, per, seq, count * lanes), BF),
            jax.ShapeDtypeStruct((3, per, 8, count * lanes), F32),
        ],
        compiler_params=pltpu.CompilerParams(vmem_limit_bytes=60 * MIB),
        cost_estimate=cost("attend_back"),
        name="attend_back",
    )(meta, shaped, shaped, shaped, grad.reshape(per, seq, width), mixed.reshape(per, seq, width), lse)
    return out.reshape(3, per * seq, count * lanes), sums


def weight_grad(name, meta, odd, lefts, rights, chunk, come=None, extra=None):
    rows = lefts[0].shape[0]
    tall = lefts[0].shape[1] // 8
    plan = []
    for li, group in enumerate(rights):
        for right in group:
            for c in range((right.shape[0] if right.ndim == 3 else 1) * (right.shape[-1] // chunk)):
                plan.append((li, right, c))
    steps = len(plan)
    flat = [r for group in rights for r in group]
    firsts, pos = [], 0
    for right in flat:
        firsts.append(pos)
        pos += (right.shape[0] if right.ndim == 3 else 1) * (right.shape[-1] // chunk)
    owners = [li for li, group in enumerate(rights) for _ in group]
    below = 0 if extra is None else extra.shape[1]
    cut = (steps + 1) // 2
    n_left = len(lefts)

    def kernel(meta_ref, *refs):
        left_refs = refs[: 4 * n_left]
        pos = 4 * n_left
        right_refs = refs[pos : pos + len(flat)]
        pos += len(flat)
        extra_refs = refs[pos : pos + 4] if below else ()
        pos += len(extra_refs)
        come_ref = refs[pos] if come is not None else None
        pos += come is not None
        outs = refs[pos:]
        c = pl.program_id(0)

        def store(lefts_here, right):
            for k in range(4):
                part = tn(lefts_here[k][...], right)
                if come is None:
                    outs[0][k, 0:tall, :] = part.astype(BF)
                    if below:
                        outs[0][k, tall:, :] = extra_refs[k][...]
                    continue
                part = (part + come_ref[k, 0:tall, :].astype(F32)).astype(BF)
                if below:
                    low = (extra_refs[k][...].astype(F32) + come_ref[k, tall:, :].astype(F32)).astype(BF)
                if k < 3:
                    outs[k][0:tall, :] = part
                    if below:
                        outs[k][tall:, :] = low
                    continue

                @pl.when(c < cut)
                def _():
                    outs[3][0:tall, :] = part
                    if below:
                        outs[3][tall:, :] = low

                @pl.when(c >= cut)
                def _():
                    outs[4][0:tall, :] = part
                    if below:
                        outs[4][tall:, :] = low

        for i, right_ref in enumerate(right_refs):
            last = firsts[i + 1] if i + 1 < len(flat) else steps
            li = owners[i]

            @pl.when((c >= firsts[i]) & (c < last))
            def _(right_ref=right_ref, li=li):
                store(left_refs[4 * li : 4 * li + 4], right_ref[...])

    def left_spec(k):
        return pl.BlockSpec((rows, tall), lambda c, m: (0, m[0] ^ (2 * k + odd)))

    def right_spec(i, right):
        last = (firsts[i + 1] if i + 1 < len(flat) else steps) - 1
        inner = right.shape[-1] // chunk

        def place(c):
            return jnp.clip(c, firsts[i], last) - firsts[i]

        if right.ndim == 3:
            return pl.BlockSpec((None, rows, chunk), lambda c, m: (place(c) // inner, 0, place(c) % inner))
        return pl.BlockSpec((rows, chunk), lambda c, m: (0, place(c)))

    def extra_spec(k):
        return pl.BlockSpec((None, below, chunk), lambda c, m: (m[0] ^ (2 * k + odd), 0, c))

    high = tall + below
    four = pl.BlockSpec((4, high, chunk), lambda c, m: (0, 0, c))
    in_specs = [left_spec(k) for _ in lefts for k in range(4)] + [right_spec(i, r) for i, r in enumerate(flat)]
    args = [left for left in lefts for _ in range(4)] + flat
    if below:
        in_specs += [extra_spec(k) for k in range(4)]
        args += [extra] * 4
    if come is None:
        out_specs = [four]
        out_shape = [jax.ShapeDtypeStruct((4, high, steps * chunk), BF)]
    else:
        in_specs.append(four)
        args.append(come)
        out_specs = [pl.BlockSpec((high, chunk), lambda c, m: (0, c))] * 3 + [
            pl.BlockSpec((high, chunk), lambda c, m: (0, jnp.minimum(c, cut - 1))),
            pl.BlockSpec((high, chunk), lambda c, m: (0, jnp.maximum(c - cut, 0))),
        ]
        out_shape = [jax.ShapeDtypeStruct((high, steps * chunk), BF)] * 3 + [
            jax.ShapeDtypeStruct((high, cut * chunk), BF),
            jax.ShapeDtypeStruct((high, (steps - cut) * chunk), BF),
        ]
    return pl.pallas_call(
        kernel,
        grid_spec=pltpu.PrefetchScalarGridSpec(
            num_scalar_prefetch=1,
            grid=(steps,),
            in_specs=in_specs,
            out_specs=out_specs,
        ),
        out_shape=out_shape,
        compiler_params=pltpu.CompilerParams(vmem_limit_bytes=60 * MIB),
        cost_estimate=cost(name),
        name=name,
    )(meta, *args)


def shards(
    tokens, lengths, w_qkv, bias_qv, w_out, bias_out, gain_one, shift_one,
    w_up, bias_up, w_down, bias_down, gain_two, shift_two, cotangent,
):
    seqs, blk, width = tokens.shape
    n = lax.axis_size("ctx")
    ndp = lax.axis_size("dp")
    me = lax.axis_index("dp")
    place = lax.axis_index("ctx")
    per = seqs // n
    rows = seqs * blk
    tile = per * blk
    ff = w_up.shape[1]
    thin = w_qkv.shape[0]
    tuned = ndp == 8
    half = width // (GROUP * HD) // 2

    own = lax.dynamic_slice_in_dim(lengths, place * per, per)
    meta = jnp.concatenate([jnp.stack([me, place]).astype(jnp.int32), own])

    vectors = (bias_qv, bias_out, gain_one, shift_one, bias_up, bias_down, gain_two, shift_two)
    sizes = [v.shape[0] for v in vectors]
    count = sum(sizes)
    line = jnp.pad(jnp.concatenate(vectors).reshape(1, count), ((0, 15), (0, 3 * width - count)))
    qkv_own = jnp.concatenate([w_qkv, line])
    mid_own = jnp.concatenate([w_out, w_up], axis=1)
    shared = tokens.reshape(n, per, blk, width)
    x = jnp.swapaxes(to_sequences(shared), 0, 1).reshape(rows, width)
    qkv_near = gather_near(qkv_own)
    mid_near = gather_near(mid_own)
    x, qkv_near, mid_near, cotangent = sync(x, qkv_near, mid_near, cotangent)
    qkv_far = gather_far(qkv_near)
    qkv_mine = gather_stack(qkv_own, qkv_near, qkv_far)
    qkv_other = swap(qkv_mine, "dp", 1)
    mid_far = gather_far(mid_near)
    cot_1 = trade(part_of(cotangent, 1), 1)

    both = jnp.concatenate([qkv_mine[:, thin, :count], qkv_other[:, thin, :count]])
    index = jnp.arange(ndp, dtype=jnp.int32) ^ me
    packed = jnp.take(both, (index >> 1) + (index & 1) * (ndp // 2), axis=0).astype(F32)
    fulls, pos = [], 0
    for size in sizes:
        fulls.append(packed[:, pos : pos + size].reshape(1, ndp * size))
        pos += size
    bqv, bout, gone, sone, bup, bdown, gtwo, stwo = fulls
    bqkv = jnp.concatenate([bqv[:, :width], jnp.zeros((1, width), F32), bqv[:, width:]], axis=1)

    qkv_w = (qkv_mine, qkv_other, thin, 0, 3 * width, 3)
    (proj,) = dense(qkv_body, "qkv", meta, rows, tile, [x], [bqkv], [qkv_w], [(3 * width, BF)], [])
    proj, mid_far, cot_1, w_down, cotangent = sync(proj, mid_far, cot_1, w_down, cotangent)
    mid_mine = gather_stack(mid_own, mid_near, mid_far)
    mid_other = swap(mid_mine, "dp", 1)
    down_near = gather_near(w_down)
    cot_2 = trade(part_of(cotangent, 2), 2)
    mixed, lse = attend(meta, proj, per, n * blk)
    mixed, mid_other, down_near, cot_2 = sync(mixed, mid_other, down_near, cot_2)
    out_w = (mid_mine, mid_other, thin, 0, width, 2)
    up_w = (mid_mine, mid_other, thin, width, ff, 8)
    down_far = gather_far(down_near)
    normed_one, inverse_one, first_low = dense(
        out_body, "out", meta, rows, tile, [mixed, x], [bout, gone, sone], [out_w], [(width, F32), (128, F32), (width, BF)], []
    )
    first_low, down_far, cotangent = sync(first_low, down_far, cotangent)
    down_mine = gather_stack(w_down, down_near, down_far)
    down_other = swap(down_mine, "dp", 1)
    cot_3 = trade(part_of(cotangent, 3), 3)
    active, deriv = dense(up_body, "up", meta, rows, tile, [first_low], [bup], [up_w], [(ff, BF), (ff, BF)], [])
    active, down_other, cot_3 = sync(active, down_other, cot_3)
    down_w = (down_mine, down_other, w_down.shape[0], 0, width, 0 if w_down.shape[0] % 128 == 0 else 1)
    cot = put_positions([part_of(cotangent, 0), cot_1, cot_2, cot_3]).reshape(rows, width)
    out_parts, sum_two, second, s_gtwo, s_stwo, s_bdown = dense(
        functools.partial(down_body, n * blk, per), "down", meta, rows, tile, [active, normed_one, cot],
        [bdown, gone, sone, gtwo, stwo], [down_w], [(width, BF), (width, F32), (width, BF)], [width] * 3,
    )
    out_parts = out_parts.reshape(per, n * blk, width)
    out_own = part_of(out_parts, 0, 1)
    out_1 = trade(part_of(out_parts, 1, 1), 1)
    cut = (per + 1) // 2

    come = ()
    if tuned:
        (away,) = weight_grad("gd_away", meta, 1, [active], [[second]], 512)
        come = swap(away, "dp", 1)
        second = after(second, away)
    hidden, s_bup = dense(hidden_body, "hidden", meta, rows, tile, [second, deriv], [], [down_w], [(ff, BF)], [ff])
    hidden, come, out_1, out_parts = sync(hidden, come, out_1, out_parts)
    part = part_of(out_parts, 2, 1)
    out_2 = trade(part[:cut], 2)
    d_far, d_near = (), ()
    if tuned:
        d_sums = weight_grad("gd_keep", meta, 0, [active], [[second]], 512, come=come)
        d_far = send_far(d_sums)
        hidden, out_2, part = sync(after(hidden, d_sums[0]), out_2, part)
    out_2b = trade(part[cut:], 2)
    if tuned:
        (away,) = weight_grad("gu_away", meta, 1, [first_low], [[hidden]], 1024)
        hidden = after(hidden, away)
        away, d_far, out_2b = sync(away, d_far, out_2b)
        come = swap(away, "dp", 1)
    hidden, d_far, out_2b, out_parts = sync(hidden, d_far, out_2b, out_parts)
    if tuned:
        d_near = send_near(d_sums, d_far)
    out_3 = trade(part_of(out_parts, 3, 1), 3)
    sum_one, branch, g_mixed, s_gone, s_sone, s_bout = dense(
        first_body, "first", meta, rows, tile, [hidden, sum_two, normed_one, inverse_one], [gone], [up_w[:5] + (4,), out_w[:5] + (1,)],
        [(width, F32), (width, BF), (width, BF)], [width] * 3,
    )
    branch, g_mixed, come, d_near, out_3 = sync(branch, g_mixed, come, d_near, out_3)
    output = put_slots([(0, 0, out_own), (1, 0, out_1), (2, 0, out_2), (2, cut, out_2b), (3, 0, out_3)], per, BF)
    u_far = ()
    if tuned:
        d_share = add_low(d_sums[0], *d_near)
        g_down = lax.psum(d_share, "ctx")
        u_sums = weight_grad("gu_keep", meta, 0, [first_low], [[hidden]], 1024, come=come)
        u_far = send_far(u_sums)
        g_mixed = after(g_mixed, u_sums[0])
    p_one, s_one = attend_back(meta, proj, g_mixed, mixed, lse, per, n * blk, 0, half)
    p_one, g_mixed, u_far = sync(p_one, g_mixed, u_far)
    u_near = ()
    if tuned:
        u_near = send_near(u_sums, u_far)
    p_two, s_two = attend_back(meta, proj, g_mixed, mixed, lse, per, n * blk, half, half)
    if tuned:
        p_two, u_near, g_down = sync(p_two, u_near, g_down)

    s_proj = jnp.concatenate([jnp.sum(s_one, axis=(1, 2)), jnp.sum(s_two, axis=(1, 2))], axis=1)
    vec = [jnp.concatenate([s_proj[0], s_proj[2]])] + [
        jnp.sum(s, axis=0) for s in (s_bout, s_gone, s_sone, s_bup, s_bdown, s_gtwo, s_stwo)
    ]
    vec = jnp.concatenate([v.reshape(ndp, -1) for v in vec], axis=1)

    come = ()
    if tuned:
        u_keep, u_away = halves_ctx(add_low(u_sums[0], *u_near), 1)
        u_come = swap(u_away, "ctx", 1)
        extra = jnp.pad(vec[:, None, :].astype(BF), ((0, 0), (0, 15), (0, 4 * width - count)))
        products = ([x, mixed], [[p_one, p_two], [branch]])
        (away,) = weight_grad("gb_away", meta, 1, *products, 512, extra=extra)
        sum_one = after(sum_one, away)
        away, u_come = sync(away, u_come)
        come = swap(away, "dp", 1)
        u_keep, u_away = halves_ctx(add_low(u_keep, u_come), 2)
        u_come = swap(u_away, "ctx", 2)
    else:
        u_come = ()
    (grad_in,) = dense(input_body, "input", meta, rows, tile, [p_one, p_two, sum_one], [], [qkv_w[:5] + (6,)], [(width, BF)], [])
    grad_in, come, u_come = sync(grad_in, come, u_come)
    grad_in = grad_in.reshape(per, n * blk, width)
    in_1 = trade(part_of(grad_in, 1, 1), 1)
    if tuned:
        u_half = add_low(u_keep, u_come)
        u_other = swap(u_half, "ctx", 2)
        b_sums = weight_grad("gb_keep", meta, 0, *products, 512, come=come, extra=extra)
        b_sums, u_other, in_1, grad_in = sync(b_sums, u_other, in_1, grad_in)
    part_2, part_3 = part_of(grad_in, 2, 1), part_of(grad_in, 3, 1)
    in_2 = trade(part_2[:cut], 2)
    if tuned:
        b_far = send_far(b_sums)
        u_whole = join_ctx(u_half, u_other, 2)
        u_other = swap(u_whole, "ctx", 1)
        b_far, in_2, u_other, part_2, part_3 = sync(b_far, in_2, u_other, part_2, part_3)
        b_near = send_near(b_sums, b_far)
    in_2b, in_3 = trade(part_2[cut:], 2), trade(part_3[:cut], 3)
    if tuned:
        b_near, in_2b, in_3, part_3 = sync(b_near, in_2b, in_3, part_3)
        b_keep, b_away = halves_ctx(add_low(b_sums[0], *b_near), 1)
        b_come = swap(b_away, "ctx", 1)
    in_3b = trade(part_3[cut:], 3)
    in_rest = [(2, 0, in_2), (2, cut, in_2b), (3, 0, in_3), (3, cut, in_3b)]
    if tuned:
        b_come, in_3b = sync(b_come, in_3b)
        b_half = add_low(b_keep, b_come)
        g_up = join_ctx(u_whole, u_other, 1)
        total = whole_ctx(whole_ctx(halve_ctx(b_half, 2), 2), 1).astype(F32)
        part = width // 2
        g_qkv = jnp.concatenate(
            [total[:thin, (p * 3 + c) * part : (p * 3 + c + 1) * part] for c in range(3) for p in range(2)], axis=1
        )
        g_out = total[:thin, 3 * width :]
        g_up = g_up.astype(F32)
        g_down = g_down.astype(F32)
        vec = total[thin, :count]
    else:
        def whole(*products):
            return jnp.concatenate([tn(a, b).astype(BF) for a, b in products], axis=1)

        def total(grad):
            return lax.psum(reduce_any(grad).astype(F32), "ctx")

        g_down = total(whole((active, second)))
        g_up = total(whole((first_low, hidden)))
        g_out = total(whole((mixed, branch)))
        g_qkv = total(whole(*[(x, p[c]) for c in range(3) for p in (p_one, p_two)]))
        vec = lax.psum(lax.psum_scatter(vec, "dp", scatter_dimension=0, tiled=True), "ctx").reshape(-1)
    grads, pos = [], 0
    for size in sizes:
        grads.append(vec[pos : pos + size])
        pos += size
    g_bqv, g_bout, g_gone, g_sone, g_bup, g_bdown, g_gtwo, g_stwo = grads
    grad_input = put_slots([(0, 0, part_of(grad_in, 0, 1)), (1, 0, in_1)] + in_rest, per, F32)
    return (
        output, grad_input, g_qkv, g_bqv, g_out, g_bout, g_gone, g_sone, g_up, g_bup, g_down, g_bdown, g_gtwo, g_stwo,
    )


def solution(mesh):
    row = P("dp", "ctx", None)
    mat = P("dp", None)
    vec = P("dp")
    weights = (mat, vec, mat, vec, vec, vec, mat, vec, mat, vec, vec, vec)
    return jax.shard_map(
        shards, mesh=mesh, in_specs=(row, vec) + weights + (row,), out_specs=(row, row) + weights, check_vma=False
    )
```

```python
import functools

import jax
import jax.numpy as jnp
from jax import lax
from jax.experimental import pallas as pl
from jax.experimental.pallas import tpu as pltpu
from jax.sharding import PartitionSpec as P

HD = 64
GROUP = 4
NEG = -1e30
EPS = 1e-06
BF = jnp.bfloat16
F32 = jnp.float32
MIB = 1024 * 1024
COSTS = {'qkv': 13, 'out': 10, 'up': 23, 'down': 21, 'hidden': 18, 'first': 23, 'input': 14, 'attend': 24, 'attend_back': 21, 'gd_away': 11, 'gd_keep': 11, 'gu_away': 11, 'gu_keep': 11, 'gb_away': 14, 'gb_keep': 3, 'gc_away': 8, 'gc_keep': 8}


def cost(name):
    return pl.CostEstimate(flops=COSTS[name] * 1000000000, bytes_accessed=1000000, transcendentals=0)


ANY = pl.BlockSpec(memory_space=pl.ANY)


def swap(x, axis, bit):
    n = lax.axis_size(axis)
    return lax.ppermute(x, axis, [(i, i ^ bit) for i in range(n)])


def after(x, *others):
    return lax.optimization_barrier((x,) + others)[0]


def sync(*values):
    return lax.optimization_barrier(values)


def gather_near(own):
    if lax.axis_size("dp") != 8:
        return ()
    return swap(own, "dp", 2), swap(own, "dp", 4)


def gather_far(near):
    if not near:
        return ()
    half = near[0].shape[1] // 2
    return swap(near[0][:, :half], "dp", 4), swap(near[1][:, half:], "dp", 2)


def gather_stack(own, near, far):
    if near:
        return jnp.stack([own, near[0], near[1], jnp.concatenate(far, axis=1)])
    mine = own[None]
    bit = 2
    while bit < lax.axis_size("dp"):
        mine = jnp.concatenate([mine, swap(mine, "dp", bit)])
        bit *= 2
    return mine


def add_low(*parts):
    total = parts[0].astype(F32)
    for part in parts[1:]:
        total = total + part.astype(F32)
    return total.astype(BF)


def reduce_any(grad):
    n = lax.axis_size("dp")
    me = lax.axis_index("dp")
    rows = grad.shape[0] // n
    width = grad.shape[1]

    def stack(odd):
        return jnp.stack(
            [lax.dynamic_slice(grad, ((me ^ (2 * k + odd)) * rows, 0), (rows, width)) for k in range(n // 2)]
        )

    mine = add_low(stack(0), swap(stack(1), "dp", 1))
    bit = n // 2
    while bit > 1:
        keep = mine.shape[0] // 2
        mine = add_low(mine[:keep], swap(mine[keep:], "dp", bit))
        bit //= 2
    return mine[0]


def send_far(sums):
    return swap(sums[3], "dp", 4), swap(sums[4], "dp", 2)


def send_near(sums, far):
    own, to_x, to_y = sums[:3]
    cut, width = far[0].shape[1], to_x.shape[1]
    to_x = add_low(to_x, jnp.pad(far[0], ((0, 0), (0, width - cut))))
    to_y = add_low(to_y, jnp.pad(far[1], ((0, 0), (cut, 0))))
    return swap(to_x, "dp", 2), swap(to_y, "dp", 4)


def halves_ctx(share, bit):
    half = share.shape[1] // 2
    mine = (lax.axis_index("ctx") // bit) % 2
    keep = lax.dynamic_slice_in_dim(share, mine * half, half, axis=1)
    return keep, lax.dynamic_slice_in_dim(share, (1 - mine) * half, half, axis=1)


def halve_ctx(share, bit):
    keep, away = halves_ctx(share, bit)
    return add_low(keep, swap(away, "ctx", bit))


def join_ctx(half, other, bit):
    low = (lax.axis_index("ctx") // bit) % 2 == 0
    return jnp.concatenate([jnp.where(low, half, other), jnp.where(low, other, half)], axis=1)


def whole_ctx(half, bit):
    return join_ctx(half, swap(half, "ctx", bit), bit)


def to_sequences(block):
    return lax.all_to_all(block, "ctx", 0, 0, tiled=True)


def part_of(block, j, axis=0):
    n = lax.axis_size("ctx")
    per = block.shape[axis] // n
    return lax.dynamic_slice_in_dim(block, (lax.axis_index("ctx") ^ j) * per, per, axis=axis)


def put_slots(pieces, per, dtype):
    n = lax.axis_size("ctx")
    out = jnp.zeros((n * per,) + pieces[0][2].shape[1:], dtype)
    for j, first, piece in pieces:
        start = (lax.axis_index("ctx") ^ j) * per + first
        out = lax.dynamic_update_slice_in_dim(out, piece.astype(dtype), start, axis=0)
    return out


def put_positions(pieces):
    n = len(pieces)
    per, blk, width = pieces[0].shape
    out = jnp.zeros((per, n * blk, width), pieces[0].dtype)
    for j in range(n):
        out = lax.dynamic_update_slice_in_dim(out, pieces[j], (lax.axis_index("ctx") ^ j) * blk, axis=1)
    return out


def trade(block, j):
    return swap(block, "ctx", j)


def nn(left, right):
    return jnp.dot(left, right, preferred_element_type=F32)


def nt(left, right):
    return lax.dot_general(left, right, (((1,), (1,)), ((), ())), preferred_element_type=F32)


def tn(left, right):
    return lax.dot_general(left, right, (((0,), (0,)), ((), ())), preferred_element_type=F32)


def fold(rows):
    return jnp.sum(rows.reshape(rows.shape[0] // 8, 8, rows.shape[1]), axis=0)


class Weight:
    def __init__(self, stacks, whole, sems, me, rows, first, pieces):
        self.whole, self.pieces = whole, pieces
        self.step = whole.shape[1] // max(pieces, 1)
        self.copies, self.starts = [], []
        for odd, stack in enumerate(stacks):
            count = stack.shape[0]
            for k in range(count):
                start = pl.multiple_of((me ^ (2 * k + odd)) * rows if len(stacks) == 2 else k * rows, rows)
                self.starts.append(pl.ds(start, rows))
                for p in range(max(pieces, 1)):
                    here, there = pl.ds(first + p * self.step, self.step), pl.ds(p * self.step, self.step)
                    copy = pltpu.make_async_copy(
                        stack.at[k, pl.ds(0, rows), here], whole.at[self.starts[-1], there], sems.at[odd * count + k, p]
                    )
                    self.copies.append((k * 2 + odd, p, copy))
        self.wait_for = False

    def start(self):
        for _, _, copy in sorted(self.copies, key=lambda c: c[1] if self.pieces else c[0]):
            copy.start()

    def cols(self, p):
        if self.wait_for:
            for _, q, copy in self.copies:
                if q == p:
                    copy.wait()
        return slice(p * self.step, (p + 1) * self.step)

    def rows(self, c):
        _, _, copy = self.copies[c]
        if self.wait_for:
            copy.wait()
        return self.starts[c]


def row_spec(tile, width):
    return pl.BlockSpec((tile, width), lambda i, *_: (i, 0))


def one_spec(height, width):
    return pl.BlockSpec((height, width), lambda i, *_: (0, 0))


def dense(body, name, meta, rows, tile, row_ins, vec_ins, weights, row_outs, sums):
    stacks, spans, scratch = [], [], []
    for mine, other, r, _, width, pieces in weights:
        held = [mine] if other is None else [mine, other]
        spans.append(slice(len(stacks), len(stacks) + len(held)))
        stacks += held
        count = mine.shape[0] * len(held)
        scratch.append(pltpu.VMEM((count * r, width), BF))
        scratch.append(pltpu.SemaphoreType.DMA((count, max(pieces, 1))))
    n_row, n_vec, n_stack = len(row_ins), len(vec_ins), len(stacks)
    n_out, n_sum = len(row_outs), len(sums)

    def kernel(meta_ref, *refs):
        pos = 0
        groups = []
        for count in (n_row, n_vec, n_stack, n_out, n_sum, 2 * len(weights)):
            groups.append(refs[pos : pos + count])
            pos += count
        row_refs, vec_refs, stack_refs, out_refs, sum_refs, scratch_refs = groups

        whole = [
            Weight(stack_refs[spans[w]], scratch_refs[2 * w], scratch_refs[2 * w + 1], meta_ref[0], weights[w][2], weights[w][3], weights[w][5])
            for w in range(len(weights))
        ]

        def work(wait_for):
            for weight in whole:
                weight.wait_for = wait_for
            body(meta_ref, row_refs, vec_refs, whole, out_refs, sum_refs)

        @pl.when(pl.program_id(0) == 0)
        def _():
            for weight in whole:
                weight.start()
            for ref in sum_refs:
                ref[...] = jnp.zeros_like(ref)
            work(True)

        @pl.when(pl.program_id(0) > 0)
        def _():
            work(False)

    in_specs = (
        [row_spec(tile, a.shape[-1]) if a.ndim == 2 else pl.BlockSpec((a.shape[0], tile, a.shape[2]), lambda i, *_: (0, i, 0)) for a in row_ins]
        + [one_spec(1, v.shape[1]) for v in vec_ins]
        + [ANY] * n_stack
    )
    out_specs = [row_spec(tile, w) for w, _ in row_outs] + [one_spec(8, w) for w in sums]
    out_shape = [jax.ShapeDtypeStruct((rows, w), d) for w, d in row_outs] + [
        jax.ShapeDtypeStruct((8, w), F32) for w in sums
    ]
    return pl.pallas_call(
        kernel,
        grid_spec=pltpu.PrefetchScalarGridSpec(
            num_scalar_prefetch=1,
            grid=(rows // tile,),
            in_specs=in_specs,
            out_specs=out_specs,
            scratch_shapes=scratch,
        ),
        out_shape=out_shape,
        compiler_params=pltpu.CompilerParams(vmem_limit_bytes=60 * MIB, dimension_semantics=("arbitrary",)),
        cost_estimate=cost(name),
        name=name,
    )(meta, *row_ins, *vec_ins, *stacks)


def by_columns(left, weight):
    parts = []
    for p in range(weight.pieces):
        cols = weight.cols(p)
        parts.append(nn(left[...], weight.whole[:, cols]))
    return jnp.concatenate(parts, axis=1)


def by_columns_turned(left, weight):
    total = None
    for p in range(weight.pieces):
        cols = weight.cols(p)
        part = nt(left[:, cols], weight.whole[:, cols])
        total = part if total is None else total + part
    return total


def by_shards(left, weight):
    if weight.pieces:
        return by_columns(left, weight)
    if not weight.wait_for:
        return nn(left[...], weight.whole[...])
    total = None
    for c in range(len(weight.copies)):
        here = weight.rows(c)
        part = nn(left[:, here], weight.whole[here, :])
        total = part if total is None else total + part
    return total


def qkv_body(meta, rows, vecs, whole, outs, sums):
    (x,) = rows
    (bias,) = vecs
    for p in range(whole[0].pieces):
        cols = whole[0].cols(p)
        outs[0][:, cols] = (nn(x[...], whole[0].whole[:, cols]) + bias[:, cols]).astype(BF)


def out_body(meta, rows, vecs, whole, outs, sums):
    mixed, x = rows
    bias, gain, shift = vecs
    total = x[...].astype(F32) + (by_columns(mixed, whole[0]) + bias[...])
    centre = total - jnp.mean(total, axis=-1, keepdims=True)
    inverse = lax.rsqrt(jnp.mean(centre * centre, axis=-1, keepdims=True) + EPS)
    normed = centre * inverse
    outs[0][...] = normed
    outs[1][...] = jnp.broadcast_to(inverse, outs[1].shape)
    outs[2][...] = (normed * gain[...] + shift[...]).astype(BF)


def up_body(meta, rows, vecs, whole, outs, sums):
    (low,) = rows
    (bias,) = vecs
    for p in range(whole[0].pieces):
        cols = whole[0].cols(p)
        hidden = nn(low[...], whole[0].whole[:, cols]) + bias[:, cols]
        cdf = 0.5 + 0.5 * lax.erf(hidden * 0.7071067811865476)
        pdf = jnp.exp(-0.5 * hidden * hidden) * 0.3989422804014327
        outs[0][:, cols] = (hidden * cdf).astype(BF)
        outs[1][:, cols] = (cdf + hidden * pdf).astype(BF)


def down_body(seq, per, meta, rows, vecs, whole, outs, sums):
    active, normed_one, cot = rows
    bias, gain_one, shift_one, gain, shift = vecs
    total = (normed_one[...] * gain_one[...] + shift_one[...]) + (by_shards(active, whole[0]) + bias[...])
    centre = total - jnp.mean(total, axis=-1, keepdims=True)
    inverse = lax.rsqrt(jnp.mean(centre * centre, axis=-1, keepdims=True) + EPS)
    normed = centre * inverse
    tile = total.shape[0]
    at = lax.broadcasted_iota(jnp.int32, (tile, 1), 0) + pl.program_id(0) * tile
    valid = jnp.zeros(at.shape, jnp.bool_)
    for s in range(per):
        valid = valid | ((at >= s * seq) & (at < s * seq + meta[2 + s]))
    keep = jnp.where(valid, 1.0, 0.0)
    outs[0][...] = ((normed * gain[...] + shift[...]) * keep).astype(BF)
    grad = cot[...].astype(F32) * keep
    sums[0][...] += fold(grad * normed)
    sums[1][...] += fold(grad)
    scaled = grad * gain[...]
    back = inverse * (
        scaled
        - jnp.mean(scaled, axis=-1, keepdims=True)
        - normed * jnp.mean(scaled * normed, axis=-1, keepdims=True)
    )
    low = back.astype(BF)
    outs[1][...] = back
    outs[2][...] = low
    sums[2][...] += fold(low.astype(F32))


def hidden_body(meta, rows, vecs, whole, outs, sums):
    second, deriv = rows
    if whole[0].pieces:
        whole[0].cols(0)
        places = [slice(c, c + 512) for c in range(0, deriv.shape[1], 512)]
    else:
        places = range(len(whole[0].copies))
    for cols in places:
        if not whole[0].pieces:
            cols = whole[0].rows(cols)
        low = (nt(second[...], whole[0].whole[cols, :]) * deriv[:, cols].astype(F32)).astype(BF)
        outs[0][:, cols] = low
        sums[0][:, cols] += fold(low.astype(F32))


def first_body(meta, rows, vecs, whole, outs, sums):
    hidden, sum_two, normed, inverse = rows
    (gain,) = vecs
    grad = sum_two[...] + by_columns_turned(hidden, whole[0])
    n1 = normed[...]
    sums[0][...] += fold(grad * n1)
    sums[1][...] += fold(grad)
    scaled = grad * gain[...]
    back = inverse[:, 0:1] * (
        scaled - jnp.mean(scaled, axis=-1, keepdims=True) - n1 * jnp.mean(scaled * n1, axis=-1, keepdims=True)
    )
    low = back.astype(BF)
    outs[0][...] = back
    outs[1][...] = low
    sums[2][...] += fold(low.astype(F32))
    whole[1].cols(0)
    outs[2][...] = nt(low, whole[1].whole[...]).astype(BF)


def input_body(meta, rows, vecs, whole, outs, sums):
    sum_one = rows[-1]
    total = sum_one[...]
    parts = len(rows) - 1
    for p in range(whole[0].pieces):
        cols = whole[0].cols(p)
        total = total + nt(rows[p % parts][p // parts], whole[0].whole[:, cols])
    outs[0][...] = total.astype(BF)


def key_mask(meta, seq):
    at = lax.broadcasted_iota(jnp.int32, (seq, 1), 0)
    return at < meta[2 + pl.program_id(0)]


def attend_kernel(meta, q_ref, k_ref, v_ref, mixed_ref, lse_ref):
    seq, lanes = q_ref.shape
    ok = key_mask(meta, seq)
    q_all = q_ref[...] * BF(HD ** (-0.5))
    k_all, v_turned = k_ref[...], v_ref[...].T
    ones = jnp.ones((16, seq), BF)
    outs = []
    for h in range(lanes // HD):
        cols = slice(h * HD, (h + 1) * HD)
        scores = jnp.where(ok, nt(k_all[:, cols], q_all[:, cols]), NEG)
        peak = jnp.max(scores, axis=0, keepdims=True)
        weights = jnp.exp(scores - peak).astype(BF)
        both = nn(jnp.concatenate([v_turned[cols], ones], axis=0), weights)
        total = both[HD : HD + 1]
        lse_ref[h : h + 1, :] = peak + jnp.log(total)
        outs.append(both[:HD] * (1.0 / total))
    mixed_ref[...] = jnp.concatenate(outs, axis=0).T.astype(BF)


def attend_back_kernel(meta, q_ref, k_ref, v_ref, g_ref, mixed_ref, lse_ref, proj_ref, sum_ref):
    seq, lanes = q_ref.shape
    ok = key_mask(meta, seq)
    scale = HD ** (-0.5)
    q_all = q_ref[...] * BF(scale)
    k_all, v_all, g_all = k_ref[...], v_ref[...], g_ref[...]
    k_turned = k_all.T
    inners = (g_all.astype(F32) * mixed_ref[...].astype(F32)).T
    gq, gk, gv = [], [], []
    for h in range(lanes // HD):
        cols = slice(h * HD, (h + 1) * HD)
        q, k, v, g = q_all[:, cols], k_all[:, cols], v_all[:, cols], g_all[:, cols]
        exact = jnp.exp(jnp.where(ok, nt(k, q), NEG) - lse_ref[h : h + 1, :])
        inner = jnp.sum(inners[cols], axis=0, keepdims=True)
        low = (exact * (nt(v, g) - inner)).astype(BF)
        gq.append(nn(k_turned[cols], low) * scale)
        gk.append(nn(low, q))
        gv.append(nn(exact.astype(BF), g))
    wholes = (jnp.concatenate(gq, axis=0).T, jnp.concatenate(gk, axis=1), jnp.concatenate(gv, axis=1))
    for c, whole in enumerate(wholes):
        low = whole.astype(BF)
        proj_ref[c] = low
        sum_ref[c] = fold(low.astype(F32))


def attend(meta, proj, per, seq):
    lanes = GROUP * HD
    groups = proj.shape[-1] // 3 // lanes
    shaped = proj.reshape(per, seq, proj.shape[-1])

    def spec(c):
        return pl.BlockSpec((None, seq, lanes), lambda s, h, *_: (s, 0, c * groups + h))

    mixed, lse = pl.pallas_call(
        attend_kernel,
        grid_spec=pltpu.PrefetchScalarGridSpec(
            num_scalar_prefetch=1,
            grid=(per, groups),
            in_specs=[spec(0), spec(1), spec(2)],
            out_specs=[spec(0), pl.BlockSpec((None, None, GROUP, seq), lambda s, h, *_: (s, h, 0, 0))],
        ),
        out_shape=[
            jax.ShapeDtypeStruct((per, seq, groups * lanes), BF),
            jax.ShapeDtypeStruct((per, groups, GROUP, seq), F32),
        ],
        compiler_params=pltpu.CompilerParams(vmem_limit_bytes=60 * MIB),
        cost_estimate=cost("attend"),
        name="attend",
    )(meta, shaped, shaped, shaped)
    return mixed.reshape(per * seq, -1), lse


def attend_back(meta, proj, grad, mixed, lse, per, seq, first, count):
    width = proj.shape[-1] // 3
    lanes = GROUP * HD
    groups = width // lanes
    shaped = proj.reshape(per, seq, proj.shape[-1])

    def spec(c):
        return pl.BlockSpec((None, seq, lanes), lambda s, h, *_: (s, 0, c * groups + first + h))

    out, sums = pl.pallas_call(
        attend_back_kernel,
        grid_spec=pltpu.PrefetchScalarGridSpec(
            num_scalar_prefetch=1,
            grid=(per, count),
            in_specs=[spec(0), spec(1), spec(2), spec(0), spec(0)]
            + [pl.BlockSpec((None, None, GROUP, seq), lambda s, h, *_: (s, first + h, 0, 0))],
            out_specs=[
                pl.BlockSpec((3, None, seq, lanes), lambda s, h, *_: (0, s, 0, h)),
                pl.BlockSpec((3, None, 8, lanes), lambda s, h, *_: (0, s, 0, h)),
            ],
        ),
        out_shape=[
            jax.ShapeDtypeStruct((3, per, seq, count * lanes), BF),
            jax.ShapeDtypeStruct((3, per, 8, count * lanes), F32),
        ],
        compiler_params=pltpu.CompilerParams(vmem_limit_bytes=60 * MIB),
        cost_estimate=cost("attend_back"),
        name="attend_back",
    )(meta, shaped, shaped, shaped, grad.reshape(per, seq, width), mixed.reshape(per, seq, width), lse)
    return out.reshape(3, per * seq, count * lanes), sums


def weight_grad(name, meta, odd, lefts, rights, chunk, come=None, extra=None):
    rows = lefts[0].shape[0]
    tall = lefts[0].shape[1] // 8
    plan = []
    for li, group in enumerate(rights):
        for right in group:
            for c in range((right.shape[0] if right.ndim == 3 else 1) * (right.shape[-1] // chunk)):
                plan.append((li, right, c))
    steps = len(plan)
    flat = [r for group in rights for r in group]
    firsts, pos = [], 0
    for right in flat:
        firsts.append(pos)
        pos += (right.shape[0] if right.ndim == 3 else 1) * (right.shape[-1] // chunk)
    owners = [li for li, group in enumerate(rights) for _ in group]
    below = 0 if extra is None else extra.shape[1]
    cut = (steps + 1) // 2
    n_left = len(lefts)

    def kernel(meta_ref, *refs):
        left_refs = refs[: 4 * n_left]
        pos = 4 * n_left
        right_refs = refs[pos : pos + len(flat)]
        pos += len(flat)
        extra_refs = refs[pos : pos + 4] if below else ()
        pos += len(extra_refs)
        come_ref = refs[pos] if come is not None else None
        pos += come is not None
        outs = refs[pos:]
        c = pl.program_id(0)

        def store(lefts_here, right):
            for k in range(4):
                part = tn(lefts_here[k][...], right)
                if come is None:
                    outs[0][k, 0:tall, :] = part.astype(BF)
                    if below:
                        outs[0][k, tall:, :] = extra_refs[k][...]
                    continue
                part = (part + come_ref[k, 0:tall, :].astype(F32)).astype(BF)
                if below:
                    low = (extra_refs[k][...].astype(F32) + come_ref[k, tall:, :].astype(F32)).astype(BF)
                if k < 3:
                    outs[k][0:tall, :] = part
                    if below:
                        outs[k][tall:, :] = low
                    continue

                @pl.when(c < cut)
                def _():
                    outs[3][0:tall, :] = part
                    if below:
                        outs[3][tall:, :] = low

                @pl.when(c >= cut)
                def _():
                    outs[4][0:tall, :] = part
                    if below:
                        outs[4][tall:, :] = low

        for i, right_ref in enumerate(right_refs):
            last = firsts[i + 1] if i + 1 < len(flat) else steps
            li = owners[i]

            @pl.when((c >= firsts[i]) & (c < last))
            def _(right_ref=right_ref, li=li):
                store(left_refs[4 * li : 4 * li + 4], right_ref[...])

    def left_spec(k):
        return pl.BlockSpec((rows, tall), lambda c, m: (0, m[0] ^ (2 * k + odd)))

    def right_spec(i, right):
        last = (firsts[i + 1] if i + 1 < len(flat) else steps) - 1
        inner = right.shape[-1] // chunk

        def place(c):
            return jnp.clip(c, firsts[i], last) - firsts[i]

        if right.ndim == 3:
            return pl.BlockSpec((None, rows, chunk), lambda c, m: (place(c) // inner, 0, place(c) % inner))
        return pl.BlockSpec((rows, chunk), lambda c, m: (0, place(c)))

    def extra_spec(k):
        return pl.BlockSpec((None, below, chunk), lambda c, m: (m[0] ^ (2 * k + odd), 0, c))

    high = tall + below
    four = pl.BlockSpec((4, high, chunk), lambda c, m: (0, 0, c))
    in_specs = [left_spec(k) for _ in lefts for k in range(4)] + [right_spec(i, r) for i, r in enumerate(flat)]
    args = [left for left in lefts for _ in range(4)] + flat
    if below:
        in_specs += [extra_spec(k) for k in range(4)]
        args += [extra] * 4
    if come is None:
        out_specs = [four]
        out_shape = [jax.ShapeDtypeStruct((4, high, steps * chunk), BF)]
    else:
        in_specs.append(four)
        args.append(come)
        out_specs = [pl.BlockSpec((high, chunk), lambda c, m: (0, c))] * 3 + [
            pl.BlockSpec((high, chunk), lambda c, m: (0, jnp.minimum(c, cut - 1))),
            pl.BlockSpec((high, chunk), lambda c, m: (0, jnp.maximum(c - cut, 0))),
        ]
        out_shape = [jax.ShapeDtypeStruct((high, steps * chunk), BF)] * 3 + [
            jax.ShapeDtypeStruct((high, cut * chunk), BF),
            jax.ShapeDtypeStruct((high, (steps - cut) * chunk), BF),
        ]
    return pl.pallas_call(
        kernel,
        grid_spec=pltpu.PrefetchScalarGridSpec(
            num_scalar_prefetch=1,
            grid=(steps,),
            in_specs=in_specs,
            out_specs=out_specs,
        ),
        out_shape=out_shape,
        compiler_params=pltpu.CompilerParams(vmem_limit_bytes=60 * MIB),
        cost_estimate=cost(name),
        name=name,
    )(meta, *args)


def shards(
    tokens, lengths, w_qkv, bias_qv, w_out, bias_out, gain_one, shift_one,
    w_up, bias_up, w_down, bias_down, gain_two, shift_two, cotangent,
):
    seqs, blk, width = tokens.shape
    n = lax.axis_size("ctx")
    ndp = lax.axis_size("dp")
    me = lax.axis_index("dp")
    place = lax.axis_index("ctx")
    per = seqs // n
    rows = seqs * blk
    tile = per * blk
    ff = w_up.shape[1]
    thin = w_qkv.shape[0]
    tuned = ndp == 8
    half = width // (GROUP * HD) // 2

    own = lax.dynamic_slice_in_dim(lengths, place * per, per)
    meta = jnp.concatenate([jnp.stack([me, place]).astype(jnp.int32), own])

    vectors = (bias_qv, bias_out, gain_one, shift_one, bias_up, bias_down, gain_two, shift_two)
    sizes = [v.shape[0] for v in vectors]
    count = sum(sizes)
    line = jnp.pad(jnp.concatenate(vectors).reshape(1, count), ((0, 15), (0, 3 * width - count)))
    qkv_own = jnp.concatenate([w_qkv, line])
    mid_own = jnp.concatenate([w_out, w_up], axis=1)
    shared = tokens.reshape(n, per, blk, width)
    x = jnp.swapaxes(to_sequences(shared), 0, 1).reshape(rows, width)
    qkv_near = gather_near(qkv_own)
    mid_near = gather_near(mid_own)
    x, qkv_near, mid_near, cotangent = sync(x, qkv_near, mid_near, cotangent)
    qkv_far = gather_far(qkv_near)
    qkv_mine = gather_stack(qkv_own, qkv_near, qkv_far)
    qkv_other = swap(qkv_mine, "dp", 1)
    mid_far = gather_far(mid_near)
    cot_1 = trade(part_of(cotangent, 1), 1)

    both = jnp.concatenate([qkv_mine[:, thin, :count], qkv_other[:, thin, :count]])
    index = jnp.arange(ndp, dtype=jnp.int32) ^ me
    packed = jnp.take(both, (index >> 1) + (index & 1) * (ndp // 2), axis=0).astype(F32)
    fulls, pos = [], 0
    for size in sizes:
        fulls.append(packed[:, pos : pos + size].reshape(1, ndp * size))
        pos += size
    bqv, bout, gone, sone, bup, bdown, gtwo, stwo = fulls
    bqkv = jnp.concatenate([bqv[:, :width], jnp.zeros((1, width), F32), bqv[:, width:]], axis=1)

    qkv_w = (qkv_mine, qkv_other, thin, 0, 3 * width, 3)
    (proj,) = dense(qkv_body, "qkv", meta, rows, tile, [x], [bqkv], [qkv_w], [(3 * width, BF)], [])
    proj, mid_far, cot_1, w_down, cotangent = sync(proj, mid_far, cot_1, w_down, cotangent)
    mid_mine = gather_stack(mid_own, mid_near, mid_far)
    mid_other = swap(mid_mine, "dp", 1)
    down_all = lax.all_gather(w_down, "dp", axis=0, tiled=True)
    cot_2 = trade(part_of(cotangent, 2), 2)
    mixed, lse = attend(meta, proj, per, n * blk)
    mixed, mid_other, cot_2 = sync(mixed, mid_other, cot_2)
    out_w = (mid_mine, mid_other, thin, 0, width, 2)
    up_w = (mid_mine, mid_other, thin, width, ff, 8)
    normed_one, inverse_one, first_low = dense(
        out_body, "out", meta, rows, tile, [mixed, x], [bout, gone, sone], [out_w], [(width, F32), (128, F32), (width, BF)], []
    )
    first_low, cotangent = sync(first_low, cotangent)
    cot_3 = trade(part_of(cotangent, 3), 3)
    active, deriv = dense(up_body, "up", meta, rows, tile, [first_low], [bup], [up_w], [(ff, BF), (ff, BF)], [])
    active, down_all, cot_3 = sync(active, down_all, cot_3)
    down_w = (down_all.reshape(8, ff // 8, width), None, ff // 8, 0, width, 0)
    cot = put_positions([part_of(cotangent, 0), cot_1, cot_2, cot_3]).reshape(rows, width)
    out_parts, sum_two, second, s_gtwo, s_stwo, s_bdown = dense(
        functools.partial(down_body, n * blk, per), "down", meta, rows, tile, [active, normed_one, cot],
        [bdown, gone, sone, gtwo, stwo], [down_w], [(width, BF), (width, F32), (width, BF)], [width] * 3,
    )
    out_parts = out_parts.reshape(per, n * blk, width)
    out_own = part_of(out_parts, 0, 1)
    out_1 = trade(part_of(out_parts, 1, 1), 1)
    cut = (per + 1) // 2

    come = ()
    if tuned:
        (away,) = weight_grad("gd_away", meta, 1, [active], [[second]], 512)
        come = swap(away, "dp", 1)
        second = after(second, away)
    hidden, s_bup = dense(hidden_body, "hidden", meta, rows, tile, [second, deriv], [], [down_w], [(ff, BF)], [ff])
    hidden, come, out_1, out_parts = sync(hidden, come, out_1, out_parts)
    part = part_of(out_parts, 2, 1)
    out_2 = trade(part[:cut], 2)
    d_far, d_near = (), ()
    if tuned:
        d_sums = weight_grad("gd_keep", meta, 0, [active], [[second]], 512, come=come)
        d_far = send_far(d_sums)
        hidden, out_2, part = sync(after(hidden, d_sums[0]), out_2, part)
    out_2b = trade(part[cut:], 2)
    if tuned:
        (away,) = weight_grad("gu_away", meta, 1, [first_low], [[hidden]], 1024)
        hidden = after(hidden, away)
        away, d_far, out_2b = sync(away, d_far, out_2b)
        come = swap(away, "dp", 1)
    hidden, d_far, out_2b, out_parts = sync(hidden, d_far, out_2b, out_parts)
    if tuned:
        d_near = send_near(d_sums, d_far)
    out_3 = trade(part_of(out_parts, 3, 1), 3)
    sum_one, branch, g_mixed, s_gone, s_sone, s_bout = dense(
        first_body, "first", meta, rows, tile, [hidden, sum_two, normed_one, inverse_one], [gone], [up_w[:5] + (4,), out_w[:5] + (1,)],
        [(width, F32), (width, BF), (width, BF)], [width] * 3,
    )
    branch, g_mixed, come, d_near, out_3 = sync(branch, g_mixed, come, d_near, out_3)
    output = put_slots([(0, 0, out_own), (1, 0, out_1), (2, 0, out_2), (2, cut, out_2b), (3, 0, out_3)], per, BF)
    u_far = ()
    if tuned:
        d_share = add_low(d_sums[0], *d_near)
        g_down = lax.psum(d_share, "ctx")
        u_sums = weight_grad("gu_keep", meta, 0, [first_low], [[hidden]], 1024, come=come)
        u_far = send_far(u_sums)
        g_mixed = after(g_mixed, u_sums[0])
    p_one, s_one = attend_back(meta, proj, g_mixed, mixed, lse, per, n * blk, 0, half)
    p_one, g_mixed, u_far = sync(p_one, g_mixed, u_far)
    u_near = ()
    if tuned:
        u_near = send_near(u_sums, u_far)
    p_two, s_two = attend_back(meta, proj, g_mixed, mixed, lse, per, n * blk, half, half)
    if tuned:
        p_two, u_near, g_down = sync(p_two, u_near, g_down)

    s_proj = jnp.concatenate([jnp.sum(s_one, axis=(1, 2)), jnp.sum(s_two, axis=(1, 2))], axis=1)
    vec = [jnp.concatenate([s_proj[0], s_proj[2]])] + [
        jnp.sum(s, axis=0) for s in (s_bout, s_gone, s_sone, s_bup, s_bdown, s_gtwo, s_stwo)
    ]
    vec = jnp.concatenate([v.reshape(ndp, -1) for v in vec], axis=1)

    come = ()
    if tuned:
        u_keep, u_away = halves_ctx(add_low(u_sums[0], *u_near), 1)
        u_come = swap(u_away, "ctx", 1)
        extra = jnp.pad(vec[:, None, :].astype(BF), ((0, 0), (0, 15), (0, 4 * width - count)))
        products = ([x, mixed], [[p_one, p_two], [branch]])
        (away,) = weight_grad("gb_away", meta, 1, *products, 512, extra=extra)
        sum_one = after(sum_one, away)
        away, u_come = sync(away, u_come)
        come = swap(away, "dp", 1)
        u_keep, u_away = halves_ctx(add_low(u_keep, u_come), 2)
        u_come = swap(u_away, "ctx", 2)
    else:
        u_come = ()
    (grad_in,) = dense(input_body, "input", meta, rows, tile, [p_one, p_two, sum_one], [], [qkv_w[:5] + (6,)], [(width, BF)], [])
    grad_in, come, u_come = sync(grad_in, come, u_come)
    grad_in = grad_in.reshape(per, n * blk, width)
    in_1 = trade(part_of(grad_in, 1, 1), 1)
    if tuned:
        u_half = add_low(u_keep, u_come)
        u_other = swap(u_half, "ctx", 2)
        b_sums = weight_grad("gb_keep", meta, 0, *products, 512, come=come, extra=extra)
        b_sums, u_other, in_1, grad_in = sync(b_sums, u_other, in_1, grad_in)
    part_2, part_3 = part_of(grad_in, 2, 1), part_of(grad_in, 3, 1)
    in_2 = trade(part_2[:cut], 2)
    if tuned:
        b_far = send_far(b_sums)
        u_whole = join_ctx(u_half, u_other, 2)
        u_other = swap(u_whole, "ctx", 1)
        b_far, in_2, u_other, part_2, part_3 = sync(b_far, in_2, u_other, part_2, part_3)
        b_near = send_near(b_sums, b_far)
    in_2b, in_3 = trade(part_2[cut:], 2), trade(part_3[:cut], 3)
    if tuned:
        b_near, in_2b, in_3, part_3 = sync(b_near, in_2b, in_3, part_3)
        b_keep, b_away = halves_ctx(add_low(b_sums[0], *b_near), 1)
        b_come = swap(b_away, "ctx", 1)
    in_3b = trade(part_3[cut:], 3)
    in_rest = [(2, 0, in_2), (2, cut, in_2b), (3, 0, in_3), (3, cut, in_3b)]
    if tuned:
        b_come, in_3b = sync(b_come, in_3b)
        b_half = add_low(b_keep, b_come)
        g_up = join_ctx(u_whole, u_other, 1)
        total = whole_ctx(whole_ctx(halve_ctx(b_half, 2), 2), 1).astype(F32)
        part = width // 2
        g_qkv = jnp.concatenate(
            [total[:thin, (p * 3 + c) * part : (p * 3 + c + 1) * part] for c in range(3) for p in range(2)], axis=1
        )
        g_out = total[:thin, 3 * width :]
        g_up = g_up.astype(F32)
        g_down = g_down.astype(F32)
        vec = total[thin, :count]
    else:
        def whole(*products):
            return jnp.concatenate([tn(a, b).astype(BF) for a, b in products], axis=1)

        def total(grad):
            return lax.psum(reduce_any(grad).astype(F32), "ctx")

        g_down = total(whole((active, second)))
        g_up = total(whole((first_low, hidden)))
        g_out = total(whole((mixed, branch)))
        g_qkv = total(whole(*[(x, p[c]) for c in range(3) for p in (p_one, p_two)]))
        vec = lax.psum(lax.psum_scatter(vec, "dp", scatter_dimension=0, tiled=True), "ctx").reshape(-1)
    grads, pos = [], 0
    for size in sizes:
        grads.append(vec[pos : pos + size])
        pos += size
    g_bqv, g_bout, g_gone, g_sone, g_bup, g_bdown, g_gtwo, g_stwo = grads
    grad_input = put_slots([(0, 0, part_of(grad_in, 0, 1)), (1, 0, in_1)] + in_rest, per, F32)
    return (
        output, grad_input, g_qkv, g_bqv, g_out, g_bout, g_gone, g_sone, g_up, g_bup, g_down, g_bdown, g_gtwo, g_stwo,
    )


def solution(mesh):
    row = P("dp", "ctx", None)
    mat = P("dp", None)
    vec = P("dp")
    weights = (mat, vec, mat, vec, vec, vec, mat, vec, mat, vec, vec, vec)
    return jax.shard_map(
        shards, mesh=mesh, in_specs=(row, vec) + weights + (row,), out_specs=(row, row) + weights, check_vma=False
    )
```

```python
import functools

import jax
import jax.numpy as jnp
from jax import lax
from jax.experimental import pallas as pl
from jax.experimental.pallas import tpu as pltpu
from jax.sharding import PartitionSpec as P

HD = 64
GROUP = 4
NEG = -1e30
EPS = 1e-06
BF = jnp.bfloat16
F32 = jnp.float32
MIB = 1024 * 1024
COSTS = {'qkv': 13, 'out': 10, 'up': 23, 'down': 21, 'hidden': 18, 'first': 23, 'input': 14, 'attend': 24, 'attend_back': 21, 'gd_away': 11, 'gd_keep': 11, 'gu_away': 11, 'gu_keep': 11, 'gb_away': 14, 'gb_keep': 3, 'gc_away': 8, 'gc_keep': 8}


def cost(name):
    return pl.CostEstimate(flops=COSTS[name] * 1000000000, bytes_accessed=1000000, transcendentals=0)


ANY = pl.BlockSpec(memory_space=pl.ANY)


def swap(x, axis, bit):
    n = lax.axis_size(axis)
    return lax.ppermute(x, axis, [(i, i ^ bit) for i in range(n)])


def after(x, *others):
    return lax.optimization_barrier((x,) + others)[0]


def sync(*values):
    return lax.optimization_barrier(values)


def gather_near(own):
    if lax.axis_size("dp") != 8:
        return ()
    return swap(own, "dp", 2), swap(own, "dp", 4)


def gather_far(near):
    if not near:
        return ()
    half = near[0].shape[1] // 2
    return swap(near[0][:, :half], "dp", 4), swap(near[1][:, half:], "dp", 2)


def gather_stack(own, near, far):
    if near:
        return jnp.stack([own, near[0], near[1], jnp.concatenate(far, axis=1)])
    mine = own[None]
    bit = 2
    while bit < lax.axis_size("dp"):
        mine = jnp.concatenate([mine, swap(mine, "dp", bit)])
        bit *= 2
    return mine


def add_low(*parts):
    total = parts[0].astype(F32)
    for part in parts[1:]:
        total = total + part.astype(F32)
    return total.astype(BF)


def reduce_any(grad):
    n = lax.axis_size("dp")
    me = lax.axis_index("dp")
    rows = grad.shape[0] // n
    width = grad.shape[1]

    def stack(odd):
        return jnp.stack(
            [lax.dynamic_slice(grad, ((me ^ (2 * k + odd)) * rows, 0), (rows, width)) for k in range(n // 2)]
        )

    mine = add_low(stack(0), swap(stack(1), "dp", 1))
    bit = n // 2
    while bit > 1:
        keep = mine.shape[0] // 2
        mine = add_low(mine[:keep], swap(mine[keep:], "dp", bit))
        bit //= 2
    return mine[0]


def send_far(sums):
    return swap(sums[3], "dp", 4), swap(sums[4], "dp", 2)


def send_near(sums, far):
    own, to_x, to_y = sums[:3]
    cut, width = far[0].shape[1], to_x.shape[1]
    to_x = add_low(to_x, jnp.pad(far[0], ((0, 0), (0, width - cut))))
    to_y = add_low(to_y, jnp.pad(far[1], ((0, 0), (cut, 0))))
    return swap(to_x, "dp", 2), swap(to_y, "dp", 4)


def halves_ctx(share, bit):
    half = share.shape[1] // 2
    mine = (lax.axis_index("ctx") // bit) % 2
    keep = lax.dynamic_slice_in_dim(share, mine * half, half, axis=1)
    return keep, lax.dynamic_slice_in_dim(share, (1 - mine) * half, half, axis=1)


def halve_ctx(share, bit):
    keep, away = halves_ctx(share, bit)
    return add_low(keep, swap(away, "ctx", bit))


def join_ctx(half, other, bit):
    low = (lax.axis_index("ctx") // bit) % 2 == 0
    return jnp.concatenate([jnp.where(low, half, other), jnp.where(low, other, half)], axis=1)


def whole_ctx(half, bit):
    return join_ctx(half, swap(half, "ctx", bit), bit)


def to_sequences(block):
    return lax.all_to_all(block, "ctx", 0, 0, tiled=True)


def part_of(block, j, axis=0):
    n = lax.axis_size("ctx")
    per = block.shape[axis] // n
    return lax.dynamic_slice_in_dim(block, (lax.axis_index("ctx") ^ j) * per, per, axis=axis)


def put_slots(pieces, per, dtype):
    n = lax.axis_size("ctx")
    out = jnp.zeros((n * per,) + pieces[0][2].shape[1:], dtype)
    for j, first, piece in pieces:
        start = (lax.axis_index("ctx") ^ j) * per + first
        out = lax.dynamic_update_slice_in_dim(out, piece.astype(dtype), start, axis=0)
    return out


def put_positions(pieces, per):
    n = lax.axis_size("ctx")
    blk, width = pieces[0][2].shape[1:]
    out = jnp.zeros((per, n * blk, width), pieces[0][2].dtype)
    for j, first, piece in pieces:
        out = lax.dynamic_update_slice(out, piece, (first, (lax.axis_index("ctx") ^ j) * blk, 0))
    return out


def trade(block, j):
    return swap(block, "ctx", j)


def nn(left, right):
    return jnp.dot(left, right, preferred_element_type=F32)


def nt(left, right):
    return lax.dot_general(left, right, (((1,), (1,)), ((), ())), preferred_element_type=F32)


def tn(left, right):
    return lax.dot_general(left, right, (((0,), (0,)), ((), ())), preferred_element_type=F32)


def fold(rows):
    return jnp.sum(rows.reshape(rows.shape[0] // 8, 8, rows.shape[1]), axis=0)


class Weight:
    def __init__(self, stacks, whole, sems, me, rows, first, pieces):
        self.whole, self.pieces = whole, pieces
        self.step = whole.shape[1] // max(pieces, 1)
        self.copies, self.starts = [], []
        for odd, stack in enumerate(stacks):
            count = stack.shape[0]
            for k in range(count):
                start = pl.multiple_of((me ^ (2 * k + odd)) * rows if len(stacks) == 2 else k * rows, rows)
                self.starts.append(pl.ds(start, rows))
                for p in range(max(pieces, 1)):
                    here, there = pl.ds(first + p * self.step, self.step), pl.ds(p * self.step, self.step)
                    copy = pltpu.make_async_copy(
                        stack.at[k, pl.ds(0, rows), here], whole.at[self.starts[-1], there], sems.at[odd * count + k, p]
                    )
                    self.copies.append((k * 2 + odd, p, copy))
        self.wait_for = False

    def start(self):
        for _, _, copy in sorted(self.copies, key=lambda c: c[1] if self.pieces else c[0]):
            copy.start()

    def cols(self, p):
        if self.wait_for:
            for _, q, copy in self.copies:
                if q == p:
                    copy.wait()
        return slice(p * self.step, (p + 1) * self.step)

    def rows(self, c):
        _, _, copy = self.copies[c]
        if self.wait_for:
            copy.wait()
        return self.starts[c]


def row_spec(tile, width):
    return pl.BlockSpec((tile, width), lambda i, *_: (i, 0))


def one_spec(height, width):
    return pl.BlockSpec((height, width), lambda i, *_: (0, 0))


def dense(body, name, meta, rows, tile, row_ins, vec_ins, weights, row_outs, sums):
    stacks, spans, scratch = [], [], []
    for mine, other, r, _, width, pieces in weights:
        held = [mine] if other is None else [mine, other]
        spans.append(slice(len(stacks), len(stacks) + len(held)))
        stacks += held
        count = mine.shape[0] * len(held)
        scratch.append(pltpu.VMEM((count * r, width), BF))
        scratch.append(pltpu.SemaphoreType.DMA((count, max(pieces, 1))))
    n_row, n_vec, n_stack = len(row_ins), len(vec_ins), len(stacks)
    n_out, n_sum = len(row_outs), len(sums)

    def kernel(meta_ref, *refs):
        pos = 0
        groups = []
        for count in (n_row, n_vec, n_stack, n_out, n_sum, 2 * len(weights)):
            groups.append(refs[pos : pos + count])
            pos += count
        row_refs, vec_refs, stack_refs, out_refs, sum_refs, scratch_refs = groups

        whole = [
            Weight(stack_refs[spans[w]], scratch_refs[2 * w], scratch_refs[2 * w + 1], meta_ref[0], weights[w][2], weights[w][3], weights[w][5])
            for w in range(len(weights))
        ]

        def work(wait_for):
            for weight in whole:
                weight.wait_for = wait_for
            body(meta_ref, row_refs, vec_refs, whole, out_refs, sum_refs)

        @pl.when(pl.program_id(0) == 0)
        def _():
            for weight in whole:
                weight.start()
            for ref in sum_refs:
                ref[...] = jnp.zeros_like(ref)
            work(True)

        @pl.when(pl.program_id(0) > 0)
        def _():
            work(False)

    in_specs = (
        [row_spec(tile, a.shape[-1]) if a.ndim == 2 else pl.BlockSpec((a.shape[0], tile, a.shape[2]), lambda i, *_: (0, i, 0)) for a in row_ins]
        + [one_spec(1, v.shape[1]) for v in vec_ins]
        + [ANY] * n_stack
    )
    out_specs = [row_spec(tile, w) for w, _ in row_outs] + [one_spec(8, w) for w in sums]
    out_shape = [jax.ShapeDtypeStruct((rows, w), d) for w, d in row_outs] + [
        jax.ShapeDtypeStruct((8, w), F32) for w in sums
    ]
    return pl.pallas_call(
        kernel,
        grid_spec=pltpu.PrefetchScalarGridSpec(
            num_scalar_prefetch=1,
            grid=(rows // tile,),
            in_specs=in_specs,
            out_specs=out_specs,
            scratch_shapes=scratch,
        ),
        out_shape=out_shape,
        compiler_params=pltpu.CompilerParams(vmem_limit_bytes=60 * MIB, dimension_semantics=("arbitrary",)),
        cost_estimate=cost(name),
        name=name,
    )(meta, *row_ins, *vec_ins, *stacks)


def by_columns(left, weight):
    parts = []
    for p in range(weight.pieces):
        cols = weight.cols(p)
        parts.append(nn(left[...], weight.whole[:, cols]))
    return jnp.concatenate(parts, axis=1)


def by_columns_turned(left, weight):
    total = None
    for p in range(weight.pieces):
        cols = weight.cols(p)
        part = nt(left[:, cols], weight.whole[:, cols])
        total = part if total is None else total + part
    return total


def by_shards(left, weight):
    if weight.pieces:
        return by_columns(left, weight)
    if not weight.wait_for:
        return nn(left[...], weight.whole[...])
    total = None
    for c in range(len(weight.copies)):
        here = weight.rows(c)
        part = nn(left[:, here], weight.whole[here, :])
        total = part if total is None else total + part
    return total


def qkv_body(meta, rows, vecs, whole, outs, sums):
    (x,) = rows
    (bias,) = vecs
    for p in range(whole[0].pieces):
        cols = whole[0].cols(p)
        outs[0][:, cols] = (nn(x[...], whole[0].whole[:, cols]) + bias[:, cols]).astype(BF)


def out_body(meta, rows, vecs, whole, outs, sums):
    mixed, x = rows
    bias, gain, shift = vecs
    total = x[...].astype(F32) + (by_columns(mixed, whole[0]) + bias[...])
    centre = total - jnp.mean(total, axis=-1, keepdims=True)
    inverse = lax.rsqrt(jnp.mean(centre * centre, axis=-1, keepdims=True) + EPS)
    normed = centre * inverse
    outs[0][...] = normed
    outs[1][...] = jnp.broadcast_to(inverse, outs[1].shape)
    outs[2][...] = (normed * gain[...] + shift[...]).astype(BF)


def up_body(meta, rows, vecs, whole, outs, sums):
    (low,) = rows
    (bias,) = vecs
    for p in range(whole[0].pieces):
        cols = whole[0].cols(p)
        hidden = nn(low[...], whole[0].whole[:, cols]) + bias[:, cols]
        cdf = 0.5 + 0.5 * lax.erf(hidden * 0.7071067811865476)
        pdf = jnp.exp(-0.5 * hidden * hidden) * 0.3989422804014327
        outs[0][:, cols] = (hidden * cdf).astype(BF)
        outs[1][:, cols] = (cdf + hidden * pdf).astype(BF)


def down_body(seq, per, meta, rows, vecs, whole, outs, sums):
    active, normed_one, cot = rows
    bias, gain_one, shift_one, gain, shift = vecs
    total = (normed_one[...] * gain_one[...] + shift_one[...]) + (by_shards(active, whole[0]) + bias[...])
    centre = total - jnp.mean(total, axis=-1, keepdims=True)
    inverse = lax.rsqrt(jnp.mean(centre * centre, axis=-1, keepdims=True) + EPS)
    normed = centre * inverse
    tile = total.shape[0]
    at = lax.broadcasted_iota(jnp.int32, (tile, 1), 0) + pl.program_id(0) * tile
    valid = jnp.zeros(at.shape, jnp.bool_)
    for s in range(per):
        valid = valid | ((at >= s * seq) & (at < s * seq + meta[2 + s]))
    keep = jnp.where(valid, 1.0, 0.0)
    outs[0][...] = ((normed * gain[...] + shift[...]) * keep).astype(BF)
    grad = cot[...].astype(F32) * keep
    sums[0][...] += fold(grad * normed)
    sums[1][...] += fold(grad)
    scaled = grad * gain[...]
    back = inverse * (
        scaled
        - jnp.mean(scaled, axis=-1, keepdims=True)
        - normed * jnp.mean(scaled * normed, axis=-1, keepdims=True)
    )
    low = back.astype(BF)
    outs[1][...] = back
    outs[2][...] = low
    sums[2][...] += fold(low.astype(F32))


def hidden_kernel(second, whole, deriv, out, total):
    low = (nt(second[...], whole[...]) * deriv[...].astype(F32)).astype(BF)
    out[...] = low
    total[...] = fold(low.astype(F32))


def hidden_grad(second, whole, deriv, step):
    rows, width = second.shape
    ff = whole.shape[0]
    cols = pl.BlockSpec((rows, step), lambda i: (0, i))
    return pl.pallas_call(
        hidden_kernel,
        grid=(ff // step,),
        in_specs=[pl.BlockSpec((rows, width), lambda i: (0, 0)), pl.BlockSpec((step, width), lambda i: (i, 0)), cols],
        out_specs=[cols, pl.BlockSpec((8, step), lambda i: (0, i))],
        out_shape=[jax.ShapeDtypeStruct((rows, ff), BF), jax.ShapeDtypeStruct((8, ff), F32)],
        compiler_params=pltpu.CompilerParams(vmem_limit_bytes=60 * MIB),
        cost_estimate=cost("hidden"),
        name="hidden",
    )(second, whole, deriv)


def first_body(meta, rows, vecs, whole, outs, sums):
    hidden, sum_two, normed, inverse = rows
    (gain,) = vecs
    grad = sum_two[...] + by_columns_turned(hidden, whole[0])
    n1 = normed[...]
    sums[0][...] += fold(grad * n1)
    sums[1][...] += fold(grad)
    scaled = grad * gain[...]
    back = inverse[:, 0:1] * (
        scaled - jnp.mean(scaled, axis=-1, keepdims=True) - n1 * jnp.mean(scaled * n1, axis=-1, keepdims=True)
    )
    low = back.astype(BF)
    outs[0][...] = back
    outs[1][...] = low
    sums[2][...] += fold(low.astype(F32))
    whole[1].cols(0)
    outs[2][...] = nt(low, whole[1].whole[...]).astype(BF)


def input_body(meta, rows, vecs, whole, outs, sums):
    sum_one = rows[-1]
    total = sum_one[...]
    parts = len(rows) - 1
    for p in range(whole[0].pieces):
        cols = whole[0].cols(p)
        total = total + nt(rows[p % parts][p // parts], whole[0].whole[:, cols])
    outs[0][...] = total.astype(BF)


def key_mask(meta, seq):
    at = lax.broadcasted_iota(jnp.int32, (seq, 1), 0)
    return at < meta[2 + pl.program_id(0)]


def attend_kernel(meta, q_ref, k_ref, v_ref, mixed_ref, lse_ref):
    seq, lanes = q_ref.shape
    ok = key_mask(meta, seq)
    q_all = q_ref[...] * BF(HD ** (-0.5))
    k_all, v_turned = k_ref[...], v_ref[...].T
    ones = jnp.ones((16, seq), BF)
    outs = []
    for h in range(lanes // HD):
        cols = slice(h * HD, (h + 1) * HD)
        scores = jnp.where(ok, nt(k_all[:, cols], q_all[:, cols]), NEG)
        peak = jnp.max(scores, axis=0, keepdims=True)
        weights = jnp.exp(scores - peak).astype(BF)
        both = nn(jnp.concatenate([v_turned[cols], ones], axis=0), weights)
        total = both[HD : HD + 1]
        lse_ref[h : h + 1, :] = peak + jnp.log(total)
        outs.append(both[:HD] * (1.0 / total))
    mixed_ref[...] = jnp.concatenate(outs, axis=0).T.astype(BF)


def attend_back_kernel(meta, q_ref, k_ref, v_ref, g_ref, mixed_ref, lse_ref, proj_ref, sum_ref):
    seq, lanes = q_ref.shape
    ok = key_mask(meta, seq)
    scale = HD ** (-0.5)
    q_all = q_ref[...] * BF(scale)
    k_all, v_all, g_all = k_ref[...], v_ref[...], g_ref[...]
    k_turned = k_all.T
    inners = (g_all.astype(F32) * mixed_ref[...].astype(F32)).T
    gq, gk, gv = [], [], []
    for h in range(lanes // HD):
        cols = slice(h * HD, (h + 1) * HD)
        q, k, v, g = q_all[:, cols], k_all[:, cols], v_all[:, cols], g_all[:, cols]
        exact = jnp.exp(jnp.where(ok, nt(k, q), NEG) - lse_ref[h : h + 1, :])
        inner = jnp.sum(inners[cols], axis=0, keepdims=True)
        low = (exact * (nt(v, g) - inner)).astype(BF)
        gq.append(nn(k_turned[cols], low) * scale)
        gk.append(nn(low, q))
        gv.append(nn(exact.astype(BF), g))
    wholes = (jnp.concatenate(gq, axis=0).T, jnp.concatenate(gk, axis=1), jnp.concatenate(gv, axis=1))
    for c, whole in enumerate(wholes):
        low = whole.astype(BF)
        proj_ref[c] = low
        sum_ref[c] = fold(low.astype(F32))


def attend(meta, proj, per, seq):
    lanes = GROUP * HD
    groups = proj.shape[-1] // 3 // lanes
    shaped = proj.reshape(per, seq, proj.shape[-1])

    def spec(c):
        return pl.BlockSpec((None, seq, lanes), lambda s, h, *_: (s, 0, c * groups + h))

    mixed, lse = pl.pallas_call(
        attend_kernel,
        grid_spec=pltpu.PrefetchScalarGridSpec(
            num_scalar_prefetch=1,
            grid=(per, groups),
            in_specs=[spec(0), spec(1), spec(2)],
            out_specs=[spec(0), pl.BlockSpec((None, None, GROUP, seq), lambda s, h, *_: (s, h, 0, 0))],
        ),
        out_shape=[
            jax.ShapeDtypeStruct((per, seq, groups * lanes), BF),
            jax.ShapeDtypeStruct((per, groups, GROUP, seq), F32),
        ],
        compiler_params=pltpu.CompilerParams(vmem_limit_bytes=60 * MIB),
        cost_estimate=cost("attend"),
        name="attend",
    )(meta, shaped, shaped, shaped)
    return mixed.reshape(per * seq, -1), lse


def attend_back(meta, proj, grad, mixed, lse, per, seq, first, count):
    width = proj.shape[-1] // 3
    lanes = GROUP * HD
    groups = width // lanes
    shaped = proj.reshape(per, seq, proj.shape[-1])

    def spec(c):
        return pl.BlockSpec((None, seq, lanes), lambda s, h, *_: (s, 0, c * groups + first + h))

    out, sums = pl.pallas_call(
        attend_back_kernel,
        grid_spec=pltpu.PrefetchScalarGridSpec(
            num_scalar_prefetch=1,
            grid=(per, count),
            in_specs=[spec(0), spec(1), spec(2), spec(0), spec(0)]
            + [pl.BlockSpec((None, None, GROUP, seq), lambda s, h, *_: (s, first + h, 0, 0))],
            out_specs=[
                pl.BlockSpec((3, None, seq, lanes), lambda s, h, *_: (0, s, 0, h)),
                pl.BlockSpec((3, None, 8, lanes), lambda s, h, *_: (0, s, 0, h)),
            ],
        ),
        out_shape=[
            jax.ShapeDtypeStruct((3, per, seq, count * lanes), BF),
            jax.ShapeDtypeStruct((3, per, 8, count * lanes), F32),
        ],
        compiler_params=pltpu.CompilerParams(vmem_limit_bytes=60 * MIB),
        cost_estimate=cost("attend_back"),
        name="attend_back",
    )(meta, shaped, shaped, shaped, grad.reshape(per, seq, width), mixed.reshape(per, seq, width), lse)
    return out.reshape(3, per * seq, count * lanes), sums


def weight_grad(name, meta, odd, lefts, rights, chunk, come=None, extra=None):
    rows = lefts[0].shape[0]
    tall = lefts[0].shape[1] // 8

    def count(right):
        return right[0].shape[0] if isinstance(right, tuple) else right.shape[1] // chunk

    flat = [r for group in rights for r in group]
    owners = [li for li, group in enumerate(rights) for _ in group]
    firsts, steps = [], 0
    for right in flat:
        firsts.append(steps)
        steps += count(right)
    spread = [(i, r) for i, right in enumerate(flat) for r in (right if isinstance(right, tuple) else (right,))]
    below = 0 if extra is None else extra.shape[1]
    cut = (steps + 1) // 2
    n_left = len(lefts)

    def kernel(meta_ref, *refs):
        left_refs = refs[: 4 * n_left]
        pos = 4 * n_left
        right_refs = [[] for _ in flat]
        for i, _ in spread:
            right_refs[i].append(refs[pos])
            pos += 1
        extra_refs = refs[pos : pos + 4] if below else ()
        pos += len(extra_refs)
        come_ref = refs[pos] if come is not None else None
        pos += come is not None
        outs = refs[pos:]
        c = pl.program_id(0)

        def store(lefts_here, right):
            joined = tn(jnp.concatenate([left[...] for left in lefts_here], axis=1), right) if tall < 256 else None
            for k in range(4):
                part = tn(lefts_here[k][...], right) if joined is None else joined[k * tall : (k + 1) * tall]
                if come is None:
                    outs[0][k, 0:tall, :] = part.astype(BF)
                    if below:
                        outs[0][k, tall:, :] = extra_refs[k][...]
                    continue
                part = (part + come_ref[k, 0:tall, :].astype(F32)).astype(BF)
                if below:
                    low = (extra_refs[k][...].astype(F32) + come_ref[k, tall:, :].astype(F32)).astype(BF)
                if k < 3:
                    outs[k][0:tall, :] = part
                    if below:
                        outs[k][tall:, :] = low
                    continue

                @pl.when(c < cut)
                def _():
                    outs[3][0:tall, :] = part
                    if below:
                        outs[3][tall:, :] = low

                @pl.when(c >= cut)
                def _():
                    outs[4][0:tall, :] = part
                    if below:
                        outs[4][tall:, :] = low

        for i in range(len(flat)):
            last = firsts[i + 1] if i + 1 < len(flat) else steps
            li = owners[i]

            @pl.when((c >= firsts[i]) & (c < last))
            def _(i=i, li=li):
                store(left_refs[4 * li : 4 * li + 4], jnp.concatenate([r[...] for r in right_refs[i]], axis=1))

    def left_spec(k):
        return pl.BlockSpec((rows, tall), lambda c, m: (0, m[0] ^ (2 * k + odd)))

    def right_spec(i, right):
        last = (firsts[i + 1] if i + 1 < len(flat) else steps) - 1

        def place(c):
            return jnp.clip(c, firsts[i], last) - firsts[i]

        if right.ndim == 3:
            return pl.BlockSpec((None, rows, right.shape[2]), lambda c, m: (place(c), 0, 0))
        return pl.BlockSpec((rows, chunk), lambda c, m: (0, place(c)))

    def extra_spec(k):
        return pl.BlockSpec((None, below, chunk), lambda c, m: (m[0] ^ (2 * k + odd), 0, c))

    high = tall + below
    four = pl.BlockSpec((4, high, chunk), lambda c, m: (0, 0, c))
    in_specs = [left_spec(k) for _ in lefts for k in range(4)] + [right_spec(i, r) for i, r in spread]
    args = [left for left in lefts for _ in range(4)] + [r for _, r in spread]
    if below:
        in_specs += [extra_spec(k) for k in range(4)]
        args += [extra] * 4
    if come is None:
        out_specs = [four]
        out_shape = [jax.ShapeDtypeStruct((4, high, steps * chunk), BF)]
    else:
        in_specs.append(four)
        args.append(come)
        out_specs = [pl.BlockSpec((high, chunk), lambda c, m: (0, c))] * 3 + [
            pl.BlockSpec((high, chunk), lambda c, m: (0, jnp.minimum(c, cut - 1))),
            pl.BlockSpec((high, chunk), lambda c, m: (0, jnp.maximum(c - cut, 0))),
        ]
        out_shape = [jax.ShapeDtypeStruct((high, steps * chunk), BF)] * 3 + [
            jax.ShapeDtypeStruct((high, cut * chunk), BF),
            jax.ShapeDtypeStruct((high, (steps - cut) * chunk), BF),
        ]
    return pl.pallas_call(
        kernel,
        grid_spec=pltpu.PrefetchScalarGridSpec(
            num_scalar_prefetch=1,
            grid=(steps,),
            in_specs=in_specs,
            out_specs=out_specs,
        ),
        out_shape=out_shape,
        compiler_params=pltpu.CompilerParams(vmem_limit_bytes=60 * MIB),
        cost_estimate=cost(name),
        name=name,
    )(meta, *args)


def shards(
    tokens, lengths, w_qkv, bias_qv, w_out, bias_out, gain_one, shift_one,
    w_up, bias_up, w_down, bias_down, gain_two, shift_two, cotangent,
):
    seqs, blk, width = tokens.shape
    n = lax.axis_size("ctx")
    ndp = lax.axis_size("dp")
    me = lax.axis_index("dp")
    place = lax.axis_index("ctx")
    per = seqs // n
    rows = seqs * blk
    tile = per * blk
    ff = w_up.shape[1]
    thin = w_qkv.shape[0]
    tuned = ndp == 8
    half = width // (GROUP * HD) // 2
    cut = (per + 1) // 2

    own = lax.dynamic_slice_in_dim(lengths, place * per, per)
    meta = jnp.concatenate([jnp.stack([me, place]).astype(jnp.int32), own])

    vectors = (bias_qv, bias_out, gain_one, shift_one, bias_up, bias_down, gain_two, shift_two)
    sizes = [v.shape[0] for v in vectors]
    count = sum(sizes)
    line = jnp.pad(jnp.concatenate(vectors).reshape(1, count), ((0, 15), (0, 3 * width - count)))
    qkv_own = jnp.concatenate([w_qkv, line])
    mid_own = jnp.concatenate([w_out, w_up], axis=1)
    shared = tokens.reshape(n, per, blk, width)
    x = jnp.swapaxes(to_sequences(shared), 0, 1).reshape(rows, width)
    qkv_near = gather_near(qkv_own)
    mid_near = gather_near(mid_own)
    x, qkv_near, mid_near, cotangent = sync(x, qkv_near, mid_near, cotangent)
    qkv_far = gather_far(qkv_near)
    qkv_mine = gather_stack(qkv_own, qkv_near, qkv_far)
    qkv_other = swap(qkv_mine, "dp", 1)
    mid_far = gather_far(mid_near)
    cot_1 = trade(part_of(cotangent, 1), 1)

    both = jnp.concatenate([qkv_mine[:, thin, :count], qkv_other[:, thin, :count]])
    index = jnp.arange(ndp, dtype=jnp.int32) ^ me
    packed = jnp.take(both, (index >> 1) + (index & 1) * (ndp // 2), axis=0).astype(F32)
    fulls, pos = [], 0
    for size in sizes:
        fulls.append(packed[:, pos : pos + size].reshape(1, ndp * size))
        pos += size
    bqv, bout, gone, sone, bup, bdown, gtwo, stwo = fulls
    bqkv = jnp.concatenate([bqv[:, :width], jnp.zeros((1, width), F32), bqv[:, width:]], axis=1)

    qkv_w = (qkv_mine, qkv_other, thin, 0, 3 * width, 3)
    (proj,) = dense(qkv_body, "qkv", meta, rows, tile, [x], [bqkv], [qkv_w], [(3 * width, BF)], [])
    proj, mid_far, cot_1, w_down, cotangent = sync(proj, mid_far, cot_1, w_down, cotangent)
    mid_mine = gather_stack(mid_own, mid_near, mid_far)
    mid_other = swap(mid_mine, "dp", 1)
    down_all = lax.all_gather(w_down, "dp", axis=0, tiled=True)
    cot_2 = trade(part_of(cotangent, 2), 2)
    mixed, lse = attend(meta, proj, per, n * blk)
    mixed, mid_other, cot_2 = sync(mixed, mid_other, cot_2)
    out_w = (mid_mine, mid_other, thin, 0, width, 2)
    up_w = (mid_mine, mid_other, thin, width, ff, 8)
    normed_one, inverse_one, first_low = dense(
        out_body, "out", meta, rows, tile, [mixed, x], [bout, gone, sone], [out_w], [(width, F32), (128, F32), (width, BF)], []
    )
    first_low, cotangent = sync(first_low, cotangent)
    cot_3 = trade(part_of(cotangent, 3), 3)
    active, deriv = dense(up_body, "up", meta, rows, tile, [first_low], [bup], [up_w], [(ff, BF), (ff, BF)], [])
    active, down_all, cot_3 = sync(active, down_all, cot_3)
    down_w = (down_all.reshape(8, ff // 8, width), None, ff // 8, 0, width, 0)
    cot = put_positions([(0, 0, part_of(cotangent, 0)), (1, 0, cot_1), (2, 0, cot_2), (3, 0, cot_3)], per).reshape(rows, width)
    out_parts, sum_two, second, s_gtwo, s_stwo, s_bdown = dense(
        functools.partial(down_body, n * blk, per), "down", meta, rows, tile, [active, normed_one, cot],
        [bdown, gone, sone, gtwo, stwo], [down_w], [(width, BF), (width, F32), (width, BF)], [width] * 3,
    )
    out_parts = out_parts.reshape(per, n * blk, width)
    out_own = part_of(out_parts, 0, 1)
    out_1 = trade(part_of(out_parts, 1, 1), 1)

    come = ()
    if tuned:
        (away,) = weight_grad("gd_away", meta, 1, [active], [[second]], 512)
        come = swap(away, "dp", 1)
        second = after(second, away)
    hidden, s_bup = hidden_grad(second, down_all, deriv, 1024)
    hidden, come, out_1, out_parts = sync(hidden, come, out_1, out_parts)
    part = part_of(out_parts, 2, 1)
    out_2 = trade(part[:cut], 2)
    d_far, d_near = (), ()
    if tuned:
        d_sums = weight_grad("gd_keep", meta, 0, [active], [[second]], 512, come=come)
        d_far = send_far(d_sums)
        hidden, out_2, part = sync(after(hidden, d_sums[0]), out_2, part)
    out_2b = trade(part[cut:], 2)
    if tuned:
        (away,) = weight_grad("gu_away", meta, 1, [first_low], [[hidden]], 1024)
        hidden = after(hidden, away)
        away, d_far, out_2b = sync(away, d_far, out_2b)
        come = swap(away, "dp", 1)
    hidden, d_far, out_2b, out_parts = sync(hidden, d_far, out_2b, out_parts)
    if tuned:
        d_near = send_near(d_sums, d_far)
    out_3 = trade(part_of(out_parts, 3, 1), 3)
    sum_one, branch, g_mixed, s_gone, s_sone, s_bout = dense(
        first_body, "first", meta, rows, tile, [hidden, sum_two, normed_one, inverse_one], [gone], [up_w[:5] + (4,), out_w[:5] + (1,)],
        [(width, F32), (width, BF), (width, BF)], [width] * 3,
    )
    branch, g_mixed, come, d_near, out_3 = sync(branch, g_mixed, come, d_near, out_3)
    output = put_slots([(0, 0, out_own), (1, 0, out_1), (2, 0, out_2), (2, cut, out_2b), (3, 0, out_3)], per, BF)
    u_far = ()
    if tuned:
        d_share = add_low(d_sums[0], *d_near)
        g_down = lax.psum(d_share, "ctx")
        u_sums = weight_grad("gu_keep", meta, 0, [first_low], [[hidden]], 1024, come=come)
        u_far = send_far(u_sums)
        g_mixed = after(g_mixed, u_sums[0])
    p_one, s_one = attend_back(meta, proj, g_mixed, mixed, lse, per, n * blk, 0, half)
    p_one, g_mixed, u_far = sync(p_one, g_mixed, u_far)
    u_near = ()
    if tuned:
        u_near = send_near(u_sums, u_far)
    p_two, s_two = attend_back(meta, proj, g_mixed, mixed, lse, per, n * blk, half, half)
    if tuned:
        p_two, u_near, g_down = sync(p_two, u_near, g_down)

    eights = (s_bout, s_gone, s_sone, s_bup, s_bdown, s_gtwo, s_stwo)
    p_two, s_one, s_two, eights = sync(p_two, s_one, s_two, eights)
    heads = jnp.sum(jnp.concatenate([s_one, s_two], axis=3), axis=(1, 2))
    vec = jnp.concatenate([heads[0], heads[2], jnp.sum(jnp.concatenate(eights, axis=1), axis=0)])
    places, pos = [], 0
    for size in sizes:
        places.append(vec[pos : pos + ndp * size])
        pos += ndp * size
    vec = places
    vec = jnp.concatenate([v.reshape(ndp, -1) for v in vec], axis=1)

    come = ()
    if tuned:
        u_keep, u_away = halves_ctx(add_low(u_sums[0], *u_near), 1)
        u_come = swap(u_away, "ctx", 1)
        extra = jnp.pad(vec[:, None, :].astype(BF), ((0, 0), (0, 15), (0, 4 * width - count)))
        products = ([x, mixed], [[(p_one, p_two)], [branch]])
        (away,) = weight_grad("gb_away", meta, 1, *products, 1024, extra=extra)
        sum_one = after(sum_one, away)
        away, u_come = sync(away, u_come)
        come = swap(away, "dp", 1)
        u_keep, u_away = halves_ctx(add_low(u_keep, u_come), 2)
        u_come = swap(u_away, "ctx", 2)
    else:
        u_come = ()
    (grad_in,) = dense(input_body, "input", meta, rows, tile, [p_one, p_two, sum_one], [], [qkv_w[:5] + (6,)], [(width, BF)], [])
    grad_in, come, u_come = sync(grad_in, come, u_come)
    grad_in = grad_in.reshape(per, n * blk, width)
    in_1 = trade(part_of(grad_in, 1, 1), 1)
    if tuned:
        u_half = add_low(u_keep, u_come)
        u_other = swap(u_half, "ctx", 2)
        b_sums = weight_grad("gb_keep", meta, 0, *products, 1024, come=come, extra=extra)
        b_sums, u_other, in_1, grad_in = sync(b_sums, u_other, in_1, grad_in)
    part_2, part_3 = part_of(grad_in, 2, 1), part_of(grad_in, 3, 1)
    in_2 = trade(part_2[:cut], 2)
    if tuned:
        b_far = send_far(b_sums)
        u_whole = join_ctx(u_half, u_other, 2)
        b_far, in_2, part_2, part_3, u_whole = sync(b_far, in_2, part_2, part_3, u_whole)
        b_near = send_near(b_sums, b_far)
        u_other = swap(u_whole, "ctx", 1)
    in_2b, in_3 = trade(part_2[cut:], 2), trade(part_3[:cut], 3)
    if tuned:
        b_near, in_2b, in_3, part_3, u_other = sync(b_near, in_2b, in_3, part_3, u_other)
        b_keep, b_away = halves_ctx(add_low(b_sums[0], *b_near), 1)
        b_come = swap(b_away, "ctx", 1)
    in_3b = trade(part_3[cut:], 3)
    in_rest = [(2, 0, in_2), (2, cut, in_2b), (3, 0, in_3), (3, cut, in_3b)]
    if tuned:
        b_come, in_3b = sync(b_come, in_3b)
        b_half = add_low(b_keep, b_come)
        g_up = join_ctx(u_whole, u_other, 1)
        total = whole_ctx(whole_ctx(halve_ctx(b_half, 2), 2), 1).astype(F32)
        g_qkv = total[:thin, : 3 * width]
        g_out = total[:thin, 3 * width :]
        g_up = g_up.astype(F32)
        g_down = g_down.astype(F32)
        vec = total[thin, :count]
    else:
        def whole(*products):
            return jnp.concatenate([tn(a, b).astype(BF) for a, b in products], axis=1)

        def total(grad):
            return lax.psum(reduce_any(grad).astype(F32), "ctx")

        g_down = total(whole((active, second)))
        g_up = total(whole((first_low, hidden)))
        g_out = total(whole((mixed, branch)))
        g_qkv = total(whole(*[(x, p[c]) for c in range(3) for p in (p_one, p_two)]))
        vec = lax.psum(lax.psum_scatter(vec, "dp", scatter_dimension=0, tiled=True), "ctx").reshape(-1)
    grads, pos = [], 0
    for size in sizes:
        grads.append(vec[pos : pos + size])
        pos += size
    g_bqv, g_bout, g_gone, g_sone, g_bup, g_bdown, g_gtwo, g_stwo = grads
    grad_input = put_slots([(0, 0, part_of(grad_in, 0, 1)), (1, 0, in_1)] + in_rest, per, F32)
    return (
        output, grad_input, g_qkv, g_bqv, g_out, g_bout, g_gone, g_sone, g_up, g_bup, g_down, g_bdown, g_gtwo, g_stwo,
    )


def solution(mesh):
    row = P("dp", "ctx", None)
    mat = P("dp", None)
    vec = P("dp")
    weights = (mat, vec, mat, vec, vec, vec, mat, vec, mat, vec, vec, vec)
    return jax.shard_map(
        shards, mesh=mesh, in_specs=(row, vec) + weights + (row,), out_specs=(row, row) + weights, check_vma=False
    )
```

```python
import functools

import jax
import jax.numpy as jnp
from jax import lax
from jax.experimental import pallas as pl
from jax.experimental.pallas import tpu as pltpu
from jax.sharding import PartitionSpec as P

HD = 64
GROUP = 4
NEG = -1e30
EPS = 1e-06
BF = jnp.bfloat16
F32 = jnp.float32
MIB = 1024 * 1024
COSTS = {'qkv': 13, 'out': 10, 'up': 23, 'down': 21, 'hidden': 18, 'first': 23, 'input': 14, 'attend': 24, 'attend_back': 21, 'gd_away': 11, 'gd_keep': 11, 'gu_away': 11, 'gu_keep': 11, 'gb_away': 14, 'gb_keep': 3, 'gc_away': 8, 'gc_keep': 8}


def cost(name):
    return pl.CostEstimate(flops=COSTS[name] * 1000000000, bytes_accessed=1000000, transcendentals=0)


ANY = pl.BlockSpec(memory_space=pl.ANY)


def swap(x, axis, bit):
    n = lax.axis_size(axis)
    return lax.ppermute(x, axis, [(i, i ^ bit) for i in range(n)])


def after(x, *others):
    return lax.optimization_barrier((x,) + others)[0]


def sync(*values):
    return lax.optimization_barrier(values)


def gather_near(own):
    if lax.axis_size("dp") != 8:
        return ()
    return swap(own, "dp", 2), swap(own, "dp", 4)


def gather_far(near):
    if not near:
        return ()
    cut = near[0].shape[0] // 32 * 16
    return swap(near[0][:cut], "dp", 4), swap(near[1][cut:], "dp", 2)


def gather_stack(own, near, far):
    if near:
        return jnp.stack([own, near[0], near[1], jnp.concatenate(far, axis=0)])
    mine = own[None]
    bit = 2
    while bit < lax.axis_size("dp"):
        mine = jnp.concatenate([mine, swap(mine, "dp", bit)])
        bit *= 2
    return mine


def add_low(*parts):
    total = parts[0].astype(F32)
    for part in parts[1:]:
        total = total + part.astype(F32)
    return total.astype(BF)


def reduce_any(grad):
    n = lax.axis_size("dp")
    me = lax.axis_index("dp")
    rows = grad.shape[0] // n
    width = grad.shape[1]

    def stack(odd):
        return jnp.stack(
            [lax.dynamic_slice(grad, ((me ^ (2 * k + odd)) * rows, 0), (rows, width)) for k in range(n // 2)]
        )

    mine = add_low(stack(0), swap(stack(1), "dp", 1))
    bit = n // 2
    while bit > 1:
        keep = mine.shape[0] // 2
        mine = add_low(mine[:keep], swap(mine[keep:], "dp", bit))
        bit //= 2
    return mine[0]


def send_far(sums):
    return swap(sums[3], "dp", 4), swap(sums[4], "dp", 2)


def send_near(sums, far):
    own, to_x, to_y = sums[:3]
    cut, width = far[0].shape[1], to_x.shape[1]
    to_x = add_low(to_x, jnp.pad(far[0], ((0, 0), (0, width - cut))))
    to_y = add_low(to_y, jnp.pad(far[1], ((0, 0), (cut, 0))))
    return swap(to_x, "dp", 2), swap(to_y, "dp", 4)


def halves_ctx(share, bit):
    half = share.shape[1] // 2
    mine = (lax.axis_index("ctx") // bit) % 2
    keep = lax.dynamic_slice_in_dim(share, mine * half, half, axis=1)
    return keep, lax.dynamic_slice_in_dim(share, (1 - mine) * half, half, axis=1)


def halve_ctx(share, bit):
    keep, away = halves_ctx(share, bit)
    return add_low(keep, swap(away, "ctx", bit))


def join_ctx(half, other, bit):
    low = (lax.axis_index("ctx") // bit) % 2 == 0
    return jnp.concatenate([jnp.where(low, half, other), jnp.where(low, other, half)], axis=1)


def whole_ctx(half, bit):
    return join_ctx(half, swap(half, "ctx", bit), bit)


def to_sequences(block):
    return lax.all_to_all(block, "ctx", 0, 0, tiled=True)


def part_of(block, j, axis=0):
    n = lax.axis_size("ctx")
    per = block.shape[axis] // n
    return lax.dynamic_slice_in_dim(block, (lax.axis_index("ctx") ^ j) * per, per, axis=axis)


def put_slots(pieces, per, out):
    for j, first, piece in pieces:
        start = (lax.axis_index("ctx") ^ j) * per + first
        out = lax.dynamic_update_slice_in_dim(out, piece.astype(out.dtype), start, axis=0)
    return out


def put_positions(pieces, per):
    n = lax.axis_size("ctx")
    blk, width = pieces[0][2].shape[1:]
    out = jnp.zeros((per, n * blk, width), pieces[0][2].dtype)
    for j, first, piece in pieces:
        out = lax.dynamic_update_slice(out, piece, (first, (lax.axis_index("ctx") ^ j) * blk, 0))
    return out


def trade(block, j):
    return swap(block, "ctx", j)


def nn(left, right):
    return jnp.dot(left, right, preferred_element_type=F32)


def nt(left, right):
    return lax.dot_general(left, right, (((1,), (1,)), ((), ())), preferred_element_type=F32)


def tn(left, right):
    return lax.dot_general(left, right, (((0,), (0,)), ((), ())), preferred_element_type=F32)


def fold(rows):
    return jnp.sum(rows.reshape(rows.shape[0] // 8, 8, rows.shape[1]), axis=0)


class Weight:
    def __init__(self, stacks, whole, sems, me, rows, first, pieces):
        self.whole, self.pieces = whole, pieces
        self.step = whole.shape[1] // max(pieces, 1)
        self.copies, self.starts = [], []
        for odd, stack in enumerate(stacks):
            count = stack.shape[0]
            for k in range(count):
                start = pl.multiple_of((me ^ (2 * k + odd)) * rows if len(stacks) == 2 else k * rows, rows)
                self.starts.append(pl.ds(start, rows))
                for p in range(max(pieces, 1)):
                    here, there = pl.ds(first + p * self.step, self.step), pl.ds(p * self.step, self.step)
                    copy = pltpu.make_async_copy(
                        stack.at[k, pl.ds(0, rows), here], whole.at[self.starts[-1], there], sems.at[odd * count + k, p]
                    )
                    self.copies.append((k * 2 + odd, p, copy))
        self.wait_for = False

    def start(self):
        for _, _, copy in sorted(self.copies, key=lambda c: c[1] if self.pieces else c[0]):
            copy.start()

    def cols(self, p):
        if self.wait_for:
            for _, q, copy in self.copies:
                if q == p:
                    copy.wait()
        return slice(p * self.step, (p + 1) * self.step)

    def rows(self, c):
        _, _, copy = self.copies[c]
        if self.wait_for:
            copy.wait()
        return self.starts[c]


def row_spec(tile, width):
    return pl.BlockSpec((tile, width), lambda i, *_: (i, 0))


def one_spec(height, width):
    return pl.BlockSpec((height, width), lambda i, *_: (0, 0))


def dense(body, name, meta, rows, tile, row_ins, vec_ins, weights, row_outs, sums):
    stacks, spans, scratch = [], [], []
    for mine, other, r, _, width, pieces in weights:
        held = [mine] if other is None else [mine, other]
        spans.append(slice(len(stacks), len(stacks) + len(held)))
        stacks += held
        count = mine.shape[0] * len(held)
        scratch.append(pltpu.VMEM((count * r, width), BF))
        scratch.append(pltpu.SemaphoreType.DMA((count, max(pieces, 1))))
    n_row, n_vec, n_stack = len(row_ins), len(vec_ins), len(stacks)
    n_out, n_sum = len(row_outs), len(sums)

    def kernel(meta_ref, *refs):
        pos = 0
        groups = []
        for count in (n_row, n_vec, n_stack, n_out, n_sum, 2 * len(weights)):
            groups.append(refs[pos : pos + count])
            pos += count
        row_refs, vec_refs, stack_refs, out_refs, sum_refs, scratch_refs = groups

        whole = [
            Weight(stack_refs[spans[w]], scratch_refs[2 * w], scratch_refs[2 * w + 1], meta_ref[0], weights[w][2], weights[w][3], weights[w][5])
            for w in range(len(weights))
        ]

        def work(wait_for):
            for weight in whole:
                weight.wait_for = wait_for
            body(meta_ref, row_refs, vec_refs, whole, out_refs, sum_refs)

        @pl.when(pl.program_id(0) == 0)
        def _():
            for weight in whole:
                weight.start()
            for ref in sum_refs:
                ref[...] = jnp.zeros_like(ref)
            work(True)

        @pl.when(pl.program_id(0) > 0)
        def _():
            work(False)

    in_specs = (
        [row_spec(tile, a.shape[-1]) if a.ndim == 2 else pl.BlockSpec((a.shape[0], tile, a.shape[2]), lambda i, *_: (0, i, 0)) for a in row_ins]
        + [one_spec(1, v.shape[1]) for v in vec_ins]
        + [ANY] * n_stack
    )
    out_specs = [row_spec(tile, w) for w, _ in row_outs] + [one_spec(8, w) for w in sums]
    out_shape = [jax.ShapeDtypeStruct((rows, w), d) for w, d in row_outs] + [
        jax.ShapeDtypeStruct((8, w), F32) for w in sums
    ]
    return pl.pallas_call(
        kernel,
        grid_spec=pltpu.PrefetchScalarGridSpec(
            num_scalar_prefetch=1,
            grid=(rows // tile,),
            in_specs=in_specs,
            out_specs=out_specs,
            scratch_shapes=scratch,
        ),
        out_shape=out_shape,
        compiler_params=pltpu.CompilerParams(vmem_limit_bytes=60 * MIB, dimension_semantics=("arbitrary",)),
        cost_estimate=cost(name),
        name=name,
    )(meta, *row_ins, *vec_ins, *stacks)


def by_columns(left, weight):
    parts = []
    for p in range(weight.pieces):
        cols = weight.cols(p)
        parts.append(nn(left[...], weight.whole[:, cols]))
    return jnp.concatenate(parts, axis=1)


def by_columns_turned(left, weight):
    total = None
    for p in range(weight.pieces):
        cols = weight.cols(p)
        part = nt(left[:, cols], weight.whole[:, cols])
        total = part if total is None else total + part
    return total


def by_shards(left, weight):
    if weight.pieces:
        return by_columns(left, weight)
    if not weight.wait_for:
        return nn(left[...], weight.whole[...])
    total = None
    for c in range(len(weight.copies)):
        here = weight.rows(c)
        part = nn(left[:, here], weight.whole[here, :])
        total = part if total is None else total + part
    return total


def qkv_body(meta, rows, vecs, whole, outs, sums):
    (x,) = rows
    (bias,) = vecs
    for p in range(whole[0].pieces):
        cols = whole[0].cols(p)
        outs[0][:, cols] = (nn(x[...], whole[0].whole[:, cols]) + bias[:, cols]).astype(BF)


def out_body(meta, rows, vecs, whole, outs, sums):
    mixed, x = rows
    bias, gain, shift = vecs
    total = x[...].astype(F32) + (by_columns(mixed, whole[0]) + bias[...])
    centre = total - jnp.mean(total, axis=-1, keepdims=True)
    inverse = lax.rsqrt(jnp.mean(centre * centre, axis=-1, keepdims=True) + EPS)
    normed = centre * inverse
    outs[0][...] = normed
    outs[1][...] = jnp.broadcast_to(inverse, outs[1].shape)
    outs[2][...] = (normed * gain[...] + shift[...]).astype(BF)


def up_body(meta, rows, vecs, whole, outs, sums):
    (low,) = rows
    (bias,) = vecs
    for p in range(whole[0].pieces):
        cols = whole[0].cols(p)
        hidden = nn(low[...], whole[0].whole[:, cols]) + bias[:, cols]
        cdf = 0.5 + 0.5 * lax.erf(hidden * 0.7071067811865476)
        pdf = jnp.exp(-0.5 * hidden * hidden) * 0.3989422804014327
        outs[0][:, cols] = (hidden * cdf).astype(BF)
        outs[1][:, cols] = (cdf + hidden * pdf).astype(BF)


def down_body(seq, per, meta, rows, vecs, whole, outs, sums):
    active, normed_one, cot = rows
    bias, gain_one, shift_one, gain, shift = vecs
    total = (normed_one[...] * gain_one[...] + shift_one[...]) + (by_shards(active, whole[0]) + bias[...])
    centre = total - jnp.mean(total, axis=-1, keepdims=True)
    inverse = lax.rsqrt(jnp.mean(centre * centre, axis=-1, keepdims=True) + EPS)
    normed = centre * inverse
    tile = total.shape[0]
    at = lax.broadcasted_iota(jnp.int32, (tile, 1), 0) + pl.program_id(0) * tile
    valid = jnp.zeros(at.shape, jnp.bool_)
    for s in range(per):
        valid = valid | ((at >= s * seq) & (at < s * seq + meta[2 + s]))
    keep = jnp.where(valid, 1.0, 0.0)
    outs[0][...] = ((normed * gain[...] + shift[...]) * keep).astype(BF)
    grad = cot[...].astype(F32) * keep
    sums[0][...] += fold(grad * normed)
    sums[1][...] += fold(grad)
    scaled = grad * gain[...]
    back = inverse * (
        scaled
        - jnp.mean(scaled, axis=-1, keepdims=True)
        - normed * jnp.mean(scaled * normed, axis=-1, keepdims=True)
    )
    low = back.astype(BF)
    outs[1][...] = back
    outs[2][...] = low
    sums[2][...] += fold(low.astype(F32))


def hidden_kernel(second, whole, deriv, out, total):
    low = (nt(second[...], whole[...]) * deriv[...].astype(F32)).astype(BF)
    out[...] = low
    total[...] = fold(low.astype(F32))


def hidden_grad(second, whole, deriv, step):
    rows, width = second.shape
    ff = whole.shape[0]
    cols = pl.BlockSpec((rows, step), lambda i: (0, i))
    return pl.pallas_call(
        hidden_kernel,
        grid=(ff // step,),
        in_specs=[pl.BlockSpec((rows, width), lambda i: (0, 0)), pl.BlockSpec((step, width), lambda i: (i, 0)), cols],
        out_specs=[cols, pl.BlockSpec((8, step), lambda i: (0, i))],
        out_shape=[jax.ShapeDtypeStruct((rows, ff), BF), jax.ShapeDtypeStruct((8, ff), F32)],
        compiler_params=pltpu.CompilerParams(vmem_limit_bytes=60 * MIB),
        cost_estimate=cost("hidden"),
        name="hidden",
    )(second, whole, deriv)


def first_body(meta, rows, vecs, whole, outs, sums):
    hidden, sum_two, normed, inverse = rows
    (gain,) = vecs
    grad = sum_two[...] + by_columns_turned(hidden, whole[0])
    n1 = normed[...]
    sums[0][...] += fold(grad * n1)
    sums[1][...] += fold(grad)
    scaled = grad * gain[...]
    back = inverse[:, 0:1] * (
        scaled - jnp.mean(scaled, axis=-1, keepdims=True) - n1 * jnp.mean(scaled * n1, axis=-1, keepdims=True)
    )
    low = back.astype(BF)
    outs[0][...] = back
    outs[1][...] = low
    sums[2][...] += fold(low.astype(F32))
    whole[1].cols(0)
    outs[2][...] = nt(low, whole[1].whole[...]).astype(BF)


def input_body(meta, rows, vecs, whole, outs, sums):
    sum_one = rows[-1]
    total = sum_one[...]
    parts = len(rows) - 1
    for p in range(whole[0].pieces):
        cols = whole[0].cols(p)
        total = total + nt(rows[p % parts][p // parts], whole[0].whole[:, cols])
    outs[0][...] = total.astype(BF)


def key_mask(meta, seq):
    at = lax.broadcasted_iota(jnp.int32, (seq, 1), 0)
    return at < meta[2 + pl.program_id(0)]


def attend_kernel(meta, q_ref, k_ref, v_ref, mixed_ref, lse_ref):
    seq, lanes = q_ref.shape
    ok = key_mask(meta, seq)
    q_all = q_ref[...] * BF(HD ** (-0.5))
    k_all, v_turned = k_ref[...], v_ref[...].T
    ones = jnp.ones((16, seq), BF)
    outs = []
    for h in range(lanes // HD):
        cols = slice(h * HD, (h + 1) * HD)
        scores = jnp.where(ok, nt(k_all[:, cols], q_all[:, cols]), NEG)
        peak = jnp.max(scores, axis=0, keepdims=True)
        weights = jnp.exp(scores - peak).astype(BF)
        both = nn(jnp.concatenate([v_turned[cols], ones], axis=0), weights)
        total = both[HD : HD + 1]
        lse_ref[h : h + 1, :] = peak + jnp.log(total)
        outs.append(both[:HD] * (1.0 / total))
    mixed_ref[...] = jnp.concatenate(outs, axis=0).T.astype(BF)


def attend_back_kernel(meta, q_ref, k_ref, v_ref, g_ref, mixed_ref, lse_ref, proj_ref, sum_ref):
    seq, lanes = q_ref.shape
    ok = key_mask(meta, seq)
    scale = HD ** (-0.5)
    q_all = q_ref[...] * BF(scale)
    k_all, v_all, g_all = k_ref[...], v_ref[...], g_ref[...]
    k_turned = k_all.T
    inners = (g_all.astype(F32) * mixed_ref[...].astype(F32)).T
    gq, gk, gv = [], [], []
    for h in range(lanes // HD):
        cols = slice(h * HD, (h + 1) * HD)
        q, k, v, g = q_all[:, cols], k_all[:, cols], v_all[:, cols], g_all[:, cols]
        exact = jnp.exp(jnp.where(ok, nt(k, q), NEG) - lse_ref[h : h + 1, :])
        inner = jnp.sum(inners[cols], axis=0, keepdims=True)
        low = (exact * (nt(v, g) - inner)).astype(BF)
        gq.append(nn(k_turned[cols], low) * scale)
        gk.append(nn(low, q))
        gv.append(nn(exact.astype(BF), g))
    wholes = (jnp.concatenate(gq, axis=0).T, jnp.concatenate(gk, axis=1), jnp.concatenate(gv, axis=1))
    for c, whole in enumerate(wholes):
        low = whole.astype(BF)
        proj_ref[c] = low
        sum_ref[c] = fold(low.astype(F32))


def attend(meta, proj, per, seq):
    lanes = GROUP * HD
    groups = proj.shape[-1] // 3 // lanes
    shaped = proj.reshape(per, seq, proj.shape[-1])

    def spec(c):
        return pl.BlockSpec((None, seq, lanes), lambda s, h, *_: (s, 0, c * groups + h))

    mixed, lse = pl.pallas_call(
        attend_kernel,
        grid_spec=pltpu.PrefetchScalarGridSpec(
            num_scalar_prefetch=1,
            grid=(per, groups),
            in_specs=[spec(0), spec(1), spec(2)],
            out_specs=[spec(0), pl.BlockSpec((None, None, GROUP, seq), lambda s, h, *_: (s, h, 0, 0))],
        ),
        out_shape=[
            jax.ShapeDtypeStruct((per, seq, groups * lanes), BF),
            jax.ShapeDtypeStruct((per, groups, GROUP, seq), F32),
        ],
        compiler_params=pltpu.CompilerParams(vmem_limit_bytes=60 * MIB),
        cost_estimate=cost("attend"),
        name="attend",
    )(meta, shaped, shaped, shaped)
    return mixed.reshape(per * seq, -1), lse


def attend_back(meta, proj, grad, mixed, lse, per, seq, first, count):
    width = proj.shape[-1] // 3
    lanes = GROUP * HD
    groups = width // lanes
    shaped = proj.reshape(per, seq, proj.shape[-1])

    def spec(c):
        return pl.BlockSpec((None, seq, lanes), lambda s, h, *_: (s, 0, c * groups + first + h))

    out, sums = pl.pallas_call(
        attend_back_kernel,
        grid_spec=pltpu.PrefetchScalarGridSpec(
            num_scalar_prefetch=1,
            grid=(per, count),
            in_specs=[spec(0), spec(1), spec(2), spec(0), spec(0)]
            + [pl.BlockSpec((None, None, GROUP, seq), lambda s, h, *_: (s, first + h, 0, 0))],
            out_specs=[
                pl.BlockSpec((3, None, seq, lanes), lambda s, h, *_: (0, s, 0, h)),
                pl.BlockSpec((3, None, 8, lanes), lambda s, h, *_: (0, s, 0, h)),
            ],
        ),
        out_shape=[
            jax.ShapeDtypeStruct((3, per, seq, count * lanes), BF),
            jax.ShapeDtypeStruct((3, per, 8, count * lanes), F32),
        ],
        compiler_params=pltpu.CompilerParams(vmem_limit_bytes=60 * MIB),
        cost_estimate=cost("attend_back"),
        name="attend_back",
    )(meta, shaped, shaped, shaped, grad.reshape(per, seq, width), mixed.reshape(per, seq, width), lse)
    return out.reshape(3, per * seq, count * lanes), sums


def line_kernel(*refs):
    one, two, *eights, out = refs
    part = one.shape[-1]
    pos = 0
    for c in (0, 2):
        for ref in (one, two):
            out[:, pos : pos + part] = jnp.sum(jnp.sum(ref[c], axis=0), axis=0, keepdims=True).astype(out.dtype)
            pos += part
    for ref in eights:
        width = ref.shape[1]
        out[:, pos : pos + width] = jnp.sum(ref[...], axis=0, keepdims=True).astype(out.dtype)
        pos += width


def one_line(one, two, eights, dtype):
    total = 4 * one.shape[-1] + sum(b.shape[1] for b in eights)
    return pl.pallas_call(
        line_kernel,
        out_shape=jax.ShapeDtypeStruct((1, total), dtype),
        compiler_params=pltpu.CompilerParams(vmem_limit_bytes=16 * MIB),
        name="line",
    )(one, two, *eights)[0]


def weight_grad(name, meta, odd, lefts, rights, chunk, come=None, extra=None):
    rows = lefts[0].shape[0]
    tall = lefts[0].shape[1] // 8

    def count(right):
        return right[0].shape[0] if isinstance(right, tuple) else right.shape[1] // chunk

    flat = [r for group in rights for r in group]
    owners = [li for li, group in enumerate(rights) for _ in group]
    firsts, steps = [], 0
    for right in flat:
        firsts.append(steps)
        steps += count(right)
    spread = [(i, r) for i, right in enumerate(flat) for r in (right if isinstance(right, tuple) else (right,))]
    below = 0 if extra is None else extra.shape[1]
    cut = (steps + 1) // 2
    n_left = len(lefts)

    def kernel(meta_ref, *refs):
        left_refs = refs[: 4 * n_left]
        pos = 4 * n_left
        right_refs = [[] for _ in flat]
        for i, _ in spread:
            right_refs[i].append(refs[pos])
            pos += 1
        extra_refs = refs[pos : pos + 4] if below else ()
        pos += len(extra_refs)
        come_ref = refs[pos] if come is not None else None
        pos += come is not None
        outs = refs[pos:]
        c = pl.program_id(0)

        def store(lefts_here, right):
            joined = tn(jnp.concatenate([left[...] for left in lefts_here], axis=1), right) if tall < 256 else None
            for k in range(4):
                part = tn(lefts_here[k][...], right) if joined is None else joined[k * tall : (k + 1) * tall]
                if come is None:
                    outs[0][k, 0:tall, :] = part.astype(BF)
                    if below:
                        outs[0][k, tall:, :] = extra_refs[k][...]
                    continue
                part = (part + come_ref[k, 0:tall, :].astype(F32)).astype(BF)
                if below:
                    low = (extra_refs[k][...].astype(F32) + come_ref[k, tall:, :].astype(F32)).astype(BF)
                if k < 3:
                    outs[k][0:tall, :] = part
                    if below:
                        outs[k][tall:, :] = low
                    continue

                @pl.when(c < cut)
                def _():
                    outs[3][0:tall, :] = part
                    if below:
                        outs[3][tall:, :] = low

                @pl.when(c >= cut)
                def _():
                    outs[4][0:tall, :] = part
                    if below:
                        outs[4][tall:, :] = low

        for i in range(len(flat)):
            last = firsts[i + 1] if i + 1 < len(flat) else steps
            li = owners[i]

            @pl.when((c >= firsts[i]) & (c < last))
            def _(i=i, li=li):
                store(left_refs[4 * li : 4 * li + 4], jnp.concatenate([r[...] for r in right_refs[i]], axis=1))

    def left_spec(k):
        return pl.BlockSpec((rows, tall), lambda c, m: (0, m[0] ^ (2 * k + odd)))

    def right_spec(i, right):
        last = (firsts[i + 1] if i + 1 < len(flat) else steps) - 1

        def place(c):
            return jnp.clip(c, firsts[i], last) - firsts[i]

        if right.ndim == 3:
            return pl.BlockSpec((None, rows, right.shape[2]), lambda c, m: (place(c), 0, 0))
        return pl.BlockSpec((rows, chunk), lambda c, m: (0, place(c)))

    def extra_spec(k):
        return pl.BlockSpec((None, below, chunk), lambda c, m: (m[0] ^ (2 * k + odd), 0, c))

    high = tall + below
    four = pl.BlockSpec((4, high, chunk), lambda c, m: (0, 0, c))
    in_specs = [left_spec(k) for _ in lefts for k in range(4)] + [right_spec(i, r) for i, r in spread]
    args = [left for left in lefts for _ in range(4)] + [r for _, r in spread]
    if below:
        in_specs += [extra_spec(k) for k in range(4)]
        args += [extra] * 4
    if come is None:
        out_specs = [four]
        out_shape = [jax.ShapeDtypeStruct((4, high, steps * chunk), BF)]
    else:
        in_specs.append(four)
        args.append(come)
        out_specs = [pl.BlockSpec((high, chunk), lambda c, m: (0, c))] * 3 + [
            pl.BlockSpec((high, chunk), lambda c, m: (0, jnp.minimum(c, cut - 1))),
            pl.BlockSpec((high, chunk), lambda c, m: (0, jnp.maximum(c - cut, 0))),
        ]
        out_shape = [jax.ShapeDtypeStruct((high, steps * chunk), BF)] * 3 + [
            jax.ShapeDtypeStruct((high, cut * chunk), BF),
            jax.ShapeDtypeStruct((high, (steps - cut) * chunk), BF),
        ]
    return pl.pallas_call(
        kernel,
        grid_spec=pltpu.PrefetchScalarGridSpec(
            num_scalar_prefetch=1,
            grid=(steps,),
            in_specs=in_specs,
            out_specs=out_specs,
        ),
        out_shape=out_shape,
        compiler_params=pltpu.CompilerParams(vmem_limit_bytes=60 * MIB),
        cost_estimate=cost(name),
        name=name,
    )(meta, *args)


def shards(
    tokens, lengths, w_qkv, bias_qv, w_out, bias_out, gain_one, shift_one,
    w_up, bias_up, w_down, bias_down, gain_two, shift_two, cotangent,
):
    seqs, blk, width = tokens.shape
    n = lax.axis_size("ctx")
    ndp = lax.axis_size("dp")
    me = lax.axis_index("dp")
    place = lax.axis_index("ctx")
    per = seqs // n
    rows = seqs * blk
    tile = per * blk
    ff = w_up.shape[1]
    thin = w_qkv.shape[0]
    tuned = ndp == 8
    half = width // (GROUP * HD) // 2
    cut = (per + 1) // 2

    own = lax.dynamic_slice_in_dim(lengths, place * per, per)
    meta = jnp.concatenate([jnp.stack([me, place]).astype(jnp.int32), own])

    vectors = (bias_qv, bias_out, gain_one, shift_one, bias_up, bias_down, gain_two, shift_two)
    sizes = [v.shape[0] for v in vectors]
    count = sum(sizes)
    line = jnp.pad(jnp.concatenate(vectors).reshape(1, count), ((0, 15), (0, 3 * width - count)))
    qkv_own = jnp.concatenate([w_qkv, line])
    mid_own = jnp.concatenate([w_out, w_up], axis=1)
    shared = tokens.reshape(n, per, blk, width)
    x = jnp.swapaxes(to_sequences(shared), 0, 1).reshape(rows, width)
    qkv_near = gather_near(qkv_own)
    mid_near = gather_near(mid_own)
    cot_parts = [part_of(cotangent, j) for j in range(n)]
    blank = jnp.zeros((seqs, blk, width), BF)
    x, qkv_near, mid_near, cot_parts, blank, meta = sync(x, qkv_near, mid_near, cot_parts, blank, meta)
    qkv_far = gather_far(qkv_near)
    qkv_mine = gather_stack(qkv_own, qkv_near, qkv_far)
    qkv_other = swap(qkv_mine, "dp", 1)
    mid_far = gather_far(mid_near)
    cot_1 = trade(cot_parts[1], 1)

    lines = qkv_mine[:, thin, :count]
    both = jnp.concatenate([lines, swap(lines, "dp", 1)])
    index = jnp.arange(ndp, dtype=jnp.int32) ^ me
    packed = jnp.take(both, (index >> 1) + (index & 1) * (ndp // 2), axis=0).astype(F32)
    fulls, pos = [], 0
    for size in sizes:
        fulls.append(packed[:, pos : pos + size].reshape(1, ndp * size))
        pos += size
    bqv, bout, gone, sone, bup, bdown, gtwo, stwo = fulls
    bqkv = jnp.concatenate([bqv[:, :width], jnp.zeros((1, width), F32), bqv[:, width:]], axis=1)

    qkv_w = (qkv_mine, qkv_other, thin, 0, 3 * width, 3)
    (proj,) = dense(qkv_body, "qkv", meta, rows, tile, [x], [bqkv], [qkv_w], [(3 * width, BF)], [])
    proj, mid_far, cot_1, w_down, cot_parts = sync(proj, mid_far, cot_1, w_down, cot_parts)
    mid_mine = gather_stack(mid_own, mid_near, mid_far)
    mid_other = swap(mid_mine, "dp", 1)
    down_all = lax.all_gather(w_down, "dp", axis=0, tiled=True)
    cot_2 = trade(cot_parts[2], 2)
    mixed, lse = attend(meta, proj, per, n * blk)
    mixed, mid_other, cot_2 = sync(mixed, mid_other, cot_2)
    out_w = (mid_mine, mid_other, thin, 0, width, 2)
    up_w = (mid_mine, mid_other, thin, width, ff, 8)
    normed_one, inverse_one, first_low = dense(
        out_body, "out", meta, rows, tile, [mixed, x], [bout, gone, sone], [out_w], [(width, F32), (128, F32), (width, BF)], []
    )
    first_low, cot_parts = sync(first_low, cot_parts)
    cot_3 = trade(cot_parts[3], 3)
    active, deriv = dense(up_body, "up", meta, rows, tile, [first_low], [bup], [up_w], [(ff, BF), (ff, BF)], [])
    active, down_all, cot_3 = sync(active, down_all, cot_3)
    down_w = (down_all.reshape(8, ff // 8, width), None, ff // 8, 0, width, 0)
    cot = put_positions([(0, 0, cot_parts[0]), (1, 0, cot_1), (2, 0, cot_2), (3, 0, cot_3)], per).reshape(rows, width)
    out_parts, sum_two, second, s_gtwo, s_stwo, s_bdown = dense(
        functools.partial(down_body, n * blk, per), "down", meta, rows, tile, [active, normed_one, cot],
        [bdown, gone, sone, gtwo, stwo], [down_w], [(width, BF), (width, F32), (width, BF)], [width] * 3,
    )
    out_parts = out_parts.reshape(per, n * blk, width)
    out_own = part_of(out_parts, 0, 1)
    out_1 = trade(part_of(out_parts, 1, 1), 1)

    come = ()
    if tuned:
        (away,) = weight_grad("gd_away", meta, 1, [active], [[second]], 512)
        come = swap(away, "dp", 1)
        second = after(second, away)
    hidden, s_bup = hidden_grad(second, down_all, deriv, 1024)
    hidden, come, out_1, out_parts = sync(hidden, come, out_1, out_parts)
    part = part_of(out_parts, 2, 1)
    out_2 = trade(part[:cut], 2)
    d_far, d_near = (), ()
    if tuned:
        d_sums = weight_grad("gd_keep", meta, 0, [active], [[second]], 512, come=come)
        d_far = send_far(d_sums)
        hidden, out_2, part = sync(after(hidden, d_sums[0]), out_2, part)
    out_2b = trade(part[cut:], 2)
    if tuned:
        (away,) = weight_grad("gu_away", meta, 1, [first_low], [[hidden]], 1024)
        hidden = after(hidden, away)
        away, d_far, out_2b = sync(away, d_far, out_2b)
        come = swap(away, "dp", 1)
    hidden, d_far, out_2b, out_parts = sync(hidden, d_far, out_2b, out_parts)
    if tuned:
        d_near = send_near(d_sums, d_far)
    out_3 = trade(part_of(out_parts, 3, 1), 3)
    sum_one, branch, g_mixed, s_gone, s_sone, s_bout = dense(
        first_body, "first", meta, rows, tile, [hidden, sum_two, normed_one, inverse_one], [gone], [up_w[:5] + (4,), out_w[:5] + (1,)],
        [(width, F32), (width, BF), (width, BF)], [width] * 3,
    )
    branch, g_mixed, come, d_near, out_3 = sync(branch, g_mixed, come, d_near, out_3)
    output = put_slots([(0, 0, out_own), (1, 0, out_1), (2, 0, out_2), (2, cut, out_2b), (3, 0, out_3)], per, blank)
    u_far = ()
    if tuned:
        d_share = add_low(d_sums[0], *d_near)
        g_down = lax.psum(d_share, "ctx")
        u_sums = weight_grad("gu_keep", meta, 0, [first_low], [[hidden]], 1024, come=come)
        u_far = send_far(u_sums)
        g_mixed = after(g_mixed, u_sums[0])
    p_one, s_one = attend_back(meta, proj, g_mixed, mixed, lse, per, n * blk, 0, half)
    p_one, g_mixed, u_far = sync(p_one, g_mixed, u_far)
    u_near = ()
    if tuned:
        u_near = send_near(u_sums, u_far)
    p_two, s_two = attend_back(meta, proj, g_mixed, mixed, lse, per, n * blk, half, half)
    if tuned:
        p_two, u_near = sync(p_two, u_near)

    eights = (s_bout, s_gone, s_sone, s_bup, s_bdown, s_gtwo, s_stwo)
    p_two, s_one, s_two, eights = sync(p_two, s_one, s_two, eights)
    vec = one_line(s_one, s_two, eights, BF if tuned else F32)
    places, pos = [], 0
    for size in sizes:
        places.append(vec[pos : pos + ndp * size])
        pos += ndp * size
    vec = places
    vec = jnp.concatenate([v.reshape(ndp, -1) for v in vec], axis=1)

    come = ()
    if tuned:
        u_keep, u_away = halves_ctx(add_low(u_sums[0], *u_near), 1)
        u_come = swap(u_away, "ctx", 1)
        extra = jnp.pad(vec[:, None, :].astype(BF), ((0, 0), (0, 15), (0, 4 * width - count)))
        products = ([x, mixed], [[(p_one, p_two)], [branch]])
        (away,) = weight_grad("gb_away", meta, 1, *products, 1024, extra=extra)
        sum_one = after(sum_one, away)
        away, u_come, g_down = sync(away, u_come, g_down)
        come = swap(away, "dp", 1)
        u_keep, u_away = halves_ctx(add_low(u_keep, u_come), 2)
        u_come = swap(u_away, "ctx", 2)
    else:
        u_come = ()
    (grad_in,) = dense(input_body, "input", meta, rows, tile, [p_one, p_two, sum_one], [], [qkv_w[:5] + (6,)], [(width, BF)], [])
    grad_in, come, u_come = sync(grad_in, come, u_come)
    grad_in = grad_in.reshape(per, n * blk, width)
    in_1 = trade(part_of(grad_in, 1, 1), 1)
    if tuned:
        u_half = add_low(u_keep, u_come)
        u_other = swap(u_half, "ctx", 2)
        b_sums = weight_grad("gb_keep", meta, 0, *products, 1024, come=come, extra=extra)
        b_sums, u_other, in_1, grad_in = sync(b_sums, u_other, in_1, grad_in)
    part_2, part_3 = part_of(grad_in, 2, 1), part_of(grad_in, 3, 1)
    in_2 = trade(part_2[:cut], 2)
    if tuned:
        b_far = send_far(b_sums)
        u_whole = join_ctx(u_half, u_other, 2)
        b_far, in_2, part_2, part_3, u_whole = sync(b_far, in_2, part_2, part_3, u_whole)
        b_near = send_near(b_sums, b_far)
        u_other = swap(u_whole, "ctx", 1)
    in_2b, in_3 = trade(part_2[cut:], 2), trade(part_3[:cut], 3)
    if tuned:
        b_near, in_2b, in_3, part_3, u_other = sync(b_near, in_2b, in_3, part_3, u_other)
        b_keep, b_away = halves_ctx(add_low(b_sums[0], *b_near), 1)
        b_come = swap(b_away, "ctx", 1)
    in_3b = trade(part_3[cut:], 3)
    in_rest = [(2, 0, in_2), (2, cut, in_2b), (3, 0, in_3), (3, cut, in_3b)]
    if tuned:
        b_come, in_3b = sync(b_come, in_3b)
        b_half = add_low(b_keep, b_come)
        g_up = join_ctx(u_whole, u_other, 1)
        b_half = whole_ctx(halve_ctx(b_half, 2), 2)
        b_other = swap(b_half, "ctx", 1)
        low = place % 2 == 0
        left = jnp.where(low, b_half, b_other).astype(F32)
        right = jnp.where(low, b_other, b_half).astype(F32)
        g_qkv = jnp.concatenate([left[:thin], right[:thin, :width]], axis=1)
        g_out = right[:thin, width:]
        g_up = g_up.astype(F32)
        g_down = g_down.astype(F32)
        vec = left[thin, :count]
    else:
        def whole(*products):
            return jnp.concatenate([tn(a, b).astype(BF) for a, b in products], axis=1)

        def total(grad):
            return lax.psum(reduce_any(grad).astype(F32), "ctx")

        g_down = total(whole((active, second)))
        g_up = total(whole((first_low, hidden)))
        g_out = total(whole((mixed, branch)))
        g_qkv = total(whole(*[(x, p[c]) for c in range(3) for p in (p_one, p_two)]))
        vec = lax.psum(lax.psum_scatter(vec, "dp", scatter_dimension=0, tiled=True), "ctx").reshape(-1)
    grads, pos = [], 0
    for size in sizes:
        grads.append(vec[pos : pos + size])
        pos += size
    g_bqv, g_bout, g_gone, g_sone, g_bup, g_bdown, g_gtwo, g_stwo = grads
    grad_input = put_slots([(0, 0, part_of(grad_in, 0, 1)), (1, 0, in_1)] + in_rest, per, jnp.zeros((seqs, blk, width), F32))
    return (
        output, grad_input, g_qkv, g_bqv, g_out, g_bout, g_gone, g_sone, g_up, g_bup, g_down, g_bdown, g_gtwo, g_stwo,
    )


def solution(mesh):
    row = P("dp", "ctx", None)
    mat = P("dp", None)
    vec = P("dp")
    weights = (mat, vec, mat, vec, vec, vec, mat, vec, mat, vec, vec, vec)
    return jax.shard_map(
        shards, mesh=mesh, in_specs=(row, vec) + weights + (row,), out_specs=(row, row) + weights, check_vma=False
    )
```

```python
import functools

import jax
import jax.numpy as jnp
from jax import lax
from jax.experimental import pallas as pl
from jax.experimental.pallas import tpu as pltpu
from jax.sharding import PartitionSpec as P

HD = 64
GROUP = 4
NEG = -1e30
EPS = 1e-06
BF = jnp.bfloat16
F32 = jnp.float32
MIB = 1024 * 1024
COSTS = {'qkv': 13, 'out': 10, 'up': 23, 'down': 21, 'hidden': 18, 'first': 23, 'input': 14, 'attend': 24, 'attend_back': 21, 'gd_away': 11, 'gd_keep': 11, 'gu_away': 11, 'gu_keep': 11, 'gb_away': 14, 'gb_keep': 3, 'gc_away': 8, 'gc_keep': 8}


def cost(name):
    return pl.CostEstimate(flops=COSTS[name] * 1000000000, bytes_accessed=1000000, transcendentals=0)


ANY = pl.BlockSpec(memory_space=pl.ANY)


def swap(x, axis, bit):
    n = lax.axis_size(axis)
    return lax.ppermute(x, axis, [(i, i ^ bit) for i in range(n)])


def after(x, *others):
    return lax.optimization_barrier((x,) + others)[0]


def sync(*values):
    return lax.optimization_barrier(values)


def gather_near(own):
    if lax.axis_size("dp") != 8:
        return ()
    return swap(own, "dp", 2), swap(own, "dp", 4)


def gather_far(near):
    if not near:
        return ()
    cut = near[0].shape[0] // 32 * 16
    return swap(near[0][:cut], "dp", 4), swap(near[1][cut:], "dp", 2)


def gather_stack(own, near, far):
    if near:
        return jnp.stack([own, near[0], near[1], jnp.concatenate(far, axis=0)])
    mine = own[None]
    bit = 2
    while bit < lax.axis_size("dp"):
        mine = jnp.concatenate([mine, swap(mine, "dp", bit)])
        bit *= 2
    return mine


def add_low(*parts):
    total = parts[0].astype(F32)
    for part in parts[1:]:
        total = total + part.astype(F32)
    return total.astype(BF)


def reduce_any(grad):
    n = lax.axis_size("dp")
    me = lax.axis_index("dp")
    rows = grad.shape[0] // n
    width = grad.shape[1]

    def stack(odd):
        return jnp.stack(
            [lax.dynamic_slice(grad, ((me ^ (2 * k + odd)) * rows, 0), (rows, width)) for k in range(n // 2)]
        )

    mine = add_low(stack(0), swap(stack(1), "dp", 1))
    bit = n // 2
    while bit > 1:
        keep = mine.shape[0] // 2
        mine = add_low(mine[:keep], swap(mine[keep:], "dp", bit))
        bit //= 2
    return mine[0]


def send_far(sums):
    return swap(sums[3], "dp", 4), swap(sums[4], "dp", 2)


def send_near(sums, far):
    own, to_x, to_y = sums[:3]
    cut, width = far[0].shape[1], to_x.shape[1]
    to_x = add_low(to_x, jnp.pad(far[0], ((0, 0), (0, width - cut))))
    to_y = add_low(to_y, jnp.pad(far[1], ((0, 0), (cut, 0))))
    return swap(to_x, "dp", 2), swap(to_y, "dp", 4)


def halves_ctx(share, bit):
    half = share.shape[1] // 2
    mine = (lax.axis_index("ctx") // bit) % 2
    keep = lax.dynamic_slice_in_dim(share, mine * half, half, axis=1)
    return keep, lax.dynamic_slice_in_dim(share, (1 - mine) * half, half, axis=1)


def halve_ctx(share, bit):
    keep, away = halves_ctx(share, bit)
    return add_low(keep, swap(away, "ctx", bit))


def join_ctx(half, other, bit):
    low = (lax.axis_index("ctx") // bit) % 2 == 0
    return jnp.concatenate([jnp.where(low, half, other), jnp.where(low, other, half)], axis=1)


def whole_ctx(half, bit):
    return join_ctx(half, swap(half, "ctx", bit), bit)


def to_sequences(block):
    return lax.all_to_all(block, "ctx", 0, 0, tiled=True)


def part_of(block, j, axis=0):
    n = lax.axis_size("ctx")
    per = block.shape[axis] // n
    return lax.dynamic_slice_in_dim(block, (lax.axis_index("ctx") ^ j) * per, per, axis=axis)


def put_slots(pieces, per, out):
    for j, first, piece in pieces:
        start = (lax.axis_index("ctx") ^ j) * per + first
        out = lax.dynamic_update_slice_in_dim(out, piece.astype(out.dtype), start, axis=0)
    return out


def put_positions(pieces, per):
    n = lax.axis_size("ctx")
    blk, width = pieces[0][2].shape[1:]
    out = jnp.zeros((per, n * blk, width), pieces[0][2].dtype)
    for j, first, piece in pieces:
        out = lax.dynamic_update_slice(out, piece, (first, (lax.axis_index("ctx") ^ j) * blk, 0))
    return out


def trade(block, j):
    return swap(block, "ctx", j)


def nn(left, right):
    return jnp.dot(left, right, preferred_element_type=F32)


def nt(left, right):
    return lax.dot_general(left, right, (((1,), (1,)), ((), ())), preferred_element_type=F32)


def tn(left, right):
    return lax.dot_general(left, right, (((0,), (0,)), ((), ())), preferred_element_type=F32)


def fold(rows):
    return jnp.sum(rows.reshape(rows.shape[0] // 8, 8, rows.shape[1]), axis=0)


class Weight:
    def __init__(self, stacks, whole, sems, me, rows, first, pieces):
        self.whole, self.pieces = whole, pieces
        self.step = whole.shape[1] // max(pieces, 1)
        self.copies, self.starts = [], []
        for odd, stack in enumerate(stacks):
            count = stack.shape[0]
            for k in range(count):
                start = pl.multiple_of((me ^ (2 * k + odd)) * rows if len(stacks) == 2 else k * rows, rows)
                self.starts.append(pl.ds(start, rows))
                for p in range(max(pieces, 1)):
                    here, there = pl.ds(first + p * self.step, self.step), pl.ds(p * self.step, self.step)
                    copy = pltpu.make_async_copy(
                        stack.at[k, pl.ds(0, rows), here], whole.at[self.starts[-1], there], sems.at[odd * count + k, p]
                    )
                    self.copies.append((k * 2 + odd, p, copy))
        self.wait_for = False

    def start(self):
        for _, _, copy in sorted(self.copies, key=lambda c: c[1] if self.pieces else c[0]):
            copy.start()

    def cols(self, p):
        if self.wait_for:
            for _, q, copy in self.copies:
                if q == p:
                    copy.wait()
        return slice(p * self.step, (p + 1) * self.step)

    def rows(self, c):
        _, _, copy = self.copies[c]
        if self.wait_for:
            copy.wait()
        return self.starts[c]


def row_spec(tile, width):
    return pl.BlockSpec((tile, width), lambda i, *_: (i, 0))


def one_spec(height, width):
    return pl.BlockSpec((height, width), lambda i, *_: (0, 0))


def dense(body, name, meta, rows, tile, row_ins, vec_ins, weights, row_outs, sums):
    stacks, spans, scratch = [], [], []
    for mine, other, r, _, width, pieces in weights:
        held = [mine] if other is None else [mine, other]
        spans.append(slice(len(stacks), len(stacks) + len(held)))
        stacks += held
        count = mine.shape[0] * len(held)
        scratch.append(pltpu.VMEM((count * r, width), BF))
        scratch.append(pltpu.SemaphoreType.DMA((count, max(pieces, 1))))
    n_row, n_vec, n_stack = len(row_ins), len(vec_ins), len(stacks)
    n_out, n_sum = len(row_outs), len(sums)

    def kernel(meta_ref, *refs):
        pos = 0
        groups = []
        for count in (n_row, n_vec, n_stack, n_out, n_sum, 2 * len(weights)):
            groups.append(refs[pos : pos + count])
            pos += count
        row_refs, vec_refs, stack_refs, out_refs, sum_refs, scratch_refs = groups

        whole = [
            Weight(stack_refs[spans[w]], scratch_refs[2 * w], scratch_refs[2 * w + 1], meta_ref[0], weights[w][2], weights[w][3], weights[w][5])
            for w in range(len(weights))
        ]

        def work(wait_for):
            for weight in whole:
                weight.wait_for = wait_for
            body(meta_ref, row_refs, vec_refs, whole, out_refs, sum_refs)

        @pl.when(pl.program_id(0) == 0)
        def _():
            for weight in whole:
                weight.start()
            for ref in sum_refs:
                ref[...] = jnp.zeros_like(ref)
            work(True)

        @pl.when(pl.program_id(0) > 0)
        def _():
            work(False)

    in_specs = (
        [row_spec(tile, a.shape[-1]) if a.ndim == 2 else pl.BlockSpec((a.shape[0], tile, a.shape[2]), lambda i, *_: (0, i, 0)) for a in row_ins]
        + [one_spec(1, v.shape[1]) for v in vec_ins]
        + [ANY] * n_stack
    )
    out_specs = [row_spec(tile, w) for w, _ in row_outs] + [one_spec(8, w) for w in sums]
    out_shape = [jax.ShapeDtypeStruct((rows, w), d) for w, d in row_outs] + [
        jax.ShapeDtypeStruct((8, w), F32) for w in sums
    ]
    return pl.pallas_call(
        kernel,
        grid_spec=pltpu.PrefetchScalarGridSpec(
            num_scalar_prefetch=1,
            grid=(rows // tile,),
            in_specs=in_specs,
            out_specs=out_specs,
            scratch_shapes=scratch,
        ),
        out_shape=out_shape,
        compiler_params=pltpu.CompilerParams(vmem_limit_bytes=60 * MIB, dimension_semantics=("arbitrary",)),
        cost_estimate=cost(name),
        name=name,
    )(meta, *row_ins, *vec_ins, *stacks)


def by_columns(left, weight):
    parts = []
    for p in range(weight.pieces):
        cols = weight.cols(p)
        parts.append(nn(left[...], weight.whole[:, cols]))
    return jnp.concatenate(parts, axis=1)


def by_columns_turned(left, weight):
    total = None
    for p in range(weight.pieces):
        cols = weight.cols(p)
        part = nt(left[:, cols], weight.whole[:, cols])
        total = part if total is None else total + part
    return total


def by_shards(left, weight):
    if weight.pieces:
        return by_columns(left, weight)
    if not weight.wait_for:
        return nn(left[...], weight.whole[...])
    total = None
    for c in range(len(weight.copies)):
        here = weight.rows(c)
        part = nn(left[:, here], weight.whole[here, :])
        total = part if total is None else total + part
    return total


def qkv_body(meta, rows, vecs, whole, outs, sums):
    (x,) = rows
    (bias,) = vecs
    for p in range(whole[0].pieces):
        cols = whole[0].cols(p)
        outs[0][:, cols] = (nn(x[...], whole[0].whole[:, cols]) + bias[:, cols]).astype(BF)


def out_body(meta, rows, vecs, whole, outs, sums):
    mixed, x = rows
    bias, gain, shift = vecs
    total = x[...].astype(F32) + (by_columns(mixed, whole[0]) + bias[...])
    centre = total - jnp.mean(total, axis=-1, keepdims=True)
    inverse = lax.rsqrt(jnp.mean(centre * centre, axis=-1, keepdims=True) + EPS)
    normed = centre * inverse
    outs[0][...] = normed
    outs[1][...] = jnp.broadcast_to(inverse, outs[1].shape)
    outs[2][...] = (normed * gain[...] + shift[...]).astype(BF)


def up_body(meta, rows, vecs, whole, outs, sums):
    (low,) = rows
    (bias,) = vecs
    for p in range(whole[0].pieces):
        cols = whole[0].cols(p)
        hidden = nn(low[...], whole[0].whole[:, cols]) + bias[:, cols]
        cdf = 0.5 + 0.5 * lax.erf(hidden * 0.7071067811865476)
        pdf = jnp.exp(-0.5 * hidden * hidden) * 0.3989422804014327
        outs[0][:, cols] = (hidden * cdf).astype(BF)
        outs[1][:, cols] = (cdf + hidden * pdf).astype(BF)


def down_body(seq, per, meta, rows, vecs, whole, outs, sums):
    active, normed_one, cot = rows
    bias, gain_one, shift_one, gain, shift = vecs
    total = (normed_one[...] * gain_one[...] + shift_one[...]) + (by_shards(active, whole[0]) + bias[...])
    centre = total - jnp.mean(total, axis=-1, keepdims=True)
    inverse = lax.rsqrt(jnp.mean(centre * centre, axis=-1, keepdims=True) + EPS)
    normed = centre * inverse
    tile = total.shape[0]
    at = lax.broadcasted_iota(jnp.int32, (tile, 1), 0) + pl.program_id(0) * tile
    valid = jnp.zeros(at.shape, jnp.bool_)
    for s in range(per):
        valid = valid | ((at >= s * seq) & (at < s * seq + meta[2 + s]))
    keep = jnp.where(valid, 1.0, 0.0)
    outs[0][...] = ((normed * gain[...] + shift[...]) * keep).astype(BF)
    grad = cot[...].astype(F32) * keep
    sums[0][...] += fold(grad * normed)
    sums[1][...] += fold(grad)
    scaled = grad * gain[...]
    back = inverse * (
        scaled
        - jnp.mean(scaled, axis=-1, keepdims=True)
        - normed * jnp.mean(scaled * normed, axis=-1, keepdims=True)
    )
    low = back.astype(BF)
    outs[1][...] = back
    outs[2][...] = low
    sums[2][...] += fold(low.astype(F32))


def hidden_kernel(second, whole, deriv, out, total):
    low = (nt(second[...], whole[...]) * deriv[...].astype(F32)).astype(BF)
    out[...] = low
    total[...] = fold(low.astype(F32))


def hidden_grad(second, whole, deriv, step):
    rows, width = second.shape
    ff = whole.shape[0]
    cols = pl.BlockSpec((rows, step), lambda i: (0, i))
    return pl.pallas_call(
        hidden_kernel,
        grid=(ff // step,),
        in_specs=[pl.BlockSpec((rows, width), lambda i: (0, 0)), pl.BlockSpec((step, width), lambda i: (i, 0)), cols],
        out_specs=[cols, pl.BlockSpec((8, step), lambda i: (0, i))],
        out_shape=[jax.ShapeDtypeStruct((rows, ff), BF), jax.ShapeDtypeStruct((8, ff), F32)],
        compiler_params=pltpu.CompilerParams(vmem_limit_bytes=60 * MIB),
        cost_estimate=cost("hidden"),
        name="hidden",
    )(second, whole, deriv)


def first_body(meta, rows, vecs, whole, outs, sums):
    hidden, sum_two, normed, inverse = rows
    (gain,) = vecs
    grad = sum_two[...] + by_columns_turned(hidden, whole[0])
    n1 = normed[...]
    sums[0][...] += fold(grad * n1)
    sums[1][...] += fold(grad)
    scaled = grad * gain[...]
    back = inverse[:, 0:1] * (
        scaled - jnp.mean(scaled, axis=-1, keepdims=True) - n1 * jnp.mean(scaled * n1, axis=-1, keepdims=True)
    )
    low = back.astype(BF)
    outs[0][...] = back
    outs[1][...] = low
    sums[2][...] += fold(low.astype(F32))
    whole[1].cols(0)
    outs[2][...] = nt(low, whole[1].whole[...]).astype(BF)


def input_body(meta, rows, vecs, whole, outs, sums):
    sum_one = rows[-1]
    total = sum_one[...]
    parts = len(rows) - 1
    for p in range(whole[0].pieces):
        cols = whole[0].cols(p)
        total = total + nt(rows[p % parts][p // parts], whole[0].whole[:, cols])
    outs[0][...] = total.astype(BF)


def key_mask(meta, seq):
    at = lax.broadcasted_iota(jnp.int32, (seq, 1), 0)
    return at < meta[2 + pl.program_id(0)]


def attend_kernel(meta, q_ref, k_ref, v_ref, mixed_ref, lse_ref):
    seq, lanes = q_ref.shape
    ok = key_mask(meta, seq)
    q_all = q_ref[...] * BF(HD ** (-0.5))
    k_all, v_turned = k_ref[...], v_ref[...].T
    ones = jnp.ones((16, seq), BF)
    outs = []
    for h in range(lanes // HD):
        cols = slice(h * HD, (h + 1) * HD)
        scores = jnp.where(ok, nt(k_all[:, cols], q_all[:, cols]), NEG)
        peak = jnp.max(scores, axis=0, keepdims=True)
        weights = jnp.exp(scores - peak).astype(BF)
        both = nn(jnp.concatenate([v_turned[cols], ones], axis=0), weights)
        total = both[HD : HD + 1]
        lse_ref[h : h + 1, :] = peak + jnp.log(total)
        outs.append(both[:HD] * (1.0 / total))
    mixed_ref[...] = jnp.concatenate(outs, axis=0).T.astype(BF)


def attend_back_kernel(meta, q_ref, k_ref, v_ref, g_ref, mixed_ref, lse_ref, proj_ref, sum_ref):
    seq, lanes = q_ref.shape
    ok = key_mask(meta, seq)
    scale = HD ** (-0.5)
    q_all = q_ref[...] * BF(scale)
    k_all, v_all, g_all = k_ref[...], v_ref[...], g_ref[...]
    k_turned = k_all.T
    inners = (g_all.astype(F32) * mixed_ref[...].astype(F32)).T
    gq, gk, gv = [], [], []
    for h in range(lanes // HD):
        cols = slice(h * HD, (h + 1) * HD)
        q, k, v, g = q_all[:, cols], k_all[:, cols], v_all[:, cols], g_all[:, cols]
        exact = jnp.exp(jnp.where(ok, nt(k, q), NEG) - lse_ref[h : h + 1, :])
        inner = jnp.sum(inners[cols], axis=0, keepdims=True)
        low = (exact * (nt(v, g) - inner)).astype(BF)
        gq.append(nn(k_turned[cols], low) * scale)
        gk.append(nn(low, q))
        gv.append(nn(exact.astype(BF), g))
    wholes = (jnp.concatenate(gq, axis=0).T, jnp.concatenate(gk, axis=1), jnp.concatenate(gv, axis=1))
    for c, whole in enumerate(wholes):
        low = whole.astype(BF)
        proj_ref[c] = low
        sum_ref[c] = fold(low.astype(F32))


def attend(meta, proj, per, seq):
    lanes = GROUP * HD
    groups = proj.shape[-1] // 3 // lanes
    shaped = proj.reshape(per, seq, proj.shape[-1])

    def spec(c):
        return pl.BlockSpec((None, seq, lanes), lambda s, h, *_: (s, 0, c * groups + h))

    mixed, lse = pl.pallas_call(
        attend_kernel,
        grid_spec=pltpu.PrefetchScalarGridSpec(
            num_scalar_prefetch=1,
            grid=(per, groups),
            in_specs=[spec(0), spec(1), spec(2)],
            out_specs=[spec(0), pl.BlockSpec((None, None, GROUP, seq), lambda s, h, *_: (s, h, 0, 0))],
        ),
        out_shape=[
            jax.ShapeDtypeStruct((per, seq, groups * lanes), BF),
            jax.ShapeDtypeStruct((per, groups, GROUP, seq), F32),
        ],
        compiler_params=pltpu.CompilerParams(vmem_limit_bytes=60 * MIB),
        cost_estimate=cost("attend"),
        name="attend",
    )(meta, shaped, shaped, shaped)
    return mixed.reshape(per * seq, -1), lse


def attend_back(meta, proj, grad, mixed, lse, per, seq, first, count):
    width = proj.shape[-1] // 3
    lanes = GROUP * HD
    groups = width // lanes
    shaped = proj.reshape(per, seq, proj.shape[-1])

    def spec(c):
        return pl.BlockSpec((None, seq, lanes), lambda s, h, *_: (s, 0, c * groups + first + h))

    out, sums = pl.pallas_call(
        attend_back_kernel,
        grid_spec=pltpu.PrefetchScalarGridSpec(
            num_scalar_prefetch=1,
            grid=(per, count),
            in_specs=[spec(0), spec(1), spec(2), spec(0), spec(0)]
            + [pl.BlockSpec((None, None, GROUP, seq), lambda s, h, *_: (s, first + h, 0, 0))],
            out_specs=[
                pl.BlockSpec((3, None, seq, lanes), lambda s, h, *_: (0, s, 0, h)),
                pl.BlockSpec((3, None, 8, lanes), lambda s, h, *_: (0, s, 0, h)),
            ],
        ),
        out_shape=[
            jax.ShapeDtypeStruct((3, per, seq, count * lanes), BF),
            jax.ShapeDtypeStruct((3, per, 8, count * lanes), F32),
        ],
        compiler_params=pltpu.CompilerParams(vmem_limit_bytes=60 * MIB),
        cost_estimate=cost("attend_back"),
        name="attend_back",
    )(meta, shaped, shaped, shaped, grad.reshape(per, seq, width), mixed.reshape(per, seq, width), lse)
    return out.reshape(3, per * seq, count * lanes), sums


def line_kernel(*refs):
    one, two, *eights, out = refs
    part = one.shape[-1]
    pos = 0
    for c in (0, 2):
        for ref in (one, two):
            out[:, pos : pos + part] = jnp.sum(jnp.sum(ref[c], axis=0), axis=0, keepdims=True)
            pos += part
    for ref in eights:
        width = ref.shape[1]
        out[:, pos : pos + width] = jnp.sum(ref[...], axis=0, keepdims=True)
        pos += width


def one_line(one, two, eights):
    total = 4 * one.shape[-1] + sum(b.shape[1] for b in eights)
    return pl.pallas_call(
        line_kernel,
        out_shape=jax.ShapeDtypeStruct((1, total), F32),
        compiler_params=pltpu.CompilerParams(vmem_limit_bytes=16 * MIB),
        name="line",
    )(one, two, *eights)[0]


def weight_grad(name, meta, odd, lefts, rights, chunk, come=None, extra=None):
    rows = lefts[0].shape[0]
    tall = lefts[0].shape[1] // 8

    def count(right):
        return right[0].shape[0] if isinstance(right, tuple) else right.shape[1] // chunk

    flat = [r for group in rights for r in group]
    owners = [li for li, group in enumerate(rights) for _ in group]
    firsts, steps = [], 0
    for right in flat:
        firsts.append(steps)
        steps += count(right)
    spread = [(i, r) for i, right in enumerate(flat) for r in (right if isinstance(right, tuple) else (right,))]
    below = 0 if extra is None else extra.shape[1]
    cut = (steps + 1) // 2
    n_left = len(lefts)

    def kernel(meta_ref, *refs):
        left_refs = refs[: 4 * n_left]
        pos = 4 * n_left
        right_refs = [[] for _ in flat]
        for i, _ in spread:
            right_refs[i].append(refs[pos])
            pos += 1
        extra_refs = refs[pos : pos + 4] if below else ()
        pos += len(extra_refs)
        come_ref = refs[pos] if come is not None else None
        pos += come is not None
        outs = refs[pos:]
        c = pl.program_id(0)

        def store(lefts_here, right):
            joined = tn(jnp.concatenate([left[...] for left in lefts_here], axis=1), right) if tall < 256 else None
            for k in range(4):
                part = tn(lefts_here[k][...], right) if joined is None else joined[k * tall : (k + 1) * tall]
                if come is None:
                    outs[0][k, 0:tall, :] = part.astype(BF)
                    if below:
                        outs[0][k, tall:, :] = extra_refs[k][...]
                    continue
                part = (part + come_ref[k, 0:tall, :].astype(F32)).astype(BF)
                if below:
                    low = (extra_refs[k][...].astype(F32) + come_ref[k, tall:, :].astype(F32)).astype(BF)
                if k < 3:
                    outs[k][0:tall, :] = part
                    if below:
                        outs[k][tall:, :] = low
                    continue

                @pl.when(c < cut)
                def _():
                    outs[3][0:tall, :] = part
                    if below:
                        outs[3][tall:, :] = low

                @pl.when(c >= cut)
                def _():
                    outs[4][0:tall, :] = part
                    if below:
                        outs[4][tall:, :] = low

        for i in range(len(flat)):
            last = firsts[i + 1] if i + 1 < len(flat) else steps
            li = owners[i]

            @pl.when((c >= firsts[i]) & (c < last))
            def _(i=i, li=li):
                store(left_refs[4 * li : 4 * li + 4], jnp.concatenate([r[...] for r in right_refs[i]], axis=1))

    def left_spec(k):
        return pl.BlockSpec((rows, tall), lambda c, m: (0, m[0] ^ (2 * k + odd)))

    def right_spec(i, right):
        last = (firsts[i + 1] if i + 1 < len(flat) else steps) - 1

        def place(c):
            return jnp.clip(c, firsts[i], last) - firsts[i]

        if right.ndim == 3:
            return pl.BlockSpec((None, rows, right.shape[2]), lambda c, m: (place(c), 0, 0))
        return pl.BlockSpec((rows, chunk), lambda c, m: (0, place(c)))

    def extra_spec(k):
        return pl.BlockSpec((None, below, chunk), lambda c, m: (m[0] ^ (2 * k + odd), 0, c))

    high = tall + below
    four = pl.BlockSpec((4, high, chunk), lambda c, m: (0, 0, c))
    in_specs = [left_spec(k) for _ in lefts for k in range(4)] + [right_spec(i, r) for i, r in spread]
    args = [left for left in lefts for _ in range(4)] + [r for _, r in spread]
    if below:
        in_specs += [extra_spec(k) for k in range(4)]
        args += [extra] * 4
    if come is None:
        out_specs = [four]
        out_shape = [jax.ShapeDtypeStruct((4, high, steps * chunk), BF)]
    else:
        in_specs.append(four)
        args.append(come)
        out_specs = [pl.BlockSpec((high, chunk), lambda c, m: (0, c))] * 3 + [
            pl.BlockSpec((high, chunk), lambda c, m: (0, jnp.minimum(c, cut - 1))),
            pl.BlockSpec((high, chunk), lambda c, m: (0, jnp.maximum(c - cut, 0))),
        ]
        out_shape = [jax.ShapeDtypeStruct((high, steps * chunk), BF)] * 3 + [
            jax.ShapeDtypeStruct((high, cut * chunk), BF),
            jax.ShapeDtypeStruct((high, (steps - cut) * chunk), BF),
        ]
    return pl.pallas_call(
        kernel,
        grid_spec=pltpu.PrefetchScalarGridSpec(
            num_scalar_prefetch=1,
            grid=(steps,),
            in_specs=in_specs,
            out_specs=out_specs,
        ),
        out_shape=out_shape,
        compiler_params=pltpu.CompilerParams(vmem_limit_bytes=60 * MIB),
        cost_estimate=cost(name),
        name=name,
    )(meta, *args)


def shards(
    tokens, lengths, w_qkv, bias_qv, w_out, bias_out, gain_one, shift_one,
    w_up, bias_up, w_down, bias_down, gain_two, shift_two, cotangent,
):
    seqs, blk, width = tokens.shape
    n = lax.axis_size("ctx")
    ndp = lax.axis_size("dp")
    me = lax.axis_index("dp")
    place = lax.axis_index("ctx")
    per = seqs // n
    rows = seqs * blk
    tile = per * blk
    ff = w_up.shape[1]
    thin = w_qkv.shape[0]
    tuned = ndp == 8
    half = width // (GROUP * HD) // 2
    cut = (per + 1) // 2

    own = lax.dynamic_slice_in_dim(lengths, place * per, per)
    meta = jnp.concatenate([jnp.stack([me, place]).astype(jnp.int32), own])

    vectors = (bias_qv, bias_out, gain_one, shift_one, bias_up, bias_down, gain_two, shift_two)
    sizes = [v.shape[0] for v in vectors]
    count = sum(sizes)
    line = jnp.pad(jnp.concatenate(vectors).reshape(1, count), ((0, 15), (0, 3 * width - count)))
    qkv_own = jnp.concatenate([w_qkv, line])
    mid_own = jnp.concatenate([w_out, w_up], axis=1)
    shared = tokens.reshape(n, per, blk, width)
    x = jnp.swapaxes(to_sequences(shared), 0, 1).reshape(rows, width)
    qkv_near = gather_near(qkv_own)
    mid_near = gather_near(mid_own)
    cot_parts = [part_of(cotangent, j) for j in range(n)]
    blank = jnp.zeros((seqs, blk, width), BF)
    x, qkv_near, mid_near, cot_parts, blank, meta = sync(x, qkv_near, mid_near, cot_parts, blank, meta)
    qkv_far = gather_far(qkv_near)
    qkv_mine = gather_stack(qkv_own, qkv_near, qkv_far)
    qkv_other = swap(qkv_mine, "dp", 1)
    mid_far = gather_far(mid_near)
    cot_1 = trade(cot_parts[1], 1)

    lines = qkv_mine[:, thin, :count]
    both = jnp.concatenate([lines, swap(lines, "dp", 1)])
    index = jnp.arange(ndp, dtype=jnp.int32) ^ me
    packed = jnp.take(both, (index >> 1) + (index & 1) * (ndp // 2), axis=0).astype(F32)
    fulls, pos = [], 0
    for size in sizes:
        fulls.append(packed[:, pos : pos + size].reshape(1, ndp * size))
        pos += size
    bqv, bout, gone, sone, bup, bdown, gtwo, stwo = fulls
    bqkv = jnp.concatenate([bqv[:, :width], jnp.zeros((1, width), F32), bqv[:, width:]], axis=1)

    qkv_w = (qkv_mine, qkv_other, thin, 0, 3 * width, 3)
    (proj,) = dense(qkv_body, "qkv", meta, rows, tile, [x], [bqkv], [qkv_w], [(3 * width, BF)], [])
    proj, mid_far, cot_1, w_down, cot_parts = sync(proj, mid_far, cot_1, w_down, cot_parts)
    mid_mine = gather_stack(mid_own, mid_near, mid_far)
    mid_other = swap(mid_mine, "dp", 1)
    down_all = lax.all_gather(w_down, "dp", axis=0, tiled=True)
    cot_2 = trade(cot_parts[2], 2)
    mixed, lse = attend(meta, proj, per, n * blk)
    mixed, mid_other, cot_2 = sync(mixed, mid_other, cot_2)
    out_w = (mid_mine, mid_other, thin, 0, width, 2)
    up_w = (mid_mine, mid_other, thin, width, ff, 8)
    normed_one, inverse_one, first_low = dense(
        out_body, "out", meta, rows, tile, [mixed, x], [bout, gone, sone], [out_w], [(width, F32), (128, F32), (width, BF)], []
    )
    first_low, cot_parts = sync(first_low, cot_parts)
    cot_3 = trade(cot_parts[3], 3)
    active, deriv = dense(up_body, "up", meta, rows, tile, [first_low], [bup], [up_w], [(ff, BF), (ff, BF)], [])
    active, down_all, cot_3 = sync(active, down_all, cot_3)
    down_w = (down_all.reshape(8, ff // 8, width), None, ff // 8, 0, width, 0)
    cot = put_positions([(0, 0, cot_parts[0]), (1, 0, cot_1), (2, 0, cot_2), (3, 0, cot_3)], per).reshape(rows, width)
    out_parts, sum_two, second, s_gtwo, s_stwo, s_bdown = dense(
        functools.partial(down_body, n * blk, per), "down", meta, rows, tile, [active, normed_one, cot],
        [bdown, gone, sone, gtwo, stwo], [down_w], [(width, BF), (width, F32), (width, BF)], [width] * 3,
    )
    out_parts = out_parts.reshape(per, n * blk, width)
    out_own = part_of(out_parts, 0, 1)
    out_1 = trade(part_of(out_parts, 1, 1), 1)

    come = ()
    if tuned:
        (away,) = weight_grad("gd_away", meta, 1, [active], [[second]], 512)
        come = swap(away, "dp", 1)
        second = after(second, away)
    hidden, s_bup = hidden_grad(second, down_all, deriv, 1024)
    hidden, come, out_1, out_parts = sync(hidden, come, out_1, out_parts)
    part = part_of(out_parts, 2, 1)
    out_2 = trade(part[:cut], 2)
    d_far, d_near = (), ()
    if tuned:
        d_sums = weight_grad("gd_keep", meta, 0, [active], [[second]], 512, come=come)
        d_far = send_far(d_sums)
        hidden, out_2, part = sync(after(hidden, d_sums[0]), out_2, part)
    out_2b = trade(part[cut:], 2)
    if tuned:
        (away,) = weight_grad("gu_away", meta, 1, [first_low], [[hidden]], 1024)
        hidden = after(hidden, away)
        away, d_far, out_2b = sync(away, d_far, out_2b)
        come = swap(away, "dp", 1)
    hidden, d_far, out_2b, out_parts = sync(hidden, d_far, out_2b, out_parts)
    if tuned:
        d_near = send_near(d_sums, d_far)
    out_3 = trade(part_of(out_parts, 3, 1), 3)
    sum_one, branch, g_mixed, s_gone, s_sone, s_bout = dense(
        first_body, "first", meta, rows, tile, [hidden, sum_two, normed_one, inverse_one], [gone], [up_w[:5] + (4,), out_w[:5] + (1,)],
        [(width, F32), (width, BF), (width, BF)], [width] * 3,
    )
    branch, g_mixed, come, d_near, out_3 = sync(branch, g_mixed, come, d_near, out_3)
    output = put_slots([(0, 0, out_own), (1, 0, out_1), (2, 0, out_2), (2, cut, out_2b), (3, 0, out_3)], per, blank)
    u_far = ()
    if tuned:
        d_share = add_low(d_sums[0], *d_near)
        g_down = lax.psum(d_share, "ctx")
        u_sums = weight_grad("gu_keep", meta, 0, [first_low], [[hidden]], 1024, come=come)
        u_far = send_far(u_sums)
        g_mixed = after(g_mixed, u_sums[0])
    p_one, s_one = attend_back(meta, proj, g_mixed, mixed, lse, per, n * blk, 0, half)
    p_one, g_mixed, u_far = sync(p_one, g_mixed, u_far)
    u_near = ()
    if tuned:
        u_near = send_near(u_sums, u_far)
    p_two, s_two = attend_back(meta, proj, g_mixed, mixed, lse, per, n * blk, half, half)
    if tuned:
        p_two, u_near = sync(p_two, u_near)

    eights = (s_bout, s_gone, s_sone, s_bup, s_bdown, s_gtwo, s_stwo)
    p_two, s_one, s_two, eights = sync(p_two, s_one, s_two, eights)
    vec = one_line(s_one, s_two, eights)
    places, pos = [], 0
    for size in sizes:
        places.append(vec[pos : pos + ndp * size])
        pos += ndp * size
    vec = places
    vec = jnp.concatenate([v.reshape(ndp, -1) for v in vec], axis=1)

    come = ()
    if tuned:
        u_keep, u_away = halves_ctx(add_low(u_sums[0], *u_near), 1)
        u_come = swap(u_away, "ctx", 1)
        extra = jnp.pad(vec[:, None, :].astype(BF), ((0, 0), (0, 15), (0, 4 * width - count)))
        products = ([x, mixed], [[(p_one, p_two)], [branch]])
        (away,) = weight_grad("gb_away", meta, 1, *products, 1024, extra=extra)
        sum_one = after(sum_one, away)
        away, u_come, g_down = sync(away, u_come, g_down)
        come = swap(away, "dp", 1)
        u_keep, u_away = halves_ctx(add_low(u_keep, u_come), 2)
        u_come = swap(u_away, "ctx", 2)
    else:
        u_come = ()
    (grad_in,) = dense(input_body, "input", meta, rows, tile, [p_one, p_two, sum_one], [], [qkv_w[:5] + (6,)], [(width, BF)], [])
    grad_in, come, u_come = sync(grad_in, come, u_come)
    grad_in = grad_in.reshape(per, n * blk, width)
    in_1 = trade(part_of(grad_in, 1, 1), 1)
    if tuned:
        u_half = add_low(u_keep, u_come)
        u_other = swap(u_half, "ctx", 2)
        b_sums = weight_grad("gb_keep", meta, 0, *products, 1024, come=come, extra=extra)
        b_sums, u_other, in_1, grad_in = sync(b_sums, u_other, in_1, grad_in)
    part_2, part_3 = part_of(grad_in, 2, 1), part_of(grad_in, 3, 1)
    in_2 = trade(part_2[:cut], 2)
    if tuned:
        b_far = send_far(b_sums)
        u_whole = join_ctx(u_half, u_other, 2)
        b_far, in_2, part_2, part_3, u_whole = sync(b_far, in_2, part_2, part_3, u_whole)
        b_near = send_near(b_sums, b_far)
        u_other = swap(u_whole, "ctx", 1)
    in_2b, in_3 = trade(part_2[cut:], 2), trade(part_3[:cut], 3)
    if tuned:
        b_near, in_2b, in_3, part_3, u_other = sync(b_near, in_2b, in_3, part_3, u_other)
        b_keep, b_away = halves_ctx(add_low(b_sums[0], *b_near), 1)
        b_come = swap(b_away, "ctx", 1)
    in_3b = trade(part_3[cut:], 3)
    in_rest = [(2, 0, in_2), (2, cut, in_2b), (3, 0, in_3), (3, cut, in_3b)]
    if tuned:
        b_come, in_3b = sync(b_come, in_3b)
        b_half = add_low(b_keep, b_come)
        g_up = join_ctx(u_whole, u_other, 1)
        b_half = whole_ctx(halve_ctx(b_half, 2), 2)
        b_other = swap(b_half, "ctx", 1)
        low = place % 2 == 0
        left = jnp.where(low, b_half, b_other).astype(F32)
        right = jnp.where(low, b_other, b_half).astype(F32)
        g_qkv = jnp.concatenate([left[:thin], right[:thin, :width]], axis=1)
        g_out = right[:thin, width:]
        g_up = g_up.astype(F32)
        g_down = g_down.astype(F32)
        vec = left[thin, :count]
    else:
        def whole(*products):
            return jnp.concatenate([tn(a, b).astype(BF) for a, b in products], axis=1)

        def total(grad):
            return lax.psum(reduce_any(grad).astype(F32), "ctx")

        g_down = total(whole((active, second)))
        g_up = total(whole((first_low, hidden)))
        g_out = total(whole((mixed, branch)))
        g_qkv = total(whole(*[(x, p[c]) for c in range(3) for p in (p_one, p_two)]))
        vec = lax.psum(lax.psum_scatter(vec, "dp", scatter_dimension=0, tiled=True), "ctx").reshape(-1)
    grads, pos = [], 0
    for size in sizes:
        grads.append(vec[pos : pos + size])
        pos += size
    g_bqv, g_bout, g_gone, g_sone, g_bup, g_bdown, g_gtwo, g_stwo = grads
    grad_input = put_slots([(0, 0, part_of(grad_in, 0, 1)), (1, 0, in_1)] + in_rest, per, jnp.zeros((seqs, blk, width), F32))
    return (
        output, grad_input, g_qkv, g_bqv, g_out, g_bout, g_gone, g_sone, g_up, g_bup, g_down, g_bdown, g_gtwo, g_stwo,
    )


def solution(mesh):
    row = P("dp", "ctx", None)
    mat = P("dp", None)
    vec = P("dp")
    weights = (mat, vec, mat, vec, vec, vec, mat, vec, mat, vec, vec, vec)
    return jax.shard_map(
        shards, mesh=mesh, in_specs=(row, vec) + weights + (row,), out_specs=(row, row) + weights, check_vma=False
    )
```

```python
import functools

import jax
import jax.numpy as jnp
from jax import lax
from jax.experimental import pallas as pl
from jax.experimental.pallas import tpu as pltpu
from jax.sharding import PartitionSpec as P

HD = 64
GROUP = 4
NEG = -1e30
EPS = 1e-06
BF = jnp.bfloat16
F32 = jnp.float32
MIB = 1024 * 1024
COSTS = {'qkv': 13, 'out': 10, 'up': 23, 'down': 21, 'hidden': 18, 'first': 23, 'input': 14, 'attend': 24, 'attend_back': 21, 'gd_away': 11, 'gd_keep': 11, 'gu_away': 11, 'gu_keep': 11, 'gb_away': 14, 'gb_keep': 3, 'gc_away': 8, 'gc_keep': 8}


def cost(name):
    return pl.CostEstimate(flops=COSTS[name] * 1000000000, bytes_accessed=1000000, transcendentals=0)


ANY = pl.BlockSpec(memory_space=pl.ANY)


def swap(x, axis, bit):
    n = lax.axis_size(axis)
    return lax.ppermute(x, axis, [(i, i ^ bit) for i in range(n)])


def after(x, *others):
    return lax.optimization_barrier((x,) + others)[0]


def sync(*values):
    return lax.optimization_barrier(values)


def gather_near(own):
    if lax.axis_size("dp") != 8:
        return ()
    return swap(own, "dp", 2), swap(own, "dp", 4)


def gather_far(near):
    if not near:
        return ()
    cut = near[0].shape[0] // 32 * 16
    return swap(near[0][:cut], "dp", 4), swap(near[1][cut:], "dp", 2)


def gather_stack(own, near, far):
    if near:
        return jnp.stack([own, near[0], near[1], jnp.concatenate(far, axis=0)])
    mine = own[None]
    bit = 2
    while bit < lax.axis_size("dp"):
        mine = jnp.concatenate([mine, swap(mine, "dp", bit)])
        bit *= 2
    return mine


def add_low(*parts):
    total = parts[0].astype(F32)
    for part in parts[1:]:
        total = total + part.astype(F32)
    return total.astype(BF)


def reduce_any(grad):
    n = lax.axis_size("dp")
    me = lax.axis_index("dp")
    rows = grad.shape[0] // n
    width = grad.shape[1]

    def stack(odd):
        return jnp.stack(
            [lax.dynamic_slice(grad, ((me ^ (2 * k + odd)) * rows, 0), (rows, width)) for k in range(n // 2)]
        )

    mine = add_low(stack(0), swap(stack(1), "dp", 1))
    bit = n // 2
    while bit > 1:
        keep = mine.shape[0] // 2
        mine = add_low(mine[:keep], swap(mine[keep:], "dp", bit))
        bit //= 2
    return mine[0]


def send_far(sums):
    return swap(sums[3], "dp", 4), swap(sums[4], "dp", 2)


def send_near(sums, far):
    own, to_x, to_y = sums[:3]
    cut, width = far[0].shape[1], to_x.shape[1]
    to_x = add_low(to_x, jnp.pad(far[0], ((0, 0), (0, width - cut))))
    to_y = add_low(to_y, jnp.pad(far[1], ((0, 0), (cut, 0))))
    return swap(to_x, "dp", 2), swap(to_y, "dp", 4)


def halves_ctx(share, bit):
    half = share.shape[1] // 2
    mine = (lax.axis_index("ctx") // bit) % 2
    keep = lax.dynamic_slice_in_dim(share, mine * half, half, axis=1)
    return keep, lax.dynamic_slice_in_dim(share, (1 - mine) * half, half, axis=1)


def halve_ctx(share, bit):
    keep, away = halves_ctx(share, bit)
    return add_low(keep, swap(away, "ctx", bit))


def join_ctx(half, other, bit):
    low = (lax.axis_index("ctx") // bit) % 2 == 0
    return jnp.concatenate([jnp.where(low, half, other), jnp.where(low, other, half)], axis=1)


def whole_ctx(half, bit):
    return join_ctx(half, swap(half, "ctx", bit), bit)


def to_sequences(block):
    return lax.all_to_all(block, "ctx", 0, 0, tiled=True)


def part_of(block, j, axis=0):
    n = lax.axis_size("ctx")
    per = block.shape[axis] // n
    return lax.dynamic_slice_in_dim(block, (lax.axis_index("ctx") ^ j) * per, per, axis=axis)


def put_slots(pieces, per, out):
    for j, first, piece in pieces:
        start = (lax.axis_index("ctx") ^ j) * per + first
        out = lax.dynamic_update_slice_in_dim(out, piece.astype(out.dtype), start, axis=0)
    return out


def put_positions(pieces, per):
    n = lax.axis_size("ctx")
    blk, width = pieces[0][2].shape[1:]
    out = jnp.zeros((per, n * blk, width), pieces[0][2].dtype)
    for j, first, piece in pieces:
        out = lax.dynamic_update_slice(out, piece, (first, (lax.axis_index("ctx") ^ j) * blk, 0))
    return out


def trade(block, j):
    return swap(block, "ctx", j)


def nn(left, right):
    return jnp.dot(left, right, preferred_element_type=F32)


def nt(left, right):
    return lax.dot_general(left, right, (((1,), (1,)), ((), ())), preferred_element_type=F32)


def tn(left, right):
    return lax.dot_general(left, right, (((0,), (0,)), ((), ())), preferred_element_type=F32)


def fold(rows):
    return jnp.sum(rows.reshape(rows.shape[0] // 8, 8, rows.shape[1]), axis=0)


class Weight:
    def __init__(self, stacks, whole, sems, me, rows, first, pieces):
        self.whole, self.pieces = whole, pieces
        self.step = whole.shape[1] // max(pieces, 1)
        self.copies, self.starts = [], []
        for odd, stack in enumerate(stacks):
            count = stack.shape[0]
            for k in range(count):
                start = pl.multiple_of((me ^ (2 * k + odd)) * rows if len(stacks) == 2 else k * rows, rows)
                self.starts.append(pl.ds(start, rows))
                for p in range(max(pieces, 1)):
                    here, there = pl.ds(first + p * self.step, self.step), pl.ds(p * self.step, self.step)
                    copy = pltpu.make_async_copy(
                        stack.at[k, pl.ds(0, rows), here], whole.at[self.starts[-1], there], sems.at[odd * count + k, p]
                    )
                    self.copies.append((k * 2 + odd, p, copy))
        self.wait_for = False

    def start(self):
        for _, _, copy in sorted(self.copies, key=lambda c: c[1] if self.pieces else c[0]):
            copy.start()

    def cols(self, p):
        if self.wait_for:
            for _, q, copy in self.copies:
                if q == p:
                    copy.wait()
        return slice(p * self.step, (p + 1) * self.step)

    def rows(self, c):
        _, _, copy = self.copies[c]
        if self.wait_for:
            copy.wait()
        return self.starts[c]


def row_spec(tile, width):
    return pl.BlockSpec((tile, width), lambda i, *_: (i, 0))


def one_spec(height, width):
    return pl.BlockSpec((height, width), lambda i, *_: (0, 0))


def dense(body, name, meta, rows, tile, row_ins, vec_ins, weights, row_outs, sums):
    stacks, spans, scratch = [], [], []
    for mine, other, r, _, width, pieces in weights:
        held = [mine] if other is None else [mine, other]
        spans.append(slice(len(stacks), len(stacks) + len(held)))
        stacks += held
        count = mine.shape[0] * len(held)
        scratch.append(pltpu.VMEM((count * r, width), BF))
        scratch.append(pltpu.SemaphoreType.DMA((count, max(pieces, 1))))
    n_row, n_vec, n_stack = len(row_ins), len(vec_ins), len(stacks)
    n_out, n_sum = len(row_outs), len(sums)

    def kernel(meta_ref, *refs):
        pos = 0
        groups = []
        for count in (n_row, n_vec, n_stack, n_out, n_sum, 2 * len(weights)):
            groups.append(refs[pos : pos + count])
            pos += count
        row_refs, vec_refs, stack_refs, out_refs, sum_refs, scratch_refs = groups

        whole = [
            Weight(stack_refs[spans[w]], scratch_refs[2 * w], scratch_refs[2 * w + 1], meta_ref[0], weights[w][2], weights[w][3], weights[w][5])
            for w in range(len(weights))
        ]

        def work(wait_for):
            for weight in whole:
                weight.wait_for = wait_for
            body(meta_ref, row_refs, vec_refs, whole, out_refs, sum_refs)

        @pl.when(pl.program_id(0) == 0)
        def _():
            for weight in whole:
                weight.start()
            for ref in sum_refs:
                ref[...] = jnp.zeros_like(ref)
            work(True)

        @pl.when(pl.program_id(0) > 0)
        def _():
            work(False)

    in_specs = (
        [row_spec(tile, a.shape[-1]) if a.ndim == 2 else pl.BlockSpec((a.shape[0], tile, a.shape[2]), lambda i, *_: (0, i, 0)) for a in row_ins]
        + [one_spec(1, v.shape[1]) for v in vec_ins]
        + [ANY] * n_stack
    )
    out_specs = [row_spec(tile, w) for w, _ in row_outs] + [one_spec(8, w) for w in sums]
    out_shape = [jax.ShapeDtypeStruct((rows, w), d) for w, d in row_outs] + [
        jax.ShapeDtypeStruct((8, w), F32) for w in sums
    ]
    return pl.pallas_call(
        kernel,
        grid_spec=pltpu.PrefetchScalarGridSpec(
            num_scalar_prefetch=1,
            grid=(rows // tile,),
            in_specs=in_specs,
            out_specs=out_specs,
            scratch_shapes=scratch,
        ),
        out_shape=out_shape,
        compiler_params=pltpu.CompilerParams(vmem_limit_bytes=60 * MIB, dimension_semantics=("arbitrary",)),
        cost_estimate=cost(name),
        name=name,
    )(meta, *row_ins, *vec_ins, *stacks)


def by_columns(left, weight):
    parts = []
    for p in range(weight.pieces):
        cols = weight.cols(p)
        parts.append(nn(left[...], weight.whole[:, cols]))
    return jnp.concatenate(parts, axis=1)


def by_columns_turned(left, weight):
    total = None
    for p in range(weight.pieces):
        cols = weight.cols(p)
        part = nt(left[:, cols], weight.whole[:, cols])
        total = part if total is None else total + part
    return total


def by_shards(left, weight):
    if weight.pieces:
        return by_columns(left, weight)
    if not weight.wait_for:
        return nn(left[...], weight.whole[...])
    total = None
    for c in range(len(weight.copies)):
        here = weight.rows(c)
        part = nn(left[:, here], weight.whole[here, :])
        total = part if total is None else total + part
    return total


def qkv_body(meta, rows, vecs, whole, outs, sums):
    (x,) = rows
    (bias,) = vecs
    for p in range(whole[0].pieces):
        cols = whole[0].cols(p)
        outs[0][:, cols] = (nn(x[...], whole[0].whole[:, cols]) + bias[:, cols]).astype(BF)


def out_body(meta, rows, vecs, whole, outs, sums):
    mixed, x = rows
    bias, gain, shift = vecs
    total = x[...].astype(F32) + (by_columns(mixed, whole[0]) + bias[...])
    centre = total - jnp.mean(total, axis=-1, keepdims=True)
    inverse = lax.rsqrt(jnp.mean(centre * centre, axis=-1, keepdims=True) + EPS)
    normed = centre * inverse
    outs[0][...] = normed
    outs[1][...] = jnp.broadcast_to(inverse, outs[1].shape)
    outs[2][...] = (normed * gain[...] + shift[...]).astype(BF)


def up_body(meta, rows, vecs, whole, outs, sums):
    (low,) = rows
    (bias,) = vecs
    for p in range(whole[0].pieces):
        cols = whole[0].cols(p)
        hidden = nn(low[...], whole[0].whole[:, cols]) + bias[:, cols]
        cdf = 0.5 + 0.5 * lax.erf(hidden * 0.7071067811865476)
        pdf = jnp.exp(-0.5 * hidden * hidden) * 0.3989422804014327
        outs[0][:, cols] = (hidden * cdf).astype(BF)
        outs[1][:, cols] = (cdf + hidden * pdf).astype(BF)


def down_body(seq, per, meta, rows, vecs, whole, outs, sums):
    active, normed_one, cot = rows
    bias, gain_one, shift_one, gain, shift = vecs
    total = (normed_one[...] * gain_one[...] + shift_one[...]) + (by_shards(active, whole[0]) + bias[...])
    centre = total - jnp.mean(total, axis=-1, keepdims=True)
    inverse = lax.rsqrt(jnp.mean(centre * centre, axis=-1, keepdims=True) + EPS)
    normed = centre * inverse
    tile = total.shape[0]
    at = lax.broadcasted_iota(jnp.int32, (tile, 1), 0) + pl.program_id(0) * tile
    valid = jnp.zeros(at.shape, jnp.bool_)
    for s in range(per):
        valid = valid | ((at >= s * seq) & (at < s * seq + meta[2 + s]))
    keep = jnp.where(valid, 1.0, 0.0)
    outs[0][...] = ((normed * gain[...] + shift[...]) * keep).astype(BF)
    grad = cot[...].astype(F32) * keep
    sums[0][...] += fold(grad * normed)
    sums[1][...] += fold(grad)
    scaled = grad * gain[...]
    back = inverse * (
        scaled
        - jnp.mean(scaled, axis=-1, keepdims=True)
        - normed * jnp.mean(scaled * normed, axis=-1, keepdims=True)
    )
    low = back.astype(BF)
    outs[1][...] = back
    outs[2][...] = low
    sums[2][...] += fold(low.astype(F32))


def hidden_kernel(second, whole, deriv, out, total):
    low = (nt(second[...], whole[...]) * deriv[...].astype(F32)).astype(BF)
    out[...] = low
    total[...] = fold(low.astype(F32))


def hidden_grad(second, whole, deriv, step):
    rows, width = second.shape
    ff = whole.shape[0]
    cols = pl.BlockSpec((rows, step), lambda i: (0, i))
    return pl.pallas_call(
        hidden_kernel,
        grid=(ff // step,),
        in_specs=[pl.BlockSpec((rows, width), lambda i: (0, 0)), pl.BlockSpec((step, width), lambda i: (i, 0)), cols],
        out_specs=[cols, pl.BlockSpec((8, step), lambda i: (0, i))],
        out_shape=[jax.ShapeDtypeStruct((rows, ff), BF), jax.ShapeDtypeStruct((8, ff), F32)],
        compiler_params=pltpu.CompilerParams(vmem_limit_bytes=60 * MIB),
        cost_estimate=cost("hidden"),
        name="hidden",
    )(second, whole, deriv)


def first_body(meta, rows, vecs, whole, outs, sums):
    hidden, sum_two, normed, inverse = rows
    (gain,) = vecs
    grad = sum_two[...] + by_columns_turned(hidden, whole[0])
    n1 = normed[...]
    sums[0][...] += fold(grad * n1)
    sums[1][...] += fold(grad)
    scaled = grad * gain[...]
    back = inverse[:, 0:1] * (
        scaled - jnp.mean(scaled, axis=-1, keepdims=True) - n1 * jnp.mean(scaled * n1, axis=-1, keepdims=True)
    )
    low = back.astype(BF)
    outs[0][...] = back
    outs[1][...] = low
    sums[2][...] += fold(low.astype(F32))
    whole[1].cols(0)
    outs[2][...] = nt(low, whole[1].whole[...]).astype(BF)


def input_body(meta, rows, vecs, whole, outs, sums):
    sum_one = rows[-1]
    total = sum_one[...]
    parts = len(rows) - 1
    for p in range(whole[0].pieces):
        cols = whole[0].cols(p)
        total = total + nt(rows[p % parts][p // parts], whole[0].whole[:, cols])
    outs[0][...] = total.astype(BF)


def key_mask(meta, seq):
    at = lax.broadcasted_iota(jnp.int32, (seq, 1), 0)
    return at < meta[2 + pl.program_id(0)]


def attend_kernel(meta, q_ref, k_ref, v_ref, mixed_ref, lse_ref):
    seq, lanes = q_ref.shape
    ok = key_mask(meta, seq)
    q_all = q_ref[...] * BF(HD ** (-0.5))
    k_all, v_turned = k_ref[...], v_ref[...].T
    ones = jnp.ones((16, seq), BF)
    outs = []
    for h in range(lanes // HD):
        cols = slice(h * HD, (h + 1) * HD)
        scores = jnp.where(ok, nt(k_all[:, cols], q_all[:, cols]), NEG)
        peak = jnp.max(scores, axis=0, keepdims=True)
        weights = jnp.exp(scores - peak).astype(BF)
        both = nn(jnp.concatenate([v_turned[cols], ones], axis=0), weights)
        total = both[HD : HD + 1]
        lse_ref[h : h + 1, :] = peak + jnp.log(total)
        outs.append(both[:HD] * (1.0 / total))
    mixed_ref[...] = jnp.concatenate(outs, axis=0).T.astype(BF)


def attend_back_kernel(meta, q_ref, k_ref, v_ref, g_ref, mixed_ref, lse_ref, proj_ref, sum_ref):
    seq, lanes = q_ref.shape
    ok = key_mask(meta, seq)
    scale = HD ** (-0.5)
    q_all = q_ref[...] * BF(scale)
    k_all, v_all, g_all = k_ref[...], v_ref[...], g_ref[...]
    k_turned = k_all.T
    inners = (g_all.astype(F32) * mixed_ref[...].astype(F32)).T
    gq, gk, gv = [], [], []
    for h in range(lanes // HD):
        cols = slice(h * HD, (h + 1) * HD)
        q, k, v, g = q_all[:, cols], k_all[:, cols], v_all[:, cols], g_all[:, cols]
        exact = jnp.exp(jnp.where(ok, nt(k, q), NEG) - lse_ref[h : h + 1, :])
        inner = jnp.sum(inners[cols], axis=0, keepdims=True)
        low = (exact * (nt(v, g) - inner)).astype(BF)
        gq.append(nn(k_turned[cols], low) * scale)
        gk.append(nn(low, q))
        gv.append(nn(exact.astype(BF), g))
    wholes = (jnp.concatenate(gq, axis=0).T, jnp.concatenate(gk, axis=1), jnp.concatenate(gv, axis=1))
    for c, whole in enumerate(wholes):
        low = whole.astype(BF)
        proj_ref[c] = low
        sum_ref[c] = fold(low.astype(F32))


def attend(meta, proj, per, seq):
    lanes = GROUP * HD
    groups = proj.shape[-1] // 3 // lanes
    shaped = proj.reshape(per, seq, proj.shape[-1])

    def spec(c):
        return pl.BlockSpec((None, seq, lanes), lambda s, h, *_: (s, 0, c * groups + h))

    mixed, lse = pl.pallas_call(
        attend_kernel,
        grid_spec=pltpu.PrefetchScalarGridSpec(
            num_scalar_prefetch=1,
            grid=(per, groups),
            in_specs=[spec(0), spec(1), spec(2)],
            out_specs=[spec(0), pl.BlockSpec((None, None, GROUP, seq), lambda s, h, *_: (s, h, 0, 0))],
        ),
        out_shape=[
            jax.ShapeDtypeStruct((per, seq, groups * lanes), BF),
            jax.ShapeDtypeStruct((per, groups, GROUP, seq), F32),
        ],
        compiler_params=pltpu.CompilerParams(vmem_limit_bytes=60 * MIB),
        cost_estimate=cost("attend"),
        name="attend",
    )(meta, shaped, shaped, shaped)
    return mixed.reshape(per * seq, -1), lse


def attend_back(meta, proj, grad, mixed, lse, per, seq, first, count):
    width = proj.shape[-1] // 3
    lanes = GROUP * HD
    groups = width // lanes
    shaped = proj.reshape(per, seq, proj.shape[-1])

    def spec(c):
        return pl.BlockSpec((None, seq, lanes), lambda s, h, *_: (s, 0, c * groups + first + h))

    out, sums = pl.pallas_call(
        attend_back_kernel,
        grid_spec=pltpu.PrefetchScalarGridSpec(
            num_scalar_prefetch=1,
            grid=(per, count),
            in_specs=[spec(0), spec(1), spec(2), spec(0), spec(0)]
            + [pl.BlockSpec((None, None, GROUP, seq), lambda s, h, *_: (s, first + h, 0, 0))],
            out_specs=[
                pl.BlockSpec((3, None, seq, lanes), lambda s, h, *_: (0, s, 0, h)),
                pl.BlockSpec((3, None, 8, lanes), lambda s, h, *_: (0, s, 0, h)),
            ],
        ),
        out_shape=[
            jax.ShapeDtypeStruct((3, per, seq, count * lanes), BF),
            jax.ShapeDtypeStruct((3, per, 8, count * lanes), F32),
        ],
        compiler_params=pltpu.CompilerParams(vmem_limit_bytes=60 * MIB),
        cost_estimate=cost("attend_back"),
        name="attend_back",
    )(meta, shaped, shaped, shaped, grad.reshape(per, seq, width), mixed.reshape(per, seq, width), lse)
    return out.reshape(3, per * seq, count * lanes), sums


def line_kernel(*refs):
    one, two, *eights, out = refs
    part = one.shape[-1]
    pos = 0
    for c in (0, 2):
        for ref in (one, two):
            out[:, pos : pos + part] = jnp.sum(jnp.sum(ref[c], axis=0), axis=0, keepdims=True)
            pos += part
    for ref in eights:
        width = ref.shape[1]
        out[:, pos : pos + width] = jnp.sum(ref[...], axis=0, keepdims=True)
        pos += width


def one_line(one, two, eights):
    total = 4 * one.shape[-1] + sum(b.shape[1] for b in eights)
    return pl.pallas_call(
        line_kernel,
        out_shape=jax.ShapeDtypeStruct((1, total), F32),
        compiler_params=pltpu.CompilerParams(vmem_limit_bytes=16 * MIB),
        name="line",
    )(one, two, *eights)[0]


def weight_grad(name, meta, odd, lefts, rights, chunk, come=None, extra=None):
    rows = lefts[0].shape[0]
    tall = lefts[0].shape[1] // 8

    def count(right):
        return right[0].shape[0] if isinstance(right, tuple) else right.shape[1] // chunk

    flat = [r for group in rights for r in group]
    owners = [li for li, group in enumerate(rights) for _ in group]
    firsts, steps = [], 0
    for right in flat:
        firsts.append(steps)
        steps += count(right)
    spread = [(i, r) for i, right in enumerate(flat) for r in (right if isinstance(right, tuple) else (right,))]
    below = 0 if extra is None else extra.shape[1]
    cut = (steps + 1) // 2
    n_left = len(lefts)

    def kernel(meta_ref, *refs):
        left_refs = refs[: 4 * n_left]
        pos = 4 * n_left
        right_refs = [[] for _ in flat]
        for i, _ in spread:
            right_refs[i].append(refs[pos])
            pos += 1
        extra_refs = refs[pos : pos + 4] if below else ()
        pos += len(extra_refs)
        come_ref = refs[pos] if come is not None else None
        pos += come is not None
        outs = refs[pos:]
        c = pl.program_id(0)

        def store(lefts_here, right):
            joined = tn(jnp.concatenate([left[...] for left in lefts_here], axis=1), right) if tall < 256 else None
            for k in range(4):
                part = tn(lefts_here[k][...], right) if joined is None else joined[k * tall : (k + 1) * tall]
                if come is None:
                    outs[0][k, 0:tall, :] = part.astype(BF)
                    if below:
                        outs[0][k, tall:, :] = extra_refs[k][...]
                    continue
                part = (part + come_ref[k, 0:tall, :].astype(F32)).astype(BF)
                if below:
                    low = (extra_refs[k][...].astype(F32) + come_ref[k, tall:, :].astype(F32)).astype(BF)
                if k < 3:
                    outs[k][0:tall, :] = part
                    if below:
                        outs[k][tall:, :] = low
                    continue

                @pl.when(c < cut)
                def _():
                    outs[3][0:tall, :] = part
                    if below:
                        outs[3][tall:, :] = low

                @pl.when(c >= cut)
                def _():
                    outs[4][0:tall, :] = part
                    if below:
                        outs[4][tall:, :] = low

        for i in range(len(flat)):
            last = firsts[i + 1] if i + 1 < len(flat) else steps
            li = owners[i]

            @pl.when((c >= firsts[i]) & (c < last))
            def _(i=i, li=li):
                store(left_refs[4 * li : 4 * li + 4], jnp.concatenate([r[...] for r in right_refs[i]], axis=1))

    def left_spec(k):
        return pl.BlockSpec((rows, tall), lambda c, m: (0, m[0] ^ (2 * k + odd)))

    def right_spec(i, right):
        last = (firsts[i + 1] if i + 1 < len(flat) else steps) - 1

        def place(c):
            return jnp.clip(c, firsts[i], last) - firsts[i]

        if right.ndim == 3:
            return pl.BlockSpec((None, rows, right.shape[2]), lambda c, m: (place(c), 0, 0))
        return pl.BlockSpec((rows, chunk), lambda c, m: (0, place(c)))

    def extra_spec(k):
        return pl.BlockSpec((None, below, chunk), lambda c, m: (m[0] ^ (2 * k + odd), 0, c))

    high = tall + below
    four = pl.BlockSpec((4, high, chunk), lambda c, m: (0, 0, c))
    in_specs = [left_spec(k) for _ in lefts for k in range(4)] + [right_spec(i, r) for i, r in spread]
    args = [left for left in lefts for _ in range(4)] + [r for _, r in spread]
    if below:
        in_specs += [extra_spec(k) for k in range(4)]
        args += [extra] * 4
    if come is None:
        out_specs = [four]
        out_shape = [jax.ShapeDtypeStruct((4, high, steps * chunk), BF)]
    else:
        in_specs.append(four)
        args.append(come)
        out_specs = [pl.BlockSpec((high, chunk), lambda c, m: (0, c))] * 3 + [
            pl.BlockSpec((high, chunk), lambda c, m: (0, jnp.minimum(c, cut - 1))),
            pl.BlockSpec((high, chunk), lambda c, m: (0, jnp.maximum(c - cut, 0))),
        ]
        out_shape = [jax.ShapeDtypeStruct((high, steps * chunk), BF)] * 3 + [
            jax.ShapeDtypeStruct((high, cut * chunk), BF),
            jax.ShapeDtypeStruct((high, (steps - cut) * chunk), BF),
        ]
    return pl.pallas_call(
        kernel,
        grid_spec=pltpu.PrefetchScalarGridSpec(
            num_scalar_prefetch=1,
            grid=(steps,),
            in_specs=in_specs,
            out_specs=out_specs,
        ),
        out_shape=out_shape,
        compiler_params=pltpu.CompilerParams(vmem_limit_bytes=60 * MIB),
        cost_estimate=cost(name),
        name=name,
    )(meta, *args)


def shards(
    tokens, lengths, w_qkv, bias_qv, w_out, bias_out, gain_one, shift_one,
    w_up, bias_up, w_down, bias_down, gain_two, shift_two, cotangent,
):
    seqs, blk, width = tokens.shape
    n = lax.axis_size("ctx")
    ndp = lax.axis_size("dp")
    me = lax.axis_index("dp")
    place = lax.axis_index("ctx")
    per = seqs // n
    rows = seqs * blk
    tile = per * blk
    ff = w_up.shape[1]
    thin = w_qkv.shape[0]
    tuned = ndp == 8
    half = width // (GROUP * HD) // 2
    cut = (per + 1) // 2

    own = lax.dynamic_slice_in_dim(lengths, place * per, per)
    meta = jnp.concatenate([jnp.stack([me, place]).astype(jnp.int32), own])

    vectors = (bias_qv, bias_out, gain_one, shift_one, bias_up, bias_down, gain_two, shift_two)
    sizes = [v.shape[0] for v in vectors]
    count = sum(sizes)
    line = jnp.pad(jnp.concatenate(vectors).reshape(1, count), ((0, 15), (0, 3 * width - count)))
    qkv_own = jnp.concatenate([w_qkv, line])
    mid_own = jnp.concatenate([w_out, w_up], axis=1)
    shared = tokens.reshape(n, per, blk, width)
    x = jnp.swapaxes(to_sequences(shared), 0, 1).reshape(rows, width)
    qkv_near = gather_near(qkv_own)
    mid_near = gather_near(mid_own)
    cot_parts = [part_of(cotangent, j) for j in range(n)]
    blank = jnp.zeros((seqs, blk, width), BF)
    x, qkv_near, mid_near, cot_parts, blank, meta = sync(x, qkv_near, mid_near, cot_parts, blank, meta)
    qkv_far = gather_far(qkv_near)
    qkv_mine = gather_stack(qkv_own, qkv_near, qkv_far)
    qkv_other = swap(qkv_mine, "dp", 1)
    mid_far = gather_far(mid_near)
    cot_1 = trade(cot_parts[1], 1)

    lines = qkv_mine[:, thin, :count]
    both = jnp.concatenate([lines, swap(lines, "dp", 1)])
    index = jnp.arange(ndp, dtype=jnp.int32) ^ me
    packed = jnp.take(both, (index >> 1) + (index & 1) * (ndp // 2), axis=0).astype(F32)
    fulls, pos = [], 0
    for size in sizes:
        fulls.append(packed[:, pos : pos + size].reshape(1, ndp * size))
        pos += size
    bqv, bout, gone, sone, bup, bdown, gtwo, stwo = fulls
    bqkv = jnp.concatenate([bqv[:, :width], jnp.zeros((1, width), F32), bqv[:, width:]], axis=1)

    qkv_w = (qkv_mine, qkv_other, thin, 0, 3 * width, 3)
    (proj,) = dense(qkv_body, "qkv", meta, rows, tile, [x], [bqkv], [qkv_w], [(3 * width, BF)], [])
    proj, mid_far, cot_1, w_down, cot_parts = sync(proj, mid_far, cot_1, w_down, cot_parts)
    mid_mine = gather_stack(mid_own, mid_near, mid_far)
    mid_other = swap(mid_mine, "dp", 1)
    down_all = lax.all_gather(w_down, "dp", axis=0, tiled=True)
    cot_2 = trade(cot_parts[2], 2)
    mixed, lse = attend(meta, proj, per, n * blk)
    mixed, mid_other, cot_2 = sync(mixed, mid_other, cot_2)
    out_w = (mid_mine, mid_other, thin, 0, width, 2)
    up_w = (mid_mine, mid_other, thin, width, ff, 4)
    normed_one, inverse_one, first_low = dense(
        out_body, "out", meta, rows, tile, [mixed, x], [bout, gone, sone], [out_w], [(width, F32), (128, F32), (width, BF)], []
    )
    first_low, cot_parts = sync(first_low, cot_parts)
    cot_3 = trade(cot_parts[3], 3)
    active, deriv = dense(up_body, "up", meta, rows, tile, [first_low], [bup], [up_w], [(ff, BF), (ff, BF)], [])
    active, down_all, cot_3 = sync(active, down_all, cot_3)
    down_w = (down_all.reshape(8, ff // 8, width), None, ff // 8, 0, width, 0)
    cot = put_positions([(0, 0, cot_parts[0]), (1, 0, cot_1), (2, 0, cot_2), (3, 0, cot_3)], per).reshape(rows, width)
    out_parts, sum_two, second, s_gtwo, s_stwo, s_bdown = dense(
        functools.partial(down_body, n * blk, per), "down", meta, rows, tile, [active, normed_one, cot],
        [bdown, gone, sone, gtwo, stwo], [down_w], [(width, BF), (width, F32), (width, BF)], [width] * 3,
    )
    out_parts = out_parts.reshape(per, n * blk, width)
    out_own = part_of(out_parts, 0, 1)
    out_1 = trade(part_of(out_parts, 1, 1), 1)

    come = ()
    if tuned:
        (away,) = weight_grad("gd_away", meta, 1, [active], [[second]], 512)
        come = swap(away, "dp", 1)
        second = after(second, away)
    hidden, s_bup = hidden_grad(second, down_all, deriv, 1024)
    hidden, come, out_1, out_parts = sync(hidden, come, out_1, out_parts)
    part = part_of(out_parts, 2, 1)
    out_2 = trade(part[:cut], 2)
    d_far, d_near = (), ()
    if tuned:
        d_sums = weight_grad("gd_keep", meta, 0, [active], [[second]], 512, come=come)
        d_far = send_far(d_sums)
        hidden, out_2, part = sync(after(hidden, d_sums[0]), out_2, part)
    out_2b = trade(part[cut:], 2)
    if tuned:
        (away,) = weight_grad("gu_away", meta, 1, [first_low], [[hidden]], 1024)
        hidden = after(hidden, away)
        away, d_far, out_2b = sync(away, d_far, out_2b)
        come = swap(away, "dp", 1)
    hidden, d_far, out_2b, out_parts = sync(hidden, d_far, out_2b, out_parts)
    if tuned:
        d_near = send_near(d_sums, d_far)
    out_3 = trade(part_of(out_parts, 3, 1), 3)
    sum_one, branch, g_mixed, s_gone, s_sone, s_bout = dense(
        first_body, "first", meta, rows, tile, [hidden, sum_two, normed_one, inverse_one], [gone], [up_w[:5] + (4,), out_w[:5] + (1,)],
        [(width, F32), (width, BF), (width, BF)], [width] * 3,
    )
    branch, g_mixed, come, d_near, out_3 = sync(branch, g_mixed, come, d_near, out_3)
    output = put_slots([(0, 0, out_own), (1, 0, out_1), (2, 0, out_2), (2, cut, out_2b), (3, 0, out_3)], per, blank)
    u_far = ()
    if tuned:
        d_share = add_low(d_sums[0], *d_near)
        g_down = lax.psum(d_share, "ctx")
        u_sums = weight_grad("gu_keep", meta, 0, [first_low], [[hidden]], 1024, come=come)
        u_far = send_far(u_sums)
        g_mixed = after(g_mixed, u_sums[0])
    p_one, s_one = attend_back(meta, proj, g_mixed, mixed, lse, per, n * blk, 0, half)
    p_one, g_mixed, u_far = sync(p_one, g_mixed, u_far)
    u_near = ()
    if tuned:
        u_near = send_near(u_sums, u_far)
    p_two, s_two = attend_back(meta, proj, g_mixed, mixed, lse, per, n * blk, half, half)
    if tuned:
        p_two, u_near = sync(p_two, u_near)

    eights = (s_bout, s_gone, s_sone, s_bup, s_bdown, s_gtwo, s_stwo)
    p_two, s_one, s_two, eights = sync(p_two, s_one, s_two, eights)
    vec = one_line(s_one, s_two, eights)
    places, pos = [], 0
    for size in sizes:
        places.append(vec[pos : pos + ndp * size])
        pos += ndp * size
    vec = places
    vec = jnp.concatenate([v.reshape(ndp, -1) for v in vec], axis=1)

    come = ()
    if tuned:
        u_keep, u_away = halves_ctx(add_low(u_sums[0], *u_near), 1)
        u_come = swap(u_away, "ctx", 1)
        extra = jnp.pad(vec[:, None, :].astype(BF), ((0, 0), (0, 15), (0, 4 * width - count)))
        products = ([x, mixed], [[(p_one, p_two)], [branch]])
        (away,) = weight_grad("gb_away", meta, 1, *products, 1024, extra=extra)
        sum_one = after(sum_one, away)
        away, u_come, g_down = sync(away, u_come, g_down)
        come = swap(away, "dp", 1)
        u_keep, u_away = halves_ctx(add_low(u_keep, u_come), 2)
        u_come = swap(u_away, "ctx", 2)
    else:
        u_come = ()
    (grad_in,) = dense(input_body, "input", meta, rows, tile, [p_one, p_two, sum_one], [], [qkv_w[:5] + (6,)], [(width, BF)], [])
    grad_in, come, u_come = sync(grad_in, come, u_come)
    grad_in = grad_in.reshape(per, n * blk, width)
    part_1 = part_of(grad_in, 1, 1)
    if tuned:
        u_half = add_low(u_keep, u_come)
        u_other = swap(u_half, "ctx", 2)
        b_sums = weight_grad("gb_keep", meta, 0, *products, 1024, come=come, extra=extra)
        b_sums, u_other, part_1, grad_in = sync(b_sums, u_other, part_1, grad_in)
    in_1 = trade(part_1, 1)
    part_2, part_3 = part_of(grad_in, 2, 1), part_of(grad_in, 3, 1)
    in_2 = trade(part_2[:cut], 2)
    if tuned:
        b_far = send_far(b_sums)
        u_whole = join_ctx(u_half, u_other, 2)
        b_far, in_1, in_2, part_2, part_3, u_whole = sync(b_far, in_1, in_2, part_2, part_3, u_whole)
        b_near = send_near(b_sums, b_far)
        u_other = swap(u_whole, "ctx", 1)
    in_2b, in_3 = trade(part_2[cut:], 2), trade(part_3[:cut], 3)
    if tuned:
        b_near, in_2b, in_3, part_3, u_other = sync(b_near, in_2b, in_3, part_3, u_other)
        b_keep, b_away = halves_ctx(add_low(b_sums[0], *b_near), 1)
        b_come = swap(b_away, "ctx", 1)
    in_3b = trade(part_3[cut:], 3)
    in_rest = [(2, 0, in_2), (2, cut, in_2b), (3, 0, in_3), (3, cut, in_3b)]
    if tuned:
        b_come, in_3b = sync(b_come, in_3b)
        b_half = add_low(b_keep, b_come)
        g_up = join_ctx(u_whole, u_other, 1)
        b_half = whole_ctx(halve_ctx(b_half, 2), 2)
        b_other = swap(b_half, "ctx", 1)
        low = place % 2 == 0
        left = jnp.where(low, b_half, b_other).astype(F32)
        right = jnp.where(low, b_other, b_half).astype(F32)
        g_qkv = jnp.concatenate([left[:thin], right[:thin, :width]], axis=1)
        g_out = right[:thin, width:]
        g_up = g_up.astype(F32)
        g_down = g_down.astype(F32)
        vec = left[thin, :count]
    else:
        def whole(*products):
            return jnp.concatenate([tn(a, b).astype(BF) for a, b in products], axis=1)

        def total(grad):
            return lax.psum(reduce_any(grad).astype(F32), "ctx")

        g_down = total(whole((active, second)))
        g_up = total(whole((first_low, hidden)))
        g_out = total(whole((mixed, branch)))
        g_qkv = total(whole(*[(x, p[c]) for c in range(3) for p in (p_one, p_two)]))
        vec = lax.psum(lax.psum_scatter(vec, "dp", scatter_dimension=0, tiled=True), "ctx").reshape(-1)
    grads, pos = [], 0
    for size in sizes:
        grads.append(vec[pos : pos + size])
        pos += size
    g_bqv, g_bout, g_gone, g_sone, g_bup, g_bdown, g_gtwo, g_stwo = grads
    grad_input = put_slots([(0, 0, part_of(grad_in, 0, 1)), (1, 0, in_1)] + in_rest, per, jnp.zeros((seqs, blk, width), F32))
    return (
        output, grad_input, g_qkv, g_bqv, g_out, g_bout, g_gone, g_sone, g_up, g_bup, g_down, g_bdown, g_gtwo, g_stwo,
    )


def solution(mesh):
    row = P("dp", "ctx", None)
    mat = P("dp", None)
    vec = P("dp")
    weights = (mat, vec, mat, vec, vec, vec, mat, vec, mat, vec, vec, vec)
    return jax.shard_map(
        shards, mesh=mesh, in_specs=(row, vec) + weights + (row,), out_specs=(row, row) + weights, check_vma=False
    )
```
